32 devices in a mesh: gx: 2 (over y), gy: 4 (over x, core), gz: 4 (over z).
Axes of the slice: x: 2, y: 2, z: 4, core: 2. Of those that a mesh axis runs over, the one named last changes fastest.
Arguments:
- old_fields: float32 [2048, 4, 512], P(('gx', 'gy', 'gz')), may hold values from 0.5 to 2.5
- new_owner: int32 [2048], P(('gx', 'gy', 'gz')), may hold values from 0 to 7, as said below
- old_owner: int32 [2048], P(('gx', 'gy', 'gz')), may hold values from 0 to 7, as said below
Outputs:
- flame_fields: float32 [4, 32, 64, 512], P(None, 'gx', 'gy', 'gz')
The draws below stay inside these ranges and needn't reach their ends.
Inputs may be any that keep to these rules, and one draw needn't show every extreme that they name: A box keeps its gy index; new_owner is the group index of the device of its gx+gz group that holds it after the move. A device sends at most 16 boxes to one device of its group, reaches that number for some device, and every device receives exactly 64 boxes. `old_owner`: agrees with new_owner: the positions of a device naming s are exactly as many as the boxes that device s of the same group and gy sends to it.
All inputs are finite; a program needn't handle non-finite values.
Results may differ from the reference program's by a relative error of at most 0.00002.
Values sent between devices are 32-bit elements; how exact they have to be, the bound alone decides.
No kernel may reach another device: no remote copies, remote signals or barrier semaphores. Data moves between devices by JAX's collectives and lax.ppermute only.
A program may use at most 64 MiB of HBM per device.

```python
import jax
import jax.numpy as jnp

EDGE = 8
FIELDS = 4
BRICK_X = 2
BRICK_Y = 2
BRICK_Z = 16
BOX_DEV = 64
CELLS = 512
NBOXES = 2048
NX = 32
NY = 64
NZ = 512
N_GX = 2
N_GY = 4
N_GZ = 4


def routing(key):
    group_size = N_GX * N_GZ
    share_count = BOX_DEV // group_size
    base_key = jax.random.fold_in(key, 7)

    def one_plane(slab_key):
        plane_keys = jax.random.split(slab_key, 4)
        mapping = jax.random.permutation(plane_keys[0], group_size)
        offsets = jax.random.randint(plane_keys[1], (share_count,), 1, group_size)
        sources = jnp.arange(group_size, dtype=jnp.int32)
        targets = jnp.arange(group_size, dtype=jnp.int32)
        counts = share_count + share_count * (mapping[:, None] == targets[None, :]).astype(jnp.int32)
        shifted = mapping[(sources[None, :] + offsets[:, None]) % group_size]
        counts = counts - jnp.sum((shifted[:, :, None] == targets[None, None, :]).astype(jnp.int32), axis=0)

        def one_source(row_counts, row_key):
            listed = jnp.repeat(targets, row_counts, total_repeat_length=BOX_DEV)
            return jax.random.permutation(row_key, listed)

        def one_target(column_counts, column_key):
            listed = jnp.repeat(sources, column_counts, total_repeat_length=BOX_DEV)
            return jax.random.permutation(column_key, listed)
        sent_to = jax.vmap(one_source)(counts, jax.random.split(plane_keys[2], group_size))
        held_from = jax.vmap(one_target)(counts.T, jax.random.split(plane_keys[3], group_size))
        return (sent_to, held_from)
    sent_to, held_from = jax.vmap(one_plane)(jax.random.split(base_key, N_GY))
    sent_to = sent_to.reshape(N_GY, N_GX, N_GZ, BOX_DEV).transpose(1, 0, 2, 3).reshape(-1)
    held_from = held_from.reshape(N_GY, N_GX, N_GZ, BOX_DEV).transpose(1, 0, 2, 3).reshape(-1)
    return (sent_to.astype(jnp.int32), held_from.astype(jnp.int32))


def draw_new_owner(key, part):
    return routing(key)[0]


def draw_old_owner(key, part):
    return routing(key)[1]


def shard_levels(key, shape, cuts, least, high):
    gain = 1.0
    for dim, shards_of in cuts:
        draws = jax.random.uniform(jax.random.fold_in(jax.random.fold_in(key, 6), dim), (shards_of,), jnp.float32, least / len(cuts), high / len(cuts))
        gain = gain * jnp.repeat(jnp.exp(draws), shape[dim] // shards_of).reshape((-1,) + (1,) * (len(shape) - 1 - dim))
    return gain


def setup_inputs(seed: int = 0) -> dict:
    seeds = jax.random.split(jax.random.key(seed), 4)
    return {
        "old_fields": jnp.clip(0.5 + 2.0 * jax.random.uniform(seeds[0], (NBOXES, FIELDS, CELLS), jnp.float32) ** shard_levels(seeds[0], (NBOXES, FIELDS, CELLS), ((0, 32),), -0.2, 0.2), 0.5, 2.5),
        "new_owner": draw_new_owner(jax.random.fold_in(seeds[3], 71), 0),
        "old_owner": draw_old_owner(jax.random.fold_in(seeds[3], 71), 0),
    }


DIFFUSION = (1.0, 3.3, 0.9, 1.2)
TIME_STEP = 0.012

def diffusion_rate(present_state):
    thermal_field = present_state[0]
    stepping_factors = jnp.array(DIFFUSION, jnp.float32)
    diffusion_coefficient = stepping_factors[:, None, None, None] * (thermal_field * jnp.sqrt(thermal_field))[None]
    summed = jnp.zeros_like(present_state)
    for direction in (1, 2, 3):
        for offset in (1, -1):
            beside = jnp.roll(present_state, offset, axis=direction)
            beside_diffusivity = jnp.roll(diffusion_coefficient, offset, axis=direction)
            summed = summed + 0.5 * (diffusion_coefficient + beside_diffusivity) * (beside - present_state)
    return summed

def reference(old_fields, new_owner, old_owner):
    group_size = N_GX * N_GZ
    row_number = jnp.arange(NBOXES, dtype=jnp.int32)
    device = row_number // BOX_DEV
    slot_number = row_number % BOX_DEV
    plane_index = device // N_GZ % N_GY
    source_group = device // (N_GY * N_GZ) * N_GZ + device % N_GZ
    target_device = (new_owner // N_GZ * N_GY + plane_index) * N_GZ + new_owner % N_GZ
    old_keys = (target_device * group_size + source_group) * BOX_DEV + slot_number
    new_keys = (device * group_size + old_owner) * BOX_DEV + slot_number
    old_order = jnp.argsort(old_keys).astype(jnp.int32)
    new_order = jnp.argsort(new_keys).astype(jnp.int32)
    sources = jnp.zeros((NBOXES,), jnp.int32).at[new_order].set(old_order)
    moved_boxes = jnp.take(old_fields, sources, axis=0)
    present_state = moved_boxes.reshape(N_GX, N_GY, N_GZ, BRICK_X, BRICK_Y, BRICK_Z, FIELDS, EDGE, EDGE, EDGE)
    present_state = present_state.transpose(6, 0, 3, 7, 1, 4, 8, 2, 5, 9).reshape(FIELDS, NX, NY, NZ)
    first_section = present_state + TIME_STEP * diffusion_rate(present_state)
    return 0.5 * present_state + 0.5 * (first_section + TIME_STEP * diffusion_rate(first_section))
```

```python
import jax
import jax.numpy as jnp
from jax import lax
from jax.experimental import pallas as pl
from jax.experimental.pallas import tpu as pltpu
from jax.sharding import PartitionSpec as P

EDGE = 8
FIELDS = 4
BRICK_X = 2
BRICK_Y = 2
BRICK_Z = 16
CELLS = EDGE**3
LANES = 128
TILES = CELLS // LANES


DIFFUSION = (1.0, 3.3, 0.9, 1.2)
TIME_STEP = 0.012

VMEM = pl.BlockSpec(memory_space=pltpu.VMEM)
SMEM = pl.BlockSpec(memory_space=pltpu.SMEM)


def padded(cells, sides, width):
    for axis, dim in sides:
        count = lax.axis_size(axis)
        head = lax.slice_in_dim(cells, 0, width, axis=dim)
        tail = lax.slice_in_dim(cells, cells.shape[dim] - width, cells.shape[dim], axis=dim)
        cells = jnp.concatenate(
            [
                lax.ppermute(tail, axis, [(i, (i + 1) % count) for i in range(count)]),
                cells,
                lax.ppermute(head, axis, [((i + 1) % count, i) for i in range(count)]),
            ],
            axis=dim,
        )
    return cells


def window(array, direction, offset):
    pieces = [slice(None), slice(1, -1), slice(1, -1), slice(1, -1)]
    length = array.shape[direction]
    pieces[direction] = slice(1 + offset, length - 1 + offset)
    return array[tuple(pieces)]


def rates_inside(bordered_fields):
    thermal_field = bordered_fields[0]
    stepping_factors = jnp.array(DIFFUSION, jnp.float32)
    diffusion_coefficient = (
        stepping_factors[:, None, None, None] * (thermal_field * jnp.sqrt(thermal_field))[None]
    )
    centre = bordered_fields[:, 1:-1, 1:-1, 1:-1]
    centre_diffusivity = diffusion_coefficient[:, 1:-1, 1:-1, 1:-1]
    summed = jnp.zeros_like(centre)
    for direction in (1, 2, 3):
        for offset in (1, -1):
            beside = window(bordered_fields, direction, offset)
            beside_diffusivity = window(diffusion_coefficient, direction, offset)
            summed = summed + 0.5 * (centre_diffusivity + beside_diffusivity) * (beside - centre)
    return summed


def with_faces(present_state):
    return padded(present_state, (("gx", 1), ("gy", 2), ("gz", 3)), 1)


def rank_table(owner, table, counts, group, capacity, boxes, empty):
    def clear(i, carry):
        table[i] = empty
        return carry

    lax.fori_loop(0, group * capacity, clear, 0)
    for g in range(group):
        counts[g] = g * capacity

    def place(b, carry):
        o = owner[b]
        slot = counts[o]
        table[slot] = b
        counts[o] = slot + 1
        return carry

    lax.fori_loop(0, boxes, place, 0, unroll=8)


def pack_boxes(old_fields, new_owner, me, group, capacity, split):
    boxes = new_owner.shape[0]
    pieces = group if split else 1
    rows = group * capacity // pieces

    def kernel(me_ref, owner, fields, *refs):
        outs, (table, counts) = refs[:pieces], refs[pieces:]
        rank_table(owner, table, counts, group, capacity, boxes, 0)
        for k, out in enumerate(outs):
            base = (me_ref[0] ^ k) * capacity if split else 0

            def copy(r, carry, out=out, base=base):
                out[r] = fields[table[base + r]]
                return carry

            lax.fori_loop(0, rows, copy, 0, unroll=8)

    return pl.pallas_call(
        kernel,
        out_shape=[jax.ShapeDtypeStruct((rows,) + old_fields.shape[1:], jnp.float32)] * pieces,
        in_specs=[SMEM, SMEM, VMEM],
        out_specs=[VMEM] * pieces,
        scratch_shapes=[
            pltpu.SMEM((group * capacity,), jnp.int32),
            pltpu.SMEM((group,), jnp.int32),
        ],
        name="pack_boxes",
    )(me, new_owner, old_fields)


def swap_boxes(columns):
    lane = lax.broadcasted_iota(jnp.int32, columns[0].shape, 1)
    for bit in range(4):
        width = EDGE << bit
        upper = (lane & width) != 0
        fresh = list(columns)
        for low in range(16):
            if low >> bit & 1:
                continue
            high = low | 1 << bit
            a, b = columns[low], columns[high]
            fresh[low] = jnp.where(upper, pltpu.roll(b, width, 1), a)
            fresh[high] = jnp.where(upper, b, pltpu.roll(a, LANES - width, 1))
        columns = fresh
    return columns


def grid_from_boxes(arrived, old_owner, me, group, capacity, split):
    boxes = old_owner.shape[0]
    pieces = len(arrived)
    rows = group * capacity // pieces

    def kernel(me_ref, owner, *refs):
        ins, (out, table, counts, held, turned) = refs[:pieces], refs[pieces:]
        rank_table(owner, table, counts, group, capacity, boxes, boxes)
        for k, rows_in in enumerate(ins):
            base = (me_ref[0] ^ k) * capacity if split else 0

            def scatter(r, carry, rows_in=rows_in, base=base):
                p = table[base + r]
                for t in range(TILES):
                    held[p, t // 2, pl.ds(t % 2 * FIELDS, FIELDS), :] = rows_in[
                        r, :, pl.ds(t * LANES, LANES)
                    ]
                return carry

            lax.fori_loop(0, rows, scatter, 0, unroll=4)
        for bx in range(BRICK_X):
            for by in range(BRICK_Y):
                first = (bx * BRICK_Y + by) * BRICK_Z
                for half in range(TILES // 2):
                    columns = swap_boxes([held[first + bz, half] for bz in range(BRICK_Z)])
                    for r in range(16):
                        turned[pl.ds(r * 8, 8), :] = columns[r]
                    for t in range(2):
                        for i in range(2):
                            x = bx * EDGE + half * 4 + t * 2 + i
                            for f in range(FIELDS):
                                out[f, x, pl.ds(by * EDGE, EDGE), :] = turned[
                                    pl.ds(i * 64 + t * FIELDS + f, 8, stride=8), :
                                ]

    return pl.pallas_call(
        kernel,
        out_shape=jax.ShapeDtypeStruct(
            (FIELDS, BRICK_X * EDGE, BRICK_Y * EDGE, BRICK_Z * EDGE), jnp.float32
        ),
        in_specs=[SMEM, SMEM] + [VMEM] * pieces,
        out_specs=VMEM,
        scratch_shapes=[
            pltpu.SMEM((group * capacity,), jnp.int32),
            pltpu.SMEM((group,), jnp.int32),
            pltpu.VMEM((boxes + 1, TILES // 2, 2 * FIELDS, LANES), jnp.float32),
            pltpu.VMEM((LANES, LANES), jnp.float32),
        ],
        name="grid_from_boxes",
    )(me, old_owner, *arrived)


def body(old_fields, new_owner, old_owner):
    group_size = lax.axis_size("gx") * lax.axis_size("gz")
    box_count = new_owner.shape[0]
    capacity = 2 * (box_count // group_size)
    split = group_size <= 8
    me = (lax.axis_index("gx") * lax.axis_size("gz") + lax.axis_index("gz")).reshape(1)
    departing = pack_boxes(old_fields, new_owner, me, group_size, capacity, split)
    if split:
        arrived = [departing[0]] + [
            lax.ppermute(departing[k], ("gx", "gz"), [(i, i ^ k) for i in range(group_size)])
            for k in range(1, group_size)
        ]
    else:
        arrived = [
            lax.all_to_all(departing[0], ("gx", "gz"), split_axis=0, concat_axis=0, tiled=True)
        ]
    present_state = grid_from_boxes(arrived, old_owner, me, group_size, capacity, split)
    first_section = present_state + TIME_STEP * rates_inside(with_faces(present_state))
    result_fields = 0.5 * present_state + 0.5 * (
        first_section + TIME_STEP * rates_inside(with_faces(first_section))
    )
    return result_fields


def solution(mesh):
    return jax.shard_map(
        body,
        mesh=mesh,
        in_specs=(P(("gx", "gy", "gz"), None, None), P(("gx", "gy", "gz")), P(("gx", "gy", "gz"))),
        out_specs=P(None, "gx", "gy", "gz"),
        check_vma=False,
    )
```

```python
import jax
import jax.numpy as jnp
from jax import lax
from jax.experimental import pallas as pl
from jax.experimental.pallas import tpu as pltpu
from jax.sharding import PartitionSpec as P

EDGE = 8
FIELDS = 4
BRICK_X = 2
BRICK_Y = 2
BRICK_Z = 16
CELLS = EDGE**3
LANES = 128
TILES = CELLS // LANES


DIFFUSION = (1.0, 3.3, 0.9, 1.2)
TIME_STEP = 0.012

VMEM = pl.BlockSpec(memory_space=pltpu.VMEM)
SMEM = pl.BlockSpec(memory_space=pltpu.SMEM)


def rank_table(owner, table, counts, group, capacity, boxes, empty):
    def clear(i, carry):
        table[i] = empty
        return carry

    lax.fori_loop(0, group * capacity, clear, 0)
    for g in range(group):
        counts[g] = g * capacity

    def place(b, carry):
        o = owner[b]
        slot = counts[o]
        table[slot] = b
        counts[o] = slot + 1
        return carry

    lax.fori_loop(0, boxes, place, 0, unroll=8)


def pack_boxes(old_fields, new_owner, me, group, capacity, split):
    boxes = new_owner.shape[0]
    pieces = group if split else 1
    rows = group * capacity // pieces

    def kernel(me_ref, owner, fields, *refs):
        outs, (table, counts) = refs[:pieces], refs[pieces:]
        rank_table(owner, table, counts, group, capacity, boxes, 0)
        for k, out in enumerate(outs):
            base = (me_ref[0] ^ k) * capacity if split else 0

            def copy(r, carry, out=out, base=base):
                out[r] = fields[table[base + r]]
                return carry

            lax.fori_loop(0, rows, copy, 0, unroll=8)

    return pl.pallas_call(
        kernel,
        out_shape=[jax.ShapeDtypeStruct((rows,) + old_fields.shape[1:], jnp.float32)] * pieces,
        in_specs=[SMEM, SMEM, VMEM],
        out_specs=[VMEM] * pieces,
        scratch_shapes=[
            pltpu.SMEM((group * capacity,), jnp.int32),
            pltpu.SMEM((group,), jnp.int32),
        ],
        name="pack_boxes",
    )(me, new_owner, old_fields)


def swap_boxes(columns):
    lane = lax.broadcasted_iota(jnp.int32, columns[0].shape, 1)
    for bit in range(4):
        width = EDGE << bit
        upper = (lane & width) != 0
        fresh = list(columns)
        for low in range(16):
            if low >> bit & 1:
                continue
            high = low | 1 << bit
            a, b = columns[low], columns[high]
            fresh[low] = jnp.where(upper, pltpu.roll(b, width, 1), a)
            fresh[high] = jnp.where(upper, b, pltpu.roll(a, LANES - width, 1))
        columns = fresh
    return columns


def ring(count, step):
    return [(i, (i + step) % count) for i in range(count)]


def boxes_in_place(arrived, old_owner, me, group, capacity, split, joined):
    boxes = old_owner.shape[0]
    pieces = len(arrived)
    rows = group * capacity // pieces
    half = boxes // BRICK_X
    face = (BRICK_Z, BRICK_Y * FIELDS, LANES)
    faces = [jax.ShapeDtypeStruct((2,) + face if joined else face, jnp.float32)] * (2 - joined)

    def kernel(me_ref, owner, *refs):
        ins, refs = refs[:pieces], refs[pieces:]
        held, outs, (table, counts) = refs[0], refs[1 : 1 + len(faces)], refs[1 + len(faces) :]
        rank_table(owner, table, counts, group, capacity, boxes, boxes)
        for k, rows_in in enumerate(ins):
            base = (me_ref[0] ^ k) * capacity if split else 0

            def scatter(r, carry, rows_in=rows_in, base=base):
                p = table[base + r]
                for t in range(TILES):
                    held[p, t // 2, pl.ds(t % 2 * FIELDS, FIELDS), :] = rows_in[
                        r, :, pl.ds(t * LANES, LANES)
                    ]
                return carry

            lax.fori_loop(0, rows, scatter, 0, unroll=4)
        for side in range(2):
            out = outs[0].at[side] if joined else outs[side]
            for by in range(BRICK_Y):
                for bz in range(BRICK_Z):
                    p = side * half + by * BRICK_Z + bz
                    out[bz, pl.ds(by * FIELDS, FIELDS), :] = held[
                        p, side, pl.ds(side * FIELDS, FIELDS), :
                    ]

    return pl.pallas_call(
        kernel,
        out_shape=[
            jax.ShapeDtypeStruct((boxes + 1, TILES // 2, 2 * FIELDS, LANES), jnp.float32)
        ]
        + faces,
        in_specs=[SMEM, SMEM] + [VMEM] * pieces,
        out_specs=[VMEM] * (1 + len(faces)),
        scratch_shapes=[
            pltpu.SMEM((group * capacity,), jnp.int32),
            pltpu.SMEM((group,), jnp.int32),
        ],
        name="boxes_in_place",
    )(me, old_owner, *arrived)


HALO = 2
NX = BRICK_X * EDGE
NY = BRICK_Y * EDGE
WIDE_X = NX + 2 * HALO
WIDE_Y = NY + EDGE
NEAR_X = NX + 2


def lay_out(columns, turned, store):
    columns = swap_boxes(columns)
    for r in range(16):
        turned[pl.ds(r * 8, 8), :] = columns[r]
    for a in range(2):
        for i in range(2):
            for f in range(FIELDS):
                store(a, i, f, turned[pl.ds(i * 64 + a * FIELDS + f, 8, stride=8), :])


def grid_from_boxes(held):
    def kernel(held, grid, turned):
        for bx in range(BRICK_X):
            for by in range(BRICK_Y):
                first = (bx * BRICK_Y + by) * BRICK_Z
                for half in range(TILES // 2):

                    def store(t, i, f, rows, x=bx * EDGE + half * 4, by=by):
                        grid[f, x + t * 2 + i, pl.ds(by * EDGE, EDGE), :] = rows

                    lay_out([held[first + bz, half] for bz in range(BRICK_Z)], turned, store)

    return pl.pallas_call(
        kernel,
        out_shape=jax.ShapeDtypeStruct((FIELDS, NX, NY, LANES), jnp.float32),
        in_specs=[VMEM],
        out_specs=VMEM,
        scratch_shapes=[pltpu.VMEM((LANES, LANES), jnp.float32)],
        cost_estimate=pl.CostEstimate(flops=2**22, bytes_accessed=2**21, transcendentals=0),
        name="grid_from_boxes",
    )(held)


def x_faces_and_y_rows(grid, faces, joined):
    def kernel(grid, *refs):
        ins, (layers, low, high, turned) = refs[: len(faces)], refs[len(faces) :]
        for side in range(2):
            face = ins[0].at[side] if joined else ins[side]

            def store(by, i, f, rows, first=0 if side else HALO):
                layers[f, first + i, pl.ds(by * EDGE, EDGE), :] = rows

            lay_out([face[bz] for bz in range(BRICK_Z)], turned, store)
        for f in range(FIELDS):
            for x in range(NEAR_X):
                cells = layers.at[f, 1 if x == 0 else 2] if x % (NX + 1) == 0 else grid.at[f, x - 1]
                low[f, x] = cells[pl.ds(0, HALO), :]
                high[f, x] = cells[pl.ds(NY - HALO, HALO), :]

    rows = jax.ShapeDtypeStruct((FIELDS, NEAR_X, HALO, LANES), jnp.float32)
    return pl.pallas_call(
        kernel,
        out_shape=[jax.ShapeDtypeStruct((FIELDS, 2 * HALO, NY, LANES), jnp.float32), rows, rows],
        in_specs=[VMEM] * (1 + len(faces)),
        out_specs=[VMEM] * 3,
        scratch_shapes=[pltpu.VMEM((LANES, LANES), jnp.float32)],
        name="x_faces_and_y_rows",
    )(grid, *faces)


def column_places():
    places = {}
    for f in range(FIELDS):
        for x in range(NX):
            places[f, x + 1] = (0, f * NX + x)
        places[f, 0] = (1, f)
        places[f, NEAR_X - 1] = (1, FIELDS + f)
    return places


def z_columns(grid, layers, below, above):
    def kernel(grid, layers, below, above, low, high, halo):
        for f in range(FIELDS):
            for x in range(NEAR_X):
                halo[f, x, pl.ds(0, HALO), :] = above[f, x]
                halo[f, x, pl.ds(EDGE - HALO, HALO), :] = below[f, x]
        for first, count in ((0, NY), (NY, EDGE)):
            pair = lax.broadcasted_iota(jnp.int32, (count, LANES), 1) // HALO
            firsts = [jnp.zeros((count, LANES), jnp.float32)] * 2
            lasts = list(firsts)
            for (f, x), (array, place) in column_places().items():
                if first:
                    cells = halo[f, x]
                elif array:
                    cells = layers[f, 2 if x else 1]
                else:
                    cells = grid[f, x - 1]
                here = pair == place
                moved = pltpu.roll(cells, place * HALO, 1) if place else cells
                firsts[array] = jnp.where(here, moved, firsts[array])
                moved = pltpu.roll(cells, (place * HALO + HALO) % LANES, 1)
                lasts[array] = jnp.where(here, moved, lasts[array])
            for array in range(2):
                low[array, pl.ds(first, count), :] = firsts[array]
                high[array, pl.ds(first, count), :] = lasts[array]

    packed = jax.ShapeDtypeStruct((2, WIDE_Y, LANES), jnp.float32)
    return pl.pallas_call(
        kernel,
        out_shape=[packed, packed],
        in_specs=[VMEM] * 4,
        out_specs=[VMEM] * 2,
        scratch_shapes=[pltpu.VMEM((FIELDS, NEAR_X, EDGE, LANES), jnp.float32)],
        name="z_columns",
    )(grid, layers, below, above)


def half_conductance(v):
    return 0.5 * (v * jnp.sqrt(v))


def whole_grid(grid, layers, below, above):
    def kernel(grid, layers, below, above, whole, halves):
        for f in range(FIELDS):
            for x in range(HALO):
                whole[f, x, pl.ds(0, NY), :] = layers[f, x]
                whole[f, HALO + NX + x, pl.ds(0, NY), :] = layers[f, HALO + x]

        def inside(x, carry):
            for f in range(FIELDS):
                whole[f, x + HALO, pl.ds(0, NY), :] = grid[f, x]
            return carry

        lax.fori_loop(0, NX, inside, 0)

        def beside(x, carry):
            for f in range(FIELDS):
                whole[f, x + 1, pl.ds(NY, HALO), :] = above[f, x]
                whole[f, x + 1, pl.ds(WIDE_Y - HALO, HALO), :] = below[f, x]
            return carry

        lax.fori_loop(0, NEAR_X, beside, 0)

        def conductances(x, carry):
            halves[x] = half_conductance(whole[0, x])
            return carry

        lax.fori_loop(0, WIDE_X, conductances, 0)

    return pl.pallas_call(
        kernel,
        out_shape=[
            jax.ShapeDtypeStruct((FIELDS, WIDE_X, WIDE_Y, LANES), jnp.float32),
            jax.ShapeDtypeStruct((WIDE_X, WIDE_Y, LANES), jnp.float32),
        ],
        in_specs=[VMEM] * 4,
        out_specs=[VMEM] * 2,
        cost_estimate=pl.CostEstimate(flops=2**22, bytes_accessed=2**21, transcendentals=0),
        name="whole_grid",
    )(grid, layers, below, above)


def section(here, beside, across, lane):
    def along_z(cells, other):
        return [
            pltpu.roll(jnp.where(lane == 0, other, cells), LANES - 1, 1),
            pltpu.roll(jnp.where(lane == LANES - 1, other, cells), 1, 1),
        ]

    def along_y(cells):
        return [pltpu.roll(cells, cells.shape[0] - 1, 0), pltpu.roll(cells, 1, 0)]

    cells, s = here
    mean = [s + n for n in along_y(s) + along_z(s, across[1]) + [b[1] for b in beside]]
    rates = []
    for f in range(FIELDS):
        v = cells[f]
        nearby = along_y(v) + along_z(v, across[0][f]) + [b[0][f] for b in beside]
        total = mean[0] * (nearby[0] - v)
        for m, n in zip(mean[1:], nearby[1:]):
            total = total + m * (n - v)
        rates.append(total)
    return rates


def two_sections(grid, halves, below, above):
    def kernel(grid, gs, below, above, out, beyond, first, first_beyond, bs, fs, fbs):
        lane = lax.broadcasted_iota(jnp.int32, (WIDE_Y, LANES), 1)
        packed = [above[0], above[1]], [below[0], below[1]]
        for (f, x), (array, place) in column_places().items():
            after, before = packed[0][array], packed[1][array]
            if place:
                after = pltpu.roll(after, LANES - place * HALO, 1)
            before = pltpu.roll(before, (LANES - HALO - place * HALO) % LANES, 1)
            beyond[f, x] = jnp.where(lane < LANES // 2, after, before)

        def conductances_beyond(x, carry):
            bs[x] = half_conductance(beyond[0, x])
            return carry

        lax.fori_loop(0, NEAR_X, conductances_beyond, 0)

        def at(ref, s, x):
            return [ref[f, x] for f in range(FIELDS)], s[x]

        def step(cells, rates):
            return [
                v + (TIME_STEP * c) * r for v, c, r in zip(cells, DIFFUSION, rates)
            ]

        def first_inside(x, carry):
            here = at(grid, gs, x + 1)
            rates = section(
                here, (at(grid, gs, x), at(grid, gs, x + 2)), at(beyond, bs, x), lane
            )
            fresh = step(here[0], rates)
            for f in range(FIELDS):
                first[f, x] = fresh[f]
            fs[x] = half_conductance(fresh[0])
            return carry

        lax.fori_loop(0, NEAR_X, first_inside, 0)

        def first_outside(x, carry):
            here = at(beyond, bs, x + 1)
            rates = section(
                here, (at(beyond, bs, x), at(beyond, bs, x + 2)), at(grid, gs, x + HALO), lane
            )
            fresh = step(here[0], rates)
            for f in range(FIELDS):
                first_beyond[f, x] = fresh[f]
            fbs[x] = half_conductance(fresh[0])
            return carry

        lax.fori_loop(0, NX, first_outside, 0)

        def second(x, carry):
            here = at(first, fs, x + 1)
            rates = section(
                here, (at(first, fs, x), at(first, fs, x + 2)), at(first_beyond, fbs, x), lane
            )
            fresh = step(here[0], rates)
            for f in range(FIELDS):
                out[f, x] = (0.5 * grid[f, x + HALO] + 0.5 * fresh[f])[:NY]
            return carry

        lax.fori_loop(0, NX, second, 0)

    def scratch(*shape):
        return pltpu.VMEM(shape + (WIDE_Y, LANES), jnp.float32)

    return pl.pallas_call(
        kernel,
        out_shape=jax.ShapeDtypeStruct((FIELDS, NX, NY, LANES), jnp.float32),
        in_specs=[VMEM] * 4,
        out_specs=VMEM,
        scratch_shapes=[
            scratch(FIELDS, NEAR_X),
            scratch(FIELDS, NEAR_X),
            scratch(FIELDS, NX),
            scratch(NEAR_X),
            scratch(NEAR_X),
            scratch(NX),
        ],
        name="two_sections",
    )(grid, halves, below, above)


def body(old_fields, new_owner, old_owner):
    across, along = lax.axis_size("gx"), lax.axis_size("gz")
    group_size = across * along
    box_count = new_owner.shape[0]
    capacity = 2 * (box_count // group_size)
    split = group_size <= 8
    joined = across == 2
    me = (lax.axis_index("gx") * along + lax.axis_index("gz")).reshape(1)
    departing = pack_boxes(old_fields, new_owner, me, group_size, capacity, split)
    if split:
        arrived = [departing[0]] + [
            lax.ppermute(departing[k], ("gx", "gz"), [(i, i ^ k) for i in range(group_size)])
            for k in range(1, group_size)
        ]
    else:
        arrived = [
            lax.all_to_all(departing[0], ("gx", "gz"), split_axis=0, concat_axis=0, tiled=True)
        ]
    held, *faces = boxes_in_place(arrived, old_owner, me, group_size, capacity, split, joined)
    if joined:
        faces = [lax.ppermute(faces[0], "gx", ring(across, 1))]
    else:
        faces = [lax.ppermute(x, "gx", ring(across, step)) for x, step in zip(faces, (-1, 1))]
    grid = grid_from_boxes(held)
    layers, low, high = x_faces_and_y_rows(grid, faces, joined)
    rows = lax.axis_size("gy")
    above = lax.ppermute(low, "gy", ring(rows, -1))
    below = lax.ppermute(high, "gy", ring(rows, 1))
    low, high = z_columns(grid, layers, below, above)
    whole, halves = whole_grid(grid, layers, below, above)
    above = lax.ppermute(low, "gz", ring(along, -1))
    below = lax.ppermute(high, "gz", ring(along, 1))
    return two_sections(whole, halves, below, above)


def solution(mesh):
    return jax.shard_map(
        body,
        mesh=mesh,
        in_specs=(P(("gx", "gy", "gz"), None, None), P(("gx", "gy", "gz")), P(("gx", "gy", "gz"))),
        out_specs=P(None, "gx", "gy", "gz"),
        check_vma=False,
    )
```

```python
import jax
import jax.numpy as jnp
from jax import lax
from jax.experimental import pallas as pl
from jax.experimental.pallas import tpu as pltpu
from jax.sharding import PartitionSpec as P

EDGE = 8
FIELDS = 4
BRICK_X = 2
BRICK_Y = 2
BRICK_Z = 16
CELLS = EDGE**3
LANES = 128
TILES = CELLS // LANES


DIFFUSION = (1.0, 3.3, 0.9, 1.2)
TIME_STEP = 0.012

VMEM = pl.BlockSpec(memory_space=pltpu.VMEM)
SMEM = pl.BlockSpec(memory_space=pltpu.SMEM)
ROOM = pltpu.CompilerParams(vmem_limit_bytes=16 * 2**20)


def rank_table(owner, table, counts, group, capacity, boxes, empty):
    def clear(i, carry):
        table[i] = empty
        return carry

    lax.fori_loop(0, group * capacity, clear, 0, unroll=16)
    for g in range(group):
        counts[g] = g * capacity

    def place(b, carry):
        o = owner[b]
        slot = counts[o]
        table[slot] = b
        counts[o] = slot + 1
        return carry

    lax.fori_loop(0, boxes, place, 0, unroll=8)


def pack_boxes(old_fields, new_owner, me, group, capacity, split):
    boxes = new_owner.shape[0]
    pieces = group if split else 1
    rows = group * capacity // pieces

    def kernel(me_ref, owner, fields, *refs):
        outs, (table, counts) = refs[:pieces], refs[pieces:]
        rank_table(owner, table, counts, group, capacity, boxes, 0)
        for k, out in enumerate(outs):
            base = (me_ref[0] ^ k) * capacity if split else 0

            def copy(r, carry, out=out, base=base):
                out[r] = fields[table[base + r]]
                return carry

            lax.fori_loop(0, rows, copy, 0, unroll=8)

    return pl.pallas_call(
        kernel,
        out_shape=[jax.ShapeDtypeStruct((rows,) + old_fields.shape[1:], jnp.float32)] * pieces,
        in_specs=[SMEM, SMEM, VMEM],
        out_specs=[VMEM] * pieces,
        scratch_shapes=[
            pltpu.SMEM((group * capacity,), jnp.int32),
            pltpu.SMEM((group,), jnp.int32),
        ],
        compiler_params=ROOM,
        name="pack_boxes",
    )(me, new_owner, old_fields)


def swap_boxes(columns):
    lane = lax.broadcasted_iota(jnp.int32, columns[0].shape, 1)
    for bit in range(4):
        width = EDGE << bit
        upper = (lane & width) != 0
        fresh = list(columns)
        for low in range(16):
            if low >> bit & 1:
                continue
            high = low | 1 << bit
            a, b = columns[low], columns[high]
            fresh[low] = jnp.where(upper, pltpu.roll(b, width, 1), a)
            fresh[high] = jnp.where(upper, b, pltpu.roll(a, LANES - width, 1))
        columns = fresh
    return columns


def ring(count, step):
    return [(i, (i + step) % count) for i in range(count)]


def boxes_in_place(arrived, old_owner, me, group, capacity, split, joined):
    boxes = old_owner.shape[0]
    pieces = len(arrived)
    rows = group * capacity // pieces
    half = boxes // BRICK_X
    face = (BRICK_Z, BRICK_Y * FIELDS, LANES)
    faces = [jax.ShapeDtypeStruct((2,) + face if joined else face, jnp.float32)] * (2 - joined)

    def kernel(me_ref, owner, *refs):
        ins, refs = refs[:pieces], refs[pieces:]
        held, outs, (table, counts) = refs[0], refs[1 : 1 + len(faces)], refs[1 + len(faces) :]
        rank_table(owner, table, counts, group, capacity, boxes, boxes)
        for k, rows_in in enumerate(ins):
            base = (me_ref[0] ^ k) * capacity if split else 0

            def scatter(r, carry, rows_in=rows_in, base=base):
                p = table[base + r]
                for t in range(TILES):
                    held[p, t // 2, pl.ds(t % 2 * FIELDS, FIELDS), :] = rows_in[
                        r, :, pl.ds(t * LANES, LANES)
                    ]
                return carry

            lax.fori_loop(0, rows, scatter, 0, unroll=4)
        for side in range(2):
            out = outs[0].at[side] if joined else outs[side]
            for by in range(BRICK_Y):
                for bz in range(BRICK_Z):
                    p = side * half + by * BRICK_Z + bz
                    out[bz, pl.ds(by * FIELDS, FIELDS), :] = held[
                        p, side, pl.ds(side * FIELDS, FIELDS), :
                    ]

    return pl.pallas_call(
        kernel,
        out_shape=[
            jax.ShapeDtypeStruct((boxes + 1, TILES // 2, 2 * FIELDS, LANES), jnp.float32)
        ]
        + faces,
        in_specs=[SMEM, SMEM] + [VMEM] * pieces,
        out_specs=[VMEM] * (1 + len(faces)),
        scratch_shapes=[
            pltpu.SMEM((group * capacity,), jnp.int32),
            pltpu.SMEM((group,), jnp.int32),
        ],
        compiler_params=ROOM,
        name="boxes_in_place",
    )(me, old_owner, *arrived)


HALO = 2
NX = BRICK_X * EDGE
NY = BRICK_Y * EDGE
WIDE_X = NX + 2 * HALO
WIDE_Y = NY + EDGE
NEAR_X = NX + 2


def lay_out(columns, turned, store):
    columns = swap_boxes(columns)
    for r in range(16):
        turned[pl.ds(r * 8, 8), :] = columns[r]
    for a in range(2):
        for i in range(2):
            for f in range(FIELDS):
                store(a, i, f, turned[pl.ds(i * 64 + a * FIELDS + f, 8, stride=8), :])


def grid_from_boxes(held):
    def kernel(held, grid, turned):
        for bx in range(BRICK_X):
            for by in range(BRICK_Y):
                first = (bx * BRICK_Y + by) * BRICK_Z
                for half in range(TILES // 2):

                    def store(t, i, f, rows, x=bx * EDGE + half * 4, by=by):
                        grid[f, x + t * 2 + i, pl.ds(by * EDGE, EDGE), :] = rows

                    lay_out([held[first + bz, half] for bz in range(BRICK_Z)], turned, store)

    return pl.pallas_call(
        kernel,
        out_shape=jax.ShapeDtypeStruct((FIELDS, NX, NY, LANES), jnp.float32),
        in_specs=[VMEM],
        out_specs=VMEM,
        scratch_shapes=[pltpu.VMEM((LANES, LANES), jnp.float32)],
        cost_estimate=pl.CostEstimate(flops=2**22, bytes_accessed=2**21, transcendentals=0),
        compiler_params=ROOM,
        name="grid_from_boxes",
    )(held)


def x_faces_and_y_rows(grid, faces, joined):
    def kernel(grid, *refs):
        ins, (layers, low, high, turned) = refs[: len(faces)], refs[len(faces) :]
        for side in range(2):
            face = ins[0].at[side] if joined else ins[side]

            def store(by, i, f, rows, first=0 if side else HALO):
                layers[f, first + i, pl.ds(by * EDGE, EDGE), :] = rows

            lay_out([face[bz] for bz in range(BRICK_Z)], turned, store)
        for f in range(FIELDS):
            for x in range(NEAR_X):
                cells = layers.at[f, 1 if x == 0 else 2] if x % (NX + 1) == 0 else grid.at[f, x - 1]
                low[f, x] = cells[pl.ds(0, HALO), :]
                high[f, x] = cells[pl.ds(NY - HALO, HALO), :]

    rows = jax.ShapeDtypeStruct((FIELDS, NEAR_X, HALO, LANES), jnp.float32)
    return pl.pallas_call(
        kernel,
        out_shape=[jax.ShapeDtypeStruct((FIELDS, 2 * HALO, NY, LANES), jnp.float32), rows, rows],
        in_specs=[VMEM] * (1 + len(faces)),
        out_specs=[VMEM] * 3,
        scratch_shapes=[pltpu.VMEM((LANES, LANES), jnp.float32)],
        compiler_params=ROOM,
        name="x_faces_and_y_rows",
    )(grid, *faces)


def column_places():
    places = {}
    for f in range(FIELDS):
        for x in range(NX):
            places[f, x + 1] = (0, f * NX + x)
        places[f, 0] = (1, f)
        places[f, NEAR_X - 1] = (1, FIELDS + f)
    return places


def z_columns(grid, layers, below, above):
    def kernel(grid, layers, below, above, low, high, halo):
        for f in range(FIELDS):
            for x in range(NEAR_X):
                halo[f, x, pl.ds(0, HALO), :] = above[f, x]
                halo[f, x, pl.ds(EDGE - HALO, HALO), :] = below[f, x]
        for first, count in ((0, NY), (NY, EDGE)):
            pair = lax.broadcasted_iota(jnp.int32, (count, LANES), 1) // HALO
            firsts = [jnp.zeros((count, LANES), jnp.float32)] * 2
            lasts = list(firsts)
            for (f, x), (array, place) in column_places().items():
                if first:
                    cells = halo[f, x]
                elif array:
                    cells = layers[f, 2 if x else 1]
                else:
                    cells = grid[f, x - 1]
                here = pair == place
                moved = pltpu.roll(cells, place * HALO, 1) if place else cells
                firsts[array] = jnp.where(here, moved, firsts[array])
                moved = pltpu.roll(cells, (place * HALO + HALO) % LANES, 1)
                lasts[array] = jnp.where(here, moved, lasts[array])
            for array in range(2):
                low[array, pl.ds(first, count), :] = firsts[array]
                high[array, pl.ds(first, count), :] = lasts[array]

    packed = jax.ShapeDtypeStruct((2, WIDE_Y, LANES), jnp.float32)
    return pl.pallas_call(
        kernel,
        out_shape=[packed, packed],
        in_specs=[VMEM] * 4,
        out_specs=[VMEM] * 2,
        scratch_shapes=[pltpu.VMEM((FIELDS, NEAR_X, EDGE, LANES), jnp.float32)],
        compiler_params=ROOM,
        name="z_columns",
    )(grid, layers, below, above)


def half_conductance(v):
    return 0.5 * (v * jnp.sqrt(v))


def whole_grid(grid, layers, below, above):
    def kernel(grid, layers, below, above, whole, halves):
        for f in range(FIELDS):
            for x in range(HALO):
                whole[f, x, pl.ds(0, NY), :] = layers[f, x]
                whole[f, HALO + NX + x, pl.ds(0, NY), :] = layers[f, HALO + x]

        def inside(x, carry):
            for f in range(FIELDS):
                whole[f, x + HALO, pl.ds(0, NY), :] = grid[f, x]
            return carry

        lax.fori_loop(0, NX, inside, 0, unroll=4)

        def beside(x, carry):
            for f in range(FIELDS):
                whole[f, x + 1, pl.ds(NY, HALO), :] = above[f, x]
                whole[f, x + 1, pl.ds(WIDE_Y - HALO, HALO), :] = below[f, x]
            return carry

        lax.fori_loop(0, NEAR_X, beside, 0, unroll=6)

        def conductances(x, carry):
            halves[x] = half_conductance(whole[0, x])
            return carry

        lax.fori_loop(0, WIDE_X, conductances, 0, unroll=5)

    return pl.pallas_call(
        kernel,
        out_shape=[
            jax.ShapeDtypeStruct((FIELDS, WIDE_X, WIDE_Y, LANES), jnp.float32),
            jax.ShapeDtypeStruct((WIDE_X, WIDE_Y, LANES), jnp.float32),
        ],
        in_specs=[VMEM] * 4,
        out_specs=[VMEM] * 2,
        cost_estimate=pl.CostEstimate(flops=2**22, bytes_accessed=2**21, transcendentals=0),
        compiler_params=ROOM,
        name="whole_grid",
    )(grid, layers, below, above)


def section(here, beside, across, lane):
    def along_z(cells, other):
        return [
            pltpu.roll(jnp.where(lane == 0, other, cells), LANES - 1, 1),
            pltpu.roll(jnp.where(lane == LANES - 1, other, cells), 1, 1),
        ]

    def along_y(cells):
        return [pltpu.roll(cells, cells.shape[0] - 1, 0), pltpu.roll(cells, 1, 0)]

    cells, s = here
    mean = [s + n for n in along_y(s) + along_z(s, across[1]) + [b[1] for b in beside]]
    rates = []
    for f in range(FIELDS):
        v = cells[f]
        nearby = along_y(v) + along_z(v, across[0][f]) + [b[0][f] for b in beside]
        total = mean[0] * (nearby[0] - v)
        for m, n in zip(mean[1:], nearby[1:]):
            total = total + m * (n - v)
        rates.append(total)
    return rates


def two_sections(grid, halves, below, above):
    def kernel(grid, gs, below, above, out, beyond, first, first_beyond, bs, fs, fbs):
        lane = lax.broadcasted_iota(jnp.int32, (WIDE_Y, LANES), 1)
        packed = [above[0], above[1]], [below[0], below[1]]
        for (f, x), (array, place) in column_places().items():
            after, before = packed[0][array], packed[1][array]
            if place:
                after = pltpu.roll(after, LANES - place * HALO, 1)
            before = pltpu.roll(before, (LANES - HALO - place * HALO) % LANES, 1)
            beyond[f, x] = jnp.where(lane < LANES // 2, after, before)

        def conductances_beyond(x, carry):
            bs[x] = half_conductance(beyond[0, x])
            return carry

        lax.fori_loop(0, NEAR_X, conductances_beyond, 0, unroll=6)

        def at(ref, s, x):
            return [ref[f, x] for f in range(FIELDS)], s[x]

        def step(cells, rates):
            return [
                v + (TIME_STEP * c) * r for v, c, r in zip(cells, DIFFUSION, rates)
            ]

        def first_inside(x, carry):
            here = at(grid, gs, x + 1)
            rates = section(
                here, (at(grid, gs, x), at(grid, gs, x + 2)), at(beyond, bs, x), lane
            )
            fresh = step(here[0], rates)
            for f in range(FIELDS):
                first[f, x] = fresh[f]
            fs[x] = half_conductance(fresh[0])
            return carry

        lax.fori_loop(0, NEAR_X, first_inside, 0, unroll=3)

        def first_outside(x, carry):
            here = at(beyond, bs, x + 1)
            rates = section(
                here, (at(beyond, bs, x), at(beyond, bs, x + 2)), at(grid, gs, x + HALO), lane
            )
            fresh = step(here[0], rates)
            for f in range(FIELDS):
                first_beyond[f, x] = fresh[f]
            fbs[x] = half_conductance(fresh[0])
            return carry

        lax.fori_loop(0, NX, first_outside, 0, unroll=4)

        def second(x, carry):
            here = at(first, fs, x + 1)
            rates = section(
                here, (at(first, fs, x), at(first, fs, x + 2)), at(first_beyond, fbs, x), lane
            )
            fresh = step(here[0], rates)
            for f in range(FIELDS):
                out[f, x] = (0.5 * grid[f, x + HALO] + 0.5 * fresh[f])[:NY]
            return carry

        lax.fori_loop(0, NX, second, 0, unroll=4)

    def scratch(*shape):
        return pltpu.VMEM(shape + (WIDE_Y, LANES), jnp.float32)

    return pl.pallas_call(
        kernel,
        out_shape=jax.ShapeDtypeStruct((FIELDS, NX, NY, LANES), jnp.float32),
        in_specs=[VMEM] * 4,
        out_specs=VMEM,
        scratch_shapes=[
            scratch(FIELDS, NEAR_X),
            scratch(FIELDS, NEAR_X),
            scratch(FIELDS, NX),
            scratch(NEAR_X),
            scratch(NEAR_X),
            scratch(NX),
        ],
        compiler_params=ROOM,
        name="two_sections",
    )(grid, halves, below, above)


def body(old_fields, new_owner, old_owner):
    across, along = lax.axis_size("gx"), lax.axis_size("gz")
    group_size = across * along
    box_count = new_owner.shape[0]
    capacity = 2 * (box_count // group_size)
    split = group_size <= 8
    joined = across == 2
    me = (lax.axis_index("gx") * along + lax.axis_index("gz")).reshape(1)
    departing = pack_boxes(old_fields, new_owner, me, group_size, capacity, split)
    if split:
        arrived = [departing[0]] + [
            lax.ppermute(departing[k], ("gx", "gz"), [(i, i ^ k) for i in range(group_size)])
            for k in range(1, group_size)
        ]
    else:
        arrived = [
            lax.all_to_all(departing[0], ("gx", "gz"), split_axis=0, concat_axis=0, tiled=True)
        ]
    held, *faces = boxes_in_place(arrived, old_owner, me, group_size, capacity, split, joined)
    if joined:
        faces = [lax.ppermute(faces[0], "gx", ring(across, 1))]
    else:
        faces = [lax.ppermute(x, "gx", ring(across, step)) for x, step in zip(faces, (-1, 1))]
    grid = grid_from_boxes(held)
    layers, low, high = x_faces_and_y_rows(grid, faces, joined)
    rows = lax.axis_size("gy")
    above = lax.ppermute(low, "gy", ring(rows, -1))
    below = lax.ppermute(high, "gy", ring(rows, 1))
    low, high = z_columns(grid, layers, below, above)
    whole, halves = whole_grid(grid, layers, below, above)
    above = lax.ppermute(low, "gz", ring(along, -1))
    below = lax.ppermute(high, "gz", ring(along, 1))
    return two_sections(whole, halves, below, above)


def solution(mesh):
    return jax.shard_map(
        body,
        mesh=mesh,
        in_specs=(P(("gx", "gy", "gz"), None, None), P(("gx", "gy", "gz")), P(("gx", "gy", "gz"))),
        out_specs=P(None, "gx", "gy", "gz"),
        check_vma=False,
    )
```

```python
import jax
import jax.numpy as jnp
from jax import lax
from jax.experimental import pallas as pl
from jax.experimental.pallas import tpu as pltpu
from jax.sharding import PartitionSpec as P

EDGE = 8
FIELDS = 4
BRICK_X = 2
BRICK_Y = 2
BRICK_Z = 16
CELLS = EDGE**3
LANES = 128

DIFFUSION = (1.0, 3.3, 0.9, 1.2)
TIME_STEP = 0.012

VMEM = pl.BlockSpec(memory_space=pltpu.VMEM)
SMEM = pl.BlockSpec(memory_space=pltpu.SMEM)
ROOM = pltpu.CompilerParams(vmem_limit_bytes=16 * 2**20)


def rank_table(owner, table, counts, group, capacity, boxes, empty):
    def clear(i, carry):
        table[i] = empty
        return carry

    lax.fori_loop(0, group * capacity, clear, 0, unroll=16)
    for g in range(group):
        counts[g] = g * capacity

    def place(b, carry):
        o = owner[b]
        slot = counts[o]
        table[slot] = b
        counts[o] = slot + 1
        return carry

    lax.fori_loop(0, boxes, place, 0, unroll=8)


HALVES = ((0, 3), (1, 2))


def ranked(new_owner, group, capacity):
    boxes = new_owner.shape[0]

    def kernel(owner, table, counts):
        rank_table(owner, table, counts, group, capacity, boxes, 0)

    return pl.pallas_call(
        kernel,
        out_shape=jax.ShapeDtypeStruct((group * capacity,), jnp.int32),
        in_specs=[SMEM],
        out_specs=SMEM,
        scratch_shapes=[pltpu.SMEM((group,), jnp.int32)],
        compiler_params=ROOM,
        cost_estimate=pl.CostEstimate(flops=0, bytes_accessed=2**22, transcendentals=0),
        name="ranked",
    )(new_owner)


def half_of(ref, half):
    return ref[half] if isinstance(ref, tuple) else ref.at[:, half]


def pieces_of(refs, whole):
    refs = list(refs)
    return [refs.pop(0) if one else (refs.pop(0), refs.pop(0)) for one in whole], refs


def pack_boxes(old_fields, table, me, rows, capacity, whole):
    def kernel(me_ref, table, fields, *refs):
        outs, _ = pieces_of(refs, whole)
        for k, out in enumerate(outs):
            base = (me_ref[0] ^ k) * capacity if len(whole) > 1 else 0

            def copy(r, carry, out=out, base=base):
                box = table[base + r]
                for half, pairs in enumerate(HALVES):
                    for n, t in enumerate(pairs):
                        half_of(out, half)[r, pl.ds(n * FIELDS, FIELDS), :] = fields[
                            box, :, pl.ds(t * LANES, LANES)
                        ]
                return carry

            lax.fori_loop(0, rows, copy, 0, unroll=8)

    def shape(*halves):
        return jax.ShapeDtypeStruct((rows,) + halves + (2 * FIELDS, LANES), jnp.float32)

    outs = [x for one in whole for x in ([shape(2)] if one else [shape()] * 2)]
    return pl.pallas_call(
        kernel,
        out_shape=outs,
        in_specs=[SMEM, SMEM, VMEM],
        out_specs=[VMEM] * len(outs),
        compiler_params=ROOM,
        name="pack_boxes",
    )(me, table, old_fields)


def swap_boxes(columns):
    lane = lax.broadcasted_iota(jnp.int32, columns[0].shape, 1)
    for bit in range(4):
        width = EDGE << bit
        upper = (lane & width) != 0
        fresh = list(columns)
        for low in range(16):
            if low >> bit & 1:
                continue
            high = low | 1 << bit
            a, b = columns[low], columns[high]
            fresh[low] = jnp.where(upper, pltpu.roll(b, width, 1), a)
            fresh[high] = jnp.where(upper, b, pltpu.roll(a, LANES - width, 1))
        columns = fresh
    return columns


def ring(count, step):
    return [(i, (i + step) % count) for i in range(count)]


HALO = 2
NX = BRICK_X * EDGE
NY = BRICK_Y * EDGE
WIDE_X = NX + 2 * HALO
WIDE_Y = NY + EDGE
NEAR_X = NX + 2


def lay_out(columns, turned, store):
    columns = swap_boxes(columns)
    for r in range(16):
        turned[pl.ds(r * 8, 8), :] = columns[r]
    for a in range(2):
        for i in range(2):
            for f in range(FIELDS):
                store(a, i, f, turned[pl.ds(i * 64 + a * FIELDS + f, 8, stride=8), :])


def place_rows(ins, held, table, me_ref, capacity):
    rows = ins[0].shape[0]
    for k, rows_in in enumerate(ins):
        base = (me_ref[0] ^ k) * capacity if len(ins) > 1 else 0

        def scatter(r, carry, rows_in=rows_in, base=base):
            held[table[base + r]] = rows_in[r]
            return carry

        lax.fori_loop(0, rows, scatter, 0, unroll=8)


def lay_out_half(held, turned, part, half):
    for bx in range(BRICK_X):
        for by in range(BRICK_Y):
            first = (bx * BRICK_Y + by) * BRICK_Z

            def store(a, i, f, rows, bx=bx, by=by):
                part[f, bx * 4 + a * 2 + i, pl.ds(by * EDGE, EDGE), :] = rows

            lay_out([held[first + bz] for bz in range(BRICK_Z)], turned, store)


def part_of(x):
    bx, pair, i = x // EDGE, x % EDGE // 2, x % 2
    half = 0 if pair in HALVES[0] else 1
    return half, bx * 4 + HALVES[half].index(pair) * 2 + i


PART = jax.ShapeDtypeStruct((FIELDS, NX // 2, NY, LANES), jnp.float32)
TURNED = pltpu.VMEM((LANES, LANES), jnp.float32)


LONG = pl.CostEstimate(flops=0, bytes_accessed=2**26, transcendentals=0)


def outer_boxes(arrived, old_owner, me, group, capacity, whole, joined):
    boxes = old_owner.shape[0]
    pieces = len(arrived)
    half = boxes // BRICK_X
    face = (BRICK_Z, BRICK_Y * FIELDS, LANES)
    faces = [jax.ShapeDtypeStruct((2,) + face if joined else face, jnp.float32)] * (2 - joined)

    def kernel(me_ref, owner, *refs):
        ins = [ref.at[:, 0] if one else ref for ref, one in zip(refs, whole)]
        refs = refs[pieces:]
        (table, part), outs = refs[:2], refs[2 : 2 + len(faces)]
        counts, held, turned = refs[2 + len(faces) :]
        rank_table(owner, table, counts, group, capacity, boxes, boxes)
        place_rows(ins, held, table, me_ref, capacity)
        for side in range(2):
            out = outs[0].at[side] if joined else outs[side]
            for by in range(BRICK_Y):
                for bz in range(BRICK_Z):
                    p = side * half + by * BRICK_Z + bz
                    out[bz, pl.ds(by * FIELDS, FIELDS), :] = held[p, pl.ds(side * FIELDS, FIELDS), :]
        lay_out_half(held, turned, part, 0)

    return pl.pallas_call(
        kernel,
        out_shape=[jax.ShapeDtypeStruct((group * capacity,), jnp.int32), PART] + faces,
        in_specs=[SMEM, SMEM] + [VMEM] * pieces,
        out_specs=[SMEM] + [VMEM] * (1 + len(faces)),
        scratch_shapes=[
            pltpu.SMEM((group,), jnp.int32),
            pltpu.VMEM((boxes + 1, 2 * FIELDS, LANES), jnp.float32),
            TURNED,
        ],
        compiler_params=ROOM,
        cost_estimate=LONG,
        name="outer_boxes",
    )(me, old_owner, *arrived)


def inner_boxes(arrived, table, me, boxes, capacity, whole):
    pieces = len(arrived)

    def kernel(me_ref, table, *refs):
        ins = [ref.at[:, 1] if one else ref for ref, one in zip(refs, whole)]
        inner, held, turned = refs[pieces:]
        place_rows(ins, held, table, me_ref, capacity)
        lay_out_half(held, turned, inner, 1)

    return pl.pallas_call(
        kernel,
        out_shape=PART,
        in_specs=[SMEM, SMEM] + [VMEM] * pieces,
        out_specs=VMEM,
        scratch_shapes=[pltpu.VMEM((boxes + 1, 2 * FIELDS, LANES), jnp.float32), TURNED],
        compiler_params=ROOM,
        cost_estimate=LONG,
        name="inner_boxes",
    )(me, table, *arrived)


def x_layers_and_y_rows(parts, faces, joined):
    def kernel(outer, inner, *refs):
        ins, (layers, low, high, turned) = refs[: len(faces)], refs[len(faces) :]
        for side in range(2):
            face = ins[0].at[side] if joined else ins[side]

            def store(by, i, f, rows, first=0 if side else HALO):
                layers[f, first + i, pl.ds(by * EDGE, EDGE), :] = rows

            lay_out([face[bz] for bz in range(BRICK_Z)], turned, store)
        for f in range(FIELDS):
            for x in range(NEAR_X):
                if x % (NX + 1) == 0:
                    cells = layers.at[f, 2 if x else 1]
                else:
                    half, layer = part_of(x - 1)
                    cells = (outer, inner)[half].at[f, layer]
                low[f, x] = cells[pl.ds(0, HALO), :]
                high[f, x] = cells[pl.ds(NY - HALO, HALO), :]

    rows = jax.ShapeDtypeStruct((FIELDS, NEAR_X, HALO, LANES), jnp.float32)
    return pl.pallas_call(
        kernel,
        out_shape=[jax.ShapeDtypeStruct((FIELDS, 2 * HALO, NY, LANES), jnp.float32), rows, rows],
        in_specs=[VMEM] * (2 + len(faces)),
        out_specs=[VMEM] * 3,
        scratch_shapes=[TURNED],
        compiler_params=ROOM,
        name="x_layers_and_y_rows",
    )(*parts, *faces)


def column_places():
    places = {}
    for f in range(FIELDS):
        for x in range(NX):
            places[f, x + 1] = (0, f * NX + x)
        places[f, 0] = (1, f)
        places[f, NEAR_X - 1] = (1, FIELDS + f)
    return places


def z_columns(parts, layers, below, above):
    def kernel(outer, inner, layers, below, above, low, high, halo):
        for f in range(FIELDS):
            for x in range(NEAR_X):
                halo[f, x, pl.ds(0, HALO), :] = above[f, x]
                halo[f, x, pl.ds(EDGE - HALO, HALO), :] = below[f, x]
        for first, count in ((0, NY), (NY, EDGE)):
            pair = lax.broadcasted_iota(jnp.int32, (count, LANES), 1) // HALO
            firsts = [jnp.zeros((count, LANES), jnp.float32)] * 2
            lasts = list(firsts)
            for (f, x), (array, place) in column_places().items():
                if first:
                    cells = halo[f, x]
                elif array:
                    cells = layers[f, 2 if x else 1]
                else:
                    half, layer = part_of(x - 1)
                    cells = (outer, inner)[half][f, layer]
                here = pair == place
                moved = pltpu.roll(cells, place * HALO, 1) if place else cells
                firsts[array] = jnp.where(here, moved, firsts[array])
                moved = pltpu.roll(cells, (place * HALO + HALO) % LANES, 1)
                lasts[array] = jnp.where(here, moved, lasts[array])
            for array in range(2):
                low[array, pl.ds(first, count), :] = firsts[array]
                high[array, pl.ds(first, count), :] = lasts[array]

    packed = jax.ShapeDtypeStruct((2, WIDE_Y, LANES), jnp.float32)
    return pl.pallas_call(
        kernel,
        out_shape=[packed, packed],
        in_specs=[VMEM] * 5,
        out_specs=[VMEM] * 2,
        scratch_shapes=[pltpu.VMEM((FIELDS, NEAR_X, EDGE, LANES), jnp.float32)],
        compiler_params=ROOM,
        name="z_columns",
    )(*parts, layers, below, above)


def half_conductance(v):
    return 0.5 * (v * jnp.sqrt(v))


def whole_grid(parts, layers, below, above):
    def kernel(outer, inner, layers, below, above, whole, halves):
        for f in range(FIELDS):
            for x in range(HALO):
                whole[f, x, pl.ds(0, NY), :] = layers[f, x]
                whole[f, HALO + NX + x, pl.ds(0, NY), :] = layers[f, HALO + x]

        for x in range(NX):
            half, layer = part_of(x)
            for f in range(FIELDS):
                whole[f, x + HALO, pl.ds(0, NY), :] = (outer, inner)[half][f, layer]

        def beside(x, carry):
            for f in range(FIELDS):
                whole[f, x + 1, pl.ds(NY, HALO), :] = above[f, x]
                whole[f, x + 1, pl.ds(WIDE_Y - HALO, HALO), :] = below[f, x]
            return carry

        lax.fori_loop(0, NEAR_X, beside, 0, unroll=6)

        def conductances(x, carry):
            halves[x] = half_conductance(whole[0, x])
            return carry

        lax.fori_loop(0, WIDE_X, conductances, 0, unroll=5)

    return pl.pallas_call(
        kernel,
        out_shape=[
            jax.ShapeDtypeStruct((FIELDS, WIDE_X, WIDE_Y, LANES), jnp.float32),
            jax.ShapeDtypeStruct((WIDE_X, WIDE_Y, LANES), jnp.float32),
        ],
        in_specs=[VMEM] * 5,
        out_specs=[VMEM] * 2,
        cost_estimate=pl.CostEstimate(flops=2**22, bytes_accessed=2**21, transcendentals=0),
        compiler_params=ROOM,
        name="whole_grid",
    )(*parts, layers, below, above)


def section(here, beside, across, lane):
    def along_z(cells, other):
        return [
            pltpu.roll(jnp.where(lane == 0, other, cells), LANES - 1, 1),
            pltpu.roll(jnp.where(lane == LANES - 1, other, cells), 1, 1),
        ]

    def along_y(cells):
        return [pltpu.roll(cells, cells.shape[0] - 1, 0), pltpu.roll(cells, 1, 0)]

    cells, s = here
    mean = [s + n for n in along_y(s) + along_z(s, across[1]) + [b[1] for b in beside]]
    rates = []
    for f in range(FIELDS):
        v = cells[f]
        nearby = along_y(v) + along_z(v, across[0][f]) + [b[0][f] for b in beside]
        total = mean[0] * (nearby[0] - v)
        for m, n in zip(mean[1:], nearby[1:]):
            total = total + m * (n - v)
        rates.append(total)
    return rates


def two_sections(grid, halves, below, above):
    def kernel(grid, gs, below, above, out, beyond, first, first_beyond, bs, fs, fbs):
        lane = lax.broadcasted_iota(jnp.int32, (WIDE_Y, LANES), 1)
        packed = [above[0], above[1]], [below[0], below[1]]
        for (f, x), (array, place) in column_places().items():
            after, before = packed[0][array], packed[1][array]
            if place:
                after = pltpu.roll(after, LANES - place * HALO, 1)
            before = pltpu.roll(before, (LANES - HALO - place * HALO) % LANES, 1)
            beyond[f, x] = jnp.where(lane < LANES // 2, after, before)

        def conductances_beyond(x, carry):
            bs[x] = half_conductance(beyond[0, x])
            return carry

        lax.fori_loop(0, NEAR_X, conductances_beyond, 0, unroll=6)

        def at(ref, s, x):
            return [ref[f, x] for f in range(FIELDS)], s[x]

        def step(cells, rates):
            return [
                v + (TIME_STEP * c) * r for v, c, r in zip(cells, DIFFUSION, rates)
            ]

        def first_inside(x, carry):
            here = at(grid, gs, x + 1)
            rates = section(
                here, (at(grid, gs, x), at(grid, gs, x + 2)), at(beyond, bs, x), lane
            )
            fresh = step(here[0], rates)
            for f in range(FIELDS):
                first[f, x] = fresh[f]
            fs[x] = half_conductance(fresh[0])
            return carry

        lax.fori_loop(0, NEAR_X, first_inside, 0, unroll=3)

        def first_outside(x, carry):
            here = at(beyond, bs, x + 1)
            rates = section(
                here, (at(beyond, bs, x), at(beyond, bs, x + 2)), at(grid, gs, x + HALO), lane
            )
            fresh = step(here[0], rates)
            for f in range(FIELDS):
                first_beyond[f, x] = fresh[f]
            fbs[x] = half_conductance(fresh[0])
            return carry

        lax.fori_loop(0, NX, first_outside, 0, unroll=4)

        def second(x, carry):
            here = at(first, fs, x + 1)
            rates = section(
                here, (at(first, fs, x), at(first, fs, x + 2)), at(first_beyond, fbs, x), lane
            )
            fresh = step(here[0], rates)
            for f in range(FIELDS):
                out[f, x] = (0.5 * grid[f, x + HALO] + 0.5 * fresh[f])[:NY]
            return carry

        lax.fori_loop(0, NX, second, 0, unroll=4)

    def scratch(*shape):
        return pltpu.VMEM(shape + (WIDE_Y, LANES), jnp.float32)

    return pl.pallas_call(
        kernel,
        out_shape=jax.ShapeDtypeStruct((FIELDS, NX, NY, LANES), jnp.float32),
        in_specs=[VMEM] * 4,
        out_specs=VMEM,
        scratch_shapes=[
            scratch(FIELDS, NEAR_X),
            scratch(FIELDS, NEAR_X),
            scratch(FIELDS, NX),
            scratch(NEAR_X),
            scratch(NEAR_X),
            scratch(NX),
        ],
        compiler_params=ROOM,
        name="two_sections",
    )(grid, halves, below, above)


def body(old_fields, new_owner, old_owner):
    across, along = lax.axis_size("gx"), lax.axis_size("gz")
    group_size = across * along
    box_count = new_owner.shape[0]
    capacity = 2 * (box_count // group_size)
    split = group_size <= 8
    joined = False
    me = (lax.axis_index("gx") * along + lax.axis_index("gz")).reshape(1)
    table = ranked(new_owner, group_size, capacity)
    if split:
        far = [k for k in range(group_size) if k % along >= along // 2]
        whole = [k not in far for k in range(group_size)]
        rows = capacity
    else:
        far, whole, rows = [], [False], group_size * capacity
    sent, _ = pieces_of(pack_boxes(old_fields, table, me, rows, capacity, whole), whole)

    def move(piece, k):
        if not split:
            return lax.all_to_all(piece, ("gx", "gz"), split_axis=0, concat_axis=0, tiled=True)
        return lax.ppermute(piece, ("gx", "gz"), [(i, i ^ k) for i in range(group_size)])

    arrived = {0: sent[0]} if split else {0: tuple(move(x, 0) for x in sent[0])}
    for k in far:
        arrived[k] = (move(sent[k][0], k), None)
    for k in range(1, len(sent)):
        if k not in far:
            arrived[k] = move(sent[k], k)
    for k in far:
        arrived[k] = (arrived[k][0], move(sent[k][1], k))
    first, second = (
        [arrived[k] if one else arrived[k][half] for k, one in enumerate(whole)] for half in range(2)
    )
    table, outer, *faces = outer_boxes(first, old_owner, me, group_size, capacity, whole, joined)
    if joined:
        faces = [lax.ppermute(faces[0], "gx", ring(across, 1))]
    else:
        faces = [lax.ppermute(x, "gx", ring(across, step)) for x, step in zip(faces, (-1, 1))]
    inner = inner_boxes(second, table, me, box_count, capacity, whole)
    parts = outer, inner
    layers, low, high = x_layers_and_y_rows(parts, faces, joined)
    rows = lax.axis_size("gy")
    above = lax.ppermute(low, "gy", ring(rows, -1))
    below = lax.ppermute(high, "gy", ring(rows, 1))
    low, high = z_columns(parts, layers, below, above)
    whole, halves = whole_grid(parts, layers, below, above)
    above = lax.ppermute(low, "gz", ring(along, -1))
    below = lax.ppermute(high, "gz", ring(along, 1))
    return two_sections(whole, halves, below, above)


def solution(mesh):
    return jax.shard_map(
        body,
        mesh=mesh,
        in_specs=(P(("gx", "gy", "gz"), None, None), P(("gx", "gy", "gz")), P(("gx", "gy", "gz"))),
        out_specs=P(None, "gx", "gy", "gz"),
        check_vma=False,
    )
```

```python
import jax
import jax.numpy as jnp
from jax import lax
from jax.experimental import pallas as pl
from jax.experimental.pallas import tpu as pltpu
from jax.sharding import PartitionSpec as P

EDGE = 8
FIELDS = 4
BRICK_X = 2
BRICK_Y = 2
BRICK_Z = 16
CELLS = EDGE**3
LANES = 128
TILES = CELLS // LANES
BOX = (TILES // 2, 2 * FIELDS, LANES)


DIFFUSION = (1.0, 3.3, 0.9, 1.2)
TIME_STEP = 0.012

VMEM = pl.BlockSpec(memory_space=pltpu.VMEM)
SMEM = pl.BlockSpec(memory_space=pltpu.SMEM)
ROOM = pltpu.CompilerParams(vmem_limit_bytes=16 * 2**20)


def rank_table(owner, table, counts, group, capacity, boxes, empty):
    def clear(i, carry):
        table[i] = empty
        return carry

    lax.fori_loop(0, group * capacity, clear, 0, unroll=16)
    for g in range(group):
        counts[g] = g * capacity

    def place(b, carry):
        o = owner[b]
        slot = counts[o]
        table[slot] = b
        counts[o] = slot + 1
        return carry

    lax.fori_loop(0, boxes, place, 0, unroll=8)


def pack_boxes(old_fields, new_owner, me, group, capacity, split):
    boxes = new_owner.shape[0]
    pieces = group if split else 1
    rows = group * capacity // pieces

    def kernel(me_ref, owner, fields, *refs):
        outs, (table, counts) = refs[:pieces], refs[pieces:]
        rank_table(owner, table, counts, group, capacity, boxes, 0)
        for k, out in enumerate(outs):
            base = (me_ref[0] ^ k) * capacity if split else 0

            def copy(r, carry, out=out, base=base):
                box = table[base + r]
                for t in range(TILES):
                    out[r, t // 2, pl.ds(t % 2 * FIELDS, FIELDS), :] = fields[
                        box, :, pl.ds(t * LANES, LANES)
                    ]
                return carry

            lax.fori_loop(0, rows, copy, 0, unroll=8)

    return pl.pallas_call(
        kernel,
        out_shape=[jax.ShapeDtypeStruct((rows,) + BOX, jnp.float32)] * pieces,
        in_specs=[SMEM, SMEM, VMEM],
        out_specs=[VMEM] * pieces,
        scratch_shapes=[
            pltpu.SMEM((group * capacity,), jnp.int32),
            pltpu.SMEM((group,), jnp.int32),
        ],
        compiler_params=ROOM,
        name="pack_boxes",
    )(me, new_owner, old_fields)


def swap_boxes(columns):
    lane = lax.broadcasted_iota(jnp.int32, columns[0].shape, 1)
    for bit in range(4):
        width = EDGE << bit
        upper = (lane & width) != 0
        fresh = list(columns)
        for low in range(16):
            if low >> bit & 1:
                continue
            high = low | 1 << bit
            a, b = columns[low], columns[high]
            fresh[low] = jnp.where(upper, pltpu.roll(b, width, 1), a)
            fresh[high] = jnp.where(upper, b, pltpu.roll(a, LANES - width, 1))
        columns = fresh
    return columns


def ring(count, step):
    return [(i, (i + step) % count) for i in range(count)]


def boxes_in_place(arrived, old_owner, me, group, capacity, split, joined):
    boxes = old_owner.shape[0]
    pieces = len(arrived)
    rows = group * capacity // pieces
    half = boxes // BRICK_X
    face = (BRICK_Z, BRICK_Y * FIELDS, LANES)
    faces = [jax.ShapeDtypeStruct((2,) + face if joined else face, jnp.float32)] * (2 - joined)
    end = jax.ShapeDtypeStruct((BRICK_X * BRICK_Y,) + BOX, jnp.float32)

    def kernel(me_ref, owner, *refs):
        ins, refs = refs[:pieces], refs[pieces:]
        (held, low, high), refs = refs[:3], refs[3:]
        outs, (table, counts) = refs[: len(faces)], refs[len(faces) :]
        rank_table(owner, table, counts, group, capacity, boxes, boxes)
        for k, rows_in in enumerate(ins):
            base = (me_ref[0] ^ k) * capacity if split else 0

            def scatter(r, carry, rows_in=rows_in, base=base):
                held[table[base + r]] = rows_in[r]
                return carry

            lax.fori_loop(0, rows, scatter, 0, unroll=8)
        for side in range(2):
            out = outs[0].at[side] if joined else outs[side]
            for by in range(BRICK_Y):
                for bz in range(BRICK_Z):
                    p = side * half + by * BRICK_Z + bz
                    out[bz, pl.ds(by * FIELDS, FIELDS), :] = held[
                        p, side, pl.ds(side * FIELDS, FIELDS), :
                    ]
        for b in range(BRICK_X * BRICK_Y):
            low[b] = held[b * BRICK_Z]
            high[b] = held[b * BRICK_Z + BRICK_Z - 1]

    return pl.pallas_call(
        kernel,
        out_shape=[jax.ShapeDtypeStruct((boxes + 1,) + BOX, jnp.float32), end, end] + faces,
        in_specs=[SMEM, SMEM] + [VMEM] * pieces,
        out_specs=[VMEM] * (3 + len(faces)),
        scratch_shapes=[
            pltpu.SMEM((group * capacity,), jnp.int32),
            pltpu.SMEM((group,), jnp.int32),
        ],
        compiler_params=ROOM,
        name="boxes_in_place",
    )(me, old_owner, *arrived)


HALO = 2
NX = BRICK_X * EDGE
NY = BRICK_Y * EDGE
WIDE_X = NX + 2 * HALO
WIDE_Y = NY + EDGE
NEAR_X = NX + 2


def lay_out(columns, turned, store):
    for r in range(16):
        turned[pl.ds(r * 8, 8), :] = columns[r]
    for a in range(2):
        for i in range(2):
            for f in range(FIELDS):
                store(a, i, f, turned[pl.ds(i * 64 + a * FIELDS + f, 8, stride=8), :])


def grid_from_boxes(held):
    def kernel(held, grid, turned):
        for bx in range(BRICK_X):
            for by in range(BRICK_Y):
                first = (bx * BRICK_Y + by) * BRICK_Z
                for half in range(TILES // 2):

                    def store(t, i, f, rows, x=bx * EDGE + half * 4, by=by):
                        grid[f, x + t * 2 + i, pl.ds(by * EDGE, EDGE), :] = rows

                    columns = swap_boxes([held[first + bz, half] for bz in range(BRICK_Z)])
                    lay_out(columns, turned, store)

    return pl.pallas_call(
        kernel,
        out_shape=jax.ShapeDtypeStruct((FIELDS, NX, NY, LANES), jnp.float32),
        in_specs=[VMEM],
        out_specs=VMEM,
        scratch_shapes=[pltpu.VMEM((LANES, LANES), jnp.float32)],
        cost_estimate=pl.CostEstimate(flops=2**22, bytes_accessed=2**21, transcendentals=0),
        compiler_params=ROOM,
        name="grid_from_boxes",
    )(held)


ROWS = FIELDS * NEAR_X * HALO
EDGES = ROWS + EDGE


def row_of(f, x):
    return (f * NEAR_X + x) * HALO


def faces_and_rows(grid, faces, above, below, joined):
    side_shape = (FIELDS, NY, LANES)
    sides = [jax.ShapeDtypeStruct((2,) + side_shape if joined else side_shape, jnp.float32)] * (
        2 - joined
    )

    def kernel(grid, above, below, *refs):
        ins, refs = refs[: len(faces)], refs[len(faces) :]
        (layers, beyond, low, high), refs = refs[:4], refs[4:]
        outs, (turned,) = refs[: len(sides)], refs[len(sides) :]
        for side in range(2):
            face = ins[0].at[side] if joined else ins[side]

            def store(by, i, f, rows, first=0 if side else HALO):
                layers[f, first + i, pl.ds(by * EDGE, EDGE), :] = rows

            lay_out(swap_boxes([face[bz] for bz in range(BRICK_Z)]), turned, store)
        lane = lax.broadcasted_iota(jnp.int32, (EDGE, LANES), 1)
        for bx in range(BRICK_X):
            for by in range(BRICK_Y):
                for half in range(TILES // 2):
                    after, before = above[bx * BRICK_Y + by, half], below[bx * BRICK_Y + by, half]
                    columns = [
                        jnp.where(
                            lane < LANES // 2,
                            pltpu.roll(after, (LANES - EDGE * r) % LANES, 1),
                            pltpu.roll(before, LANES - EDGE - EDGE * r, 1),
                        )
                        for r in range(16)
                    ]

                    def store(t, i, f, rows, x=bx * EDGE + half * 4, by=by):
                        beyond[f, x + t * 2 + i, pl.ds(by * EDGE, EDGE), :] = rows

                    lay_out(columns, turned, store)
        for f in range(FIELDS):
            for x in range(NEAR_X):
                cells = layers.at[f, 2 if x else 1] if x % (NX + 1) == 0 else grid.at[f, x - 1]
                low[pl.ds(row_of(f, x), HALO), :] = cells[pl.ds(0, HALO), :]
                high[pl.ds(row_of(f, x), HALO), :] = cells[pl.ds(NY - HALO, HALO), :]
        pair = lane // 2
        for first, out in ((0, low), (NY - EDGE, high)):
            edge = jnp.zeros((EDGE, LANES), jnp.float32)
            for f in range(FIELDS):
                for x in range(NX):
                    place = f * NX + x
                    moved = pltpu.roll(beyond[f, x, pl.ds(first, EDGE), :], 2 * place + 1, 1)
                    edge = jnp.where(pair == place, moved, edge)
            out[pl.ds(ROWS, EDGE), :] = edge
        for side in range(2):
            out = outs[0].at[side] if joined else outs[side]
            for f in range(FIELDS):
                out[f] = beyond[f, side * (NX - 1)]

    rows = jax.ShapeDtypeStruct((EDGES, LANES), jnp.float32)
    return pl.pallas_call(
        kernel,
        out_shape=[
            jax.ShapeDtypeStruct((FIELDS, 2 * HALO, NY, LANES), jnp.float32),
            jax.ShapeDtypeStruct((FIELDS, NX, NY, LANES), jnp.float32),
            rows,
            rows,
        ]
        + sides,
        in_specs=[VMEM] * (3 + len(faces)),
        out_specs=[VMEM] * (4 + len(sides)),
        scratch_shapes=[pltpu.VMEM((LANES, LANES), jnp.float32)],
        compiler_params=ROOM,
        name="faces_and_rows",
    )(grid, above, below, *faces)


def half_conductance(v):
    return 0.5 * (v * jnp.sqrt(v))


def wide_grid(grid, layers):
    def kernel(grid, layers, wide, halves):
        for f in range(FIELDS):
            for x in range(WIDE_X):
                inside = HALO <= x < HALO + NX
                wide[f, x] = grid[f, x - HALO] if inside else layers[f, x % (NX + HALO) + (x > HALO) * HALO]

        def conductances(x, carry):
            halves[x] = half_conductance(wide[0, x])
            return carry

        lax.fori_loop(0, WIDE_X, conductances, 0, unroll=5)

    return pl.pallas_call(
        kernel,
        out_shape=[
            jax.ShapeDtypeStruct((FIELDS, WIDE_X, NY, LANES), jnp.float32),
            jax.ShapeDtypeStruct((WIDE_X, NY, LANES), jnp.float32),
        ],
        in_specs=[VMEM] * 2,
        out_specs=[VMEM] * 2,
        compiler_params=ROOM,
        cost_estimate=pl.CostEstimate(flops=2**22, bytes_accessed=2**21, transcendentals=0),
        name="wide_grid",
    )(grid, layers)


def section(here, beside, across, rows):
    lane = lax.broadcasted_iota(jnp.int32, (rows, LANES), 1)

    def nearby(cells, other, left, right):
        inside, other = cells[:rows], other[:rows]
        return [
            pltpu.roll(cells, WIDE_Y - 1, 0)[:rows],
            pltpu.roll(cells, 1, 0)[:rows],
            pltpu.roll(jnp.where(lane == 0, other, inside), LANES - 1, 1),
            pltpu.roll(jnp.where(lane == LANES - 1, other, inside), 1, 1),
            left[:rows],
            right[:rows],
        ]

    (cells, s), ((left, s_left), (right, s_right)), (other, s_other) = here, beside, across
    mean = [s[:rows] + n for n in nearby(s, s_other, s_left, s_right)]
    rates = []
    for f in range(FIELDS):
        v = cells[f][:rows]
        terms = [m * (n - v) for m, n in zip(mean, nearby(cells[f], other[f], left[f], right[f]))]
        rates.append(sum(terms[1:], terms[0]))
    return rates


def two_sections(wide, halves, beyond, above, below, sides, joined):
    def kernel(wide, halves, inner_beyond, above, below, *refs):
        ins, refs = refs[: len(sides)], refs[len(sides) :]
        out, ring_rows, ring_halves, beyond, first, first_beyond, bs, fs, fbs = refs
        for f in range(FIELDS):
            for x in range(NEAR_X):
                ring_rows[f, x, pl.ds(0, HALO), :] = above[pl.ds(row_of(f, x), HALO), :]
                ring_rows[f, x, pl.ds(EDGE - HALO, HALO), :] = below[pl.ds(row_of(f, x), HALO), :]
        row = lax.broadcasted_iota(jnp.int32, (EDGE, LANES), 0)
        edge = jnp.where(row < EDGE // 2, above[pl.ds(ROWS, EDGE), :], below[pl.ds(ROWS, EDGE), :])
        for f in range(FIELDS):
            for x in range(NX):
                beyond[f, x + 1, pl.ds(0, NY), :] = inner_beyond[f, x]
                beyond[f, x + 1, pl.ds(NY, EDGE), :] = pltpu.roll(
                    edge, LANES - 1 - 2 * (f * NX + x), 1
                )
            for side in range(2):
                got = ins[0].at[side] if joined else ins[side]
                beyond[f, 0 if side else NX + 1, pl.ds(0, NY), :] = got[f]

        def conductances(x, carry):
            ring_halves[x] = half_conductance(ring_rows[0, x])
            bs[x] = half_conductance(beyond[0, x])
            return carry

        lax.fori_loop(0, NEAR_X, conductances, 0, unroll=6)

        def at(ref, s, x):
            return [ref[f, x] for f in range(FIELDS)], s[x]

        def whole(x):
            cells = [
                jnp.concatenate([wide[f, x + 1], ring_rows[f, x]], 0) for f in range(FIELDS)
            ]
            return cells, jnp.concatenate([halves[x + 1], ring_halves[x]], 0)

        def step(cells, rates):
            rows = rates[0].shape[0]
            return [
                v[:rows] + (TIME_STEP * c) * r for v, c, r in zip(cells, DIFFUSION, rates)
            ]

        def first_inside(x, carry):
            here = whole(x)
            rates = section(here, (narrow(x), narrow(x + 2)), at(beyond, bs, x), WIDE_Y)
            fresh = step(here[0], rates)
            for f in range(FIELDS):
                first[f, x] = fresh[f]
            fs[x] = half_conductance(fresh[0])
            return carry

        def narrow(x):
            inner = jnp.clip(x - 1, 0, NEAR_X - 1)
            cells = [
                jnp.concatenate([wide[f, x], ring_rows[f, inner]], 0) for f in range(FIELDS)
            ]
            return cells, jnp.concatenate([halves[x], ring_halves[inner]], 0)

        lax.fori_loop(0, NEAR_X, first_inside, 0, unroll=3)

        def first_outside(x, carry):
            here = at(beyond, bs, x + 1)
            across = [wide[f, x + HALO] for f in range(FIELDS)], halves[x + HALO]
            rates = section(here, (at(beyond, bs, x), at(beyond, bs, x + 2)), across, NY)
            fresh = step(here[0], rates)
            for f in range(FIELDS):
                first_beyond[f, x] = fresh[f]
            fbs[x] = half_conductance(fresh[0])
            return carry

        lax.fori_loop(0, NX, first_outside, 0, unroll=4)

        def second(x, carry):
            here = at(first, fs, x + 1)
            beside = at(first, fs, x), at(first, fs, x + 2)
            fresh = step(here[0], section(here, beside, at(first_beyond, fbs, x), NY))
            for f in range(FIELDS):
                out[f, x] = 0.5 * wide[f, x + HALO] + 0.5 * fresh[f]
            return carry

        lax.fori_loop(0, NX, second, 0, unroll=4)

    def scratch(*shape):
        return pltpu.VMEM(shape + (LANES,), jnp.float32)

    return pl.pallas_call(
        kernel,
        out_shape=jax.ShapeDtypeStruct((FIELDS, NX, NY, LANES), jnp.float32),
        in_specs=[VMEM] * (5 + len(sides)),
        out_specs=VMEM,
        scratch_shapes=[
            scratch(FIELDS, NEAR_X, EDGE),
            scratch(NEAR_X, EDGE),
            scratch(FIELDS, NEAR_X, WIDE_Y),
            scratch(FIELDS, NEAR_X, WIDE_Y),
            scratch(FIELDS, NX, NY),
            scratch(NEAR_X, WIDE_Y),
            scratch(NEAR_X, WIDE_Y),
            scratch(NX, NY),
        ],
        compiler_params=ROOM,
        name="two_sections",
    )(wide, halves, beyond, above, below, *sides)


def body(old_fields, new_owner, old_owner):
    across, along = lax.axis_size("gx"), lax.axis_size("gz")
    group_size = across * along
    box_count = new_owner.shape[0]
    capacity = 2 * (box_count // group_size)
    split = group_size <= 8
    joined = across == 2
    me = (lax.axis_index("gx") * along + lax.axis_index("gz")).reshape(1)
    departing = pack_boxes(old_fields, new_owner, me, group_size, capacity, split)
    if split:
        arrived = [departing[0]] + [
            lax.ppermute(departing[k], ("gx", "gz"), [(i, i ^ k) for i in range(group_size)])
            for k in range(1, group_size)
        ]
    else:
        arrived = [
            lax.all_to_all(departing[0], ("gx", "gz"), split_axis=0, concat_axis=0, tiled=True)
        ]
    held, low, high, *faces = boxes_in_place(
        arrived, old_owner, me, group_size, capacity, split, joined
    )

    def along_x(sides):
        if joined:
            return [lax.ppermute(sides[0], "gx", ring(across, 1))]
        return [lax.ppermute(side, "gx", ring(across, step)) for side, step in zip(sides, (-1, 1))]

    faces = along_x(faces)
    above = lax.ppermute(low, "gz", ring(along, -1))
    below = lax.ppermute(high, "gz", ring(along, 1))
    grid = grid_from_boxes(held)
    layers, beyond, low, high, *sides = faces_and_rows(grid, faces, above, below, joined)
    rows = lax.axis_size("gy")
    above = lax.ppermute(low, "gy", ring(rows, -1))
    below = lax.ppermute(high, "gy", ring(rows, 1))
    sides = along_x(sides)
    wide, halves = wide_grid(grid, layers)
    return two_sections(wide, halves, beyond, above, below, sides, joined)


def solution(mesh):
    return jax.shard_map(
        body,
        mesh=mesh,
        in_specs=(P(("gx", "gy", "gz"), None, None), P(("gx", "gy", "gz")), P(("gx", "gy", "gz"))),
        out_specs=P(None, "gx", "gy", "gz"),
        check_vma=False,
    )
```

```python
import jax
import jax.numpy as jnp
from jax import lax
from jax.experimental import pallas as pl
from jax.experimental.pallas import tpu as pltpu
from jax.sharding import PartitionSpec as P

EDGE = 8
FIELDS = 4
BRICK_X = 2
BRICK_Y = 2
BRICK_Z = 16
CELLS = EDGE**3
LANES = 128
TILES = CELLS // LANES
BOX = (TILES // 2, 2 * FIELDS, LANES)


DIFFUSION = (1.0, 3.3, 0.9, 1.2)
TIME_STEP = 0.012

VMEM = pl.BlockSpec(memory_space=pltpu.VMEM)
SMEM = pl.BlockSpec(memory_space=pltpu.SMEM)
ROOM = pltpu.CompilerParams(vmem_limit_bytes=16 * 2**20)


def rank_table(owner, table, counts, group, capacity, boxes, empty):
    def clear(i, carry):
        table[i] = empty
        return carry

    lax.fori_loop(0, group * capacity, clear, 0, unroll=16)
    for g in range(group):
        counts[g] = g * capacity

    def place(b, carry):
        o = owner[b]
        slot = counts[o]
        table[slot] = b
        counts[o] = slot + 1
        return carry

    lax.fori_loop(0, boxes, place, 0, unroll=8)


def pack_boxes(old_fields, new_owner, me, group, capacity, split):
    boxes = new_owner.shape[0]
    pieces = group if split else 1
    rows = group * capacity // pieces

    def kernel(me_ref, owner, fields, *refs):
        outs, (table, counts) = refs[:pieces], refs[pieces:]
        rank_table(owner, table, counts, group, capacity, boxes, 0)
        for k, out in enumerate(outs):
            base = (me_ref[0] ^ k) * capacity if split else 0

            def copy(r, carry, out=out, base=base):
                box = table[base + r]
                for t in range(TILES):
                    out[r, t // 2, pl.ds(t % 2 * FIELDS, FIELDS), :] = fields[
                        box, :, pl.ds(t * LANES, LANES)
                    ]
                return carry

            lax.fori_loop(0, rows, copy, 0, unroll=8)

    return pl.pallas_call(
        kernel,
        out_shape=[jax.ShapeDtypeStruct((rows,) + BOX, jnp.float32)] * pieces,
        in_specs=[SMEM, SMEM, VMEM],
        out_specs=[VMEM] * pieces,
        scratch_shapes=[
            pltpu.SMEM((group * capacity,), jnp.int32),
            pltpu.SMEM((group,), jnp.int32),
        ],
        compiler_params=ROOM,
        name="pack_boxes",
    )(me, new_owner, old_fields)


def position_table(old_owner, group, capacity):
    boxes = old_owner.shape[0]

    def kernel(owner, table, counts):
        rank_table(owner, table, counts, group, capacity, boxes, boxes)

    return pl.pallas_call(
        kernel,
        out_shape=jax.ShapeDtypeStruct((group * capacity,), jnp.int32),
        in_specs=[SMEM],
        out_specs=SMEM,
        scratch_shapes=[pltpu.SMEM((group,), jnp.int32)],
        compiler_params=ROOM,
        cost_estimate=pl.CostEstimate(flops=0, bytes_accessed=2**22, transcendentals=0),
        name="position_table",
    )(old_owner)


def swap_boxes(columns):
    lane = lax.broadcasted_iota(jnp.int32, columns[0].shape, 1)
    for bit in range(4):
        width = EDGE << bit
        upper = (lane & width) != 0
        fresh = list(columns)
        for low in range(16):
            if low >> bit & 1:
                continue
            high = low | 1 << bit
            a, b = columns[low], columns[high]
            fresh[low] = jnp.where(upper, pltpu.roll(b, width, 1), a)
            fresh[high] = jnp.where(upper, b, pltpu.roll(a, LANES - width, 1))
        columns = fresh
    return columns


def ring(count, step):
    return [(i, (i + step) % count) for i in range(count)]


def boxes_in_place(arrived, table, me, boxes, capacity, split, joined):
    pieces = len(arrived)
    rows = table.shape[0] // pieces
    half = boxes // BRICK_X
    face = (BRICK_Z, BRICK_Y * FIELDS, LANES)
    faces = [jax.ShapeDtypeStruct((2,) + face if joined else face, jnp.float32)] * (2 - joined)
    end = jax.ShapeDtypeStruct((2, 2 * FIELDS, LANES), jnp.float32)

    def kernel(me_ref, table, *refs):
        ins, refs = refs[:pieces], refs[pieces:]
        held, low, high, *outs = refs
        for k, rows_in in enumerate(ins):
            base = (me_ref[0] ^ k) * capacity if split else 0

            def scatter(r, carry, rows_in=rows_in, base=base):
                held[table[base + r]] = rows_in[r]
                return carry

            lax.fori_loop(0, rows, scatter, 0, unroll=8)
        for side in range(2):
            out = outs[0].at[side] if joined else outs[side]
            for by in range(BRICK_Y):
                for bz in range(BRICK_Z):
                    p = side * half + by * BRICK_Z + bz
                    out[bz, pl.ds(by * FIELDS, FIELDS), :] = held[
                        p, side, pl.ds(side * FIELDS, FIELDS), :
                    ]
        pair = lax.broadcasted_iota(jnp.int32, (2 * FIELDS, LANES), 1) % EDGE // HALO
        for out, bz, first in ((low, 0, 0), (high, BRICK_Z - 1, EDGE - HALO)):
            for group in range(2):
                packed = jnp.zeros((2 * FIELDS, LANES), jnp.float32)
                for n in range(4):
                    b, part = divmod(group * 4 + n, 2)
                    cells = held[b * BRICK_Z + bz, part]
                    shift = (n * HALO - first) % LANES
                    packed = jnp.where(pair == n, pltpu.roll(cells, shift, 1) if shift else cells, packed)
                out[group] = packed

    return pl.pallas_call(
        kernel,
        out_shape=[jax.ShapeDtypeStruct((boxes + 1,) + BOX, jnp.float32), end, end] + faces,
        in_specs=[SMEM, SMEM] + [VMEM] * pieces,
        out_specs=[VMEM] * (3 + len(faces)),
        compiler_params=ROOM,
        name="boxes_in_place",
    )(me, table, *arrived)


HALO = 2
NX = BRICK_X * EDGE
NY = BRICK_Y * EDGE
WIDE_X = NX + 2 * HALO
WIDE_Y = NY + EDGE
NEAR_X = NX + 2


def lay_out(columns, turned, store):
    for r in range(16):
        turned[pl.ds(r * 8, 8), :] = columns[r]
    for a in range(2):
        for i in range(2):
            for f in range(FIELDS):
                store(a, i, f, turned[pl.ds(i * 64 + a * FIELDS + f, 8, stride=8), :])


def grid_from_boxes(held):
    def kernel(held, grid, turned):
        for bx in range(BRICK_X):
            for by in range(BRICK_Y):
                first = (bx * BRICK_Y + by) * BRICK_Z
                for half in range(TILES // 2):

                    def store(t, i, f, rows, x=bx * EDGE + half * 4, by=by):
                        grid[f, x + t * 2 + i, pl.ds(by * EDGE, EDGE), :] = rows

                    columns = swap_boxes([held[first + bz, half] for bz in range(BRICK_Z)])
                    lay_out(columns, turned, store)

    return pl.pallas_call(
        kernel,
        out_shape=jax.ShapeDtypeStruct((FIELDS, NX, NY, LANES), jnp.float32),
        in_specs=[VMEM],
        out_specs=VMEM,
        scratch_shapes=[pltpu.VMEM((LANES, LANES), jnp.float32)],
        cost_estimate=pl.CostEstimate(flops=2**22, bytes_accessed=2**21, transcendentals=0),
        compiler_params=ROOM,
        name="grid_from_boxes",
    )(held)


ROWS = FIELDS * NEAR_X * HALO
EDGES = ROWS + EDGE


def row_of(f, x):
    return (f * NEAR_X + x) * HALO


def side_place(side, f):
    return side * FIELDS + f


def faces_and_rows(grid, faces, above, below, joined):
    sides = [jax.ShapeDtypeStruct((NY, LANES), jnp.float32)] * (2 - joined)

    def kernel(grid, above, below, *refs):
        ins, refs = refs[: len(faces)], refs[len(faces) :]
        (layers, beyond, low, high), refs = refs[:4], refs[4:]
        outs, (turned,) = refs[: len(sides)], refs[len(sides) :]
        for side in range(2):
            face = ins[0].at[side] if joined else ins[side]

            def store(by, i, f, rows, first=0 if side else HALO):
                layers[f, first + i, pl.ds(by * EDGE, EDGE), :] = rows

            lay_out(swap_boxes([face[bz] for bz in range(BRICK_Z)]), turned, store)
        lane = lax.broadcasted_iota(jnp.int32, (EDGE, LANES), 1)
        for bx in range(BRICK_X):
            for by in range(BRICK_Y):
                for half in range(TILES // 2):
                    group, n = divmod((bx * BRICK_Y + by) * 2 + half, 4)
                    after, before = above[group], below[group]
                    columns = [
                        jnp.where(
                            lane < LANES // 2,
                            pltpu.roll(after, (LANES - EDGE * r - HALO * n) % LANES, 1),
                            pltpu.roll(before, (2 * LANES - HALO - EDGE * r - HALO * n) % LANES, 1),
                        )
                        for r in range(16)
                    ]

                    def store(t, i, f, rows, x=bx * EDGE + half * 4, by=by):
                        beyond[f, x + t * 2 + i, pl.ds(by * EDGE, EDGE), :] = rows

                    lay_out(columns, turned, store)
        for f in range(FIELDS):
            for x in range(NEAR_X):
                cells = layers.at[f, 2 if x else 1] if x % (NX + 1) == 0 else grid.at[f, x - 1]
                low[pl.ds(row_of(f, x), HALO), :] = cells[pl.ds(0, HALO), :]
                high[pl.ds(row_of(f, x), HALO), :] = cells[pl.ds(NY - HALO, HALO), :]
        pair = lane // 2
        for first, out in ((0, low), (NY - EDGE, high)):
            edge = jnp.zeros((EDGE, LANES), jnp.float32)
            for f in range(FIELDS):
                for x in range(NX):
                    place = f * NX + x
                    moved = pltpu.roll(beyond[f, x, pl.ds(first, EDGE), :], 2 * place + 1, 1)
                    edge = jnp.where(pair == place, moved, edge)
            out[pl.ds(ROWS, EDGE), :] = edge
        pair = lax.broadcasted_iota(jnp.int32, (NY, LANES), 1) // 2
        edges = [jnp.zeros((NY, LANES), jnp.float32)] * 2
        for side in range(2):
            for f in range(FIELDS):
                moved = pltpu.roll(beyond[f, side * (NX - 1)], 2 * side_place(side, f) + 1, 1)
                edges[side] = jnp.where(pair == side_place(side, f), moved, edges[side])
        if joined:
            outs[0][...] = jnp.where(pair < FIELDS, edges[0], edges[1])
        else:
            for out, edge in zip(outs, edges):
                out[...] = edge

    rows = jax.ShapeDtypeStruct((EDGES, LANES), jnp.float32)
    return pl.pallas_call(
        kernel,
        out_shape=[
            jax.ShapeDtypeStruct((FIELDS, 2 * HALO, NY, LANES), jnp.float32),
            jax.ShapeDtypeStruct((FIELDS, NX, NY, LANES), jnp.float32),
            rows,
            rows,
        ]
        + sides,
        in_specs=[VMEM] * (3 + len(faces)),
        out_specs=[VMEM] * (4 + len(sides)),
        scratch_shapes=[pltpu.VMEM((LANES, LANES), jnp.float32)],
        compiler_params=ROOM,
        name="faces_and_rows",
    )(grid, above, below, *faces)


def half_conductance(v):
    return 0.5 * (v * jnp.sqrt(v))


def step(cells, rates):
    return [v + (TIME_STEP * c) * r for v, c, r in zip(cells, DIFFUSION, rates)]


def rates(cells, s, beside):
    means = [s + n for _, n in beside]
    sums = []
    for f, v in enumerate(cells):
        terms = [m * (fields[f] - v) for m, (fields, _) in zip(means, beside)]
        sums.append(sum(terms[1:], terms[0]))
    return sums


def each(function, cells, *others):
    fields, s = cells
    columns = zip(fields, *[other[0] for other in others])
    return [function(*c) for c in columns], function(s, *[other[1] for other in others])


def z_beside(cells, across):
    lane = lax.broadcasted_iota(jnp.int32, cells[1].shape, 1)

    def after(v, other):
        return pltpu.roll(jnp.where(lane == 0, other, v), LANES - 1, 1)

    def before(v, other):
        return pltpu.roll(jnp.where(lane == LANES - 1, other, v), 1, 1)

    return [each(after, cells, across), each(before, cells, across)]


def y_beside(cells):
    row = lax.broadcasted_iota(jnp.int32, (NY, LANES), 0)

    def after(v):
        return jnp.where(row == NY - 1, v, pltpu.roll(v, NY - 1, 0))

    def before(v):
        return jnp.where(row == 0, v, pltpu.roll(v, 1, 0))

    return [each(after, cells), each(before, cells)]


def first_inside(grid, layers, beyond):
    def kernel(grid, layers, beyond, wide, halves, first, first_beyond, halves_beyond):
        for f in range(FIELDS):
            for x in range(HALO):
                wide[f, x] = layers[f, x]
                wide[f, HALO + NX + x] = layers[f, HALO + x]
        for x in range(HALO):
            halves[x] = half_conductance(layers[0, x])
            halves[HALO + NX + x] = half_conductance(layers[0, HALO + x])

        def prepare(x, carry):
            for f in range(FIELDS):
                wide[f, x + HALO] = grid[f, x]
            halves[x + HALO] = half_conductance(grid[0, x])
            halves_beyond[x] = half_conductance(beyond[0, x])
            return carry

        lax.fori_loop(0, NX, prepare, 0, unroll=4)

        def at(ref, s, x):
            return [ref[f, x] for f in range(FIELDS)], s[x]

        def inside(x, carry):
            here, over = at(wide, halves, x + HALO), at(beyond, halves_beyond, x)
            beside = [at(wide, halves, x + HALO - 1), at(wide, halves, x + HALO + 1)]
            beside += y_beside(here) + z_beside(here, over)
            for f, v in enumerate(step(here[0], rates(*here, beside))):
                first[f, x] = v
            left, right = jnp.maximum(x - 1, 0), jnp.minimum(x + 1, NX - 1)
            beside = [at(beyond, halves_beyond, left), at(beyond, halves_beyond, right)]
            beside += y_beside(over) + z_beside(over, here)
            for f, v in enumerate(step(over[0], rates(*over, beside))):
                first_beyond[f, x] = v
            return carry

        lax.fori_loop(0, NX, inside, 0, unroll=2)

    def shape(*sizes):
        return jax.ShapeDtypeStruct(sizes + (NY, LANES), jnp.float32)

    return pl.pallas_call(
        kernel,
        out_shape=[
            shape(FIELDS, WIDE_X),
            shape(WIDE_X),
            shape(FIELDS, NX),
            shape(FIELDS, NX),
            shape(NX),
        ],
        in_specs=[VMEM] * 3,
        out_specs=[VMEM] * 5,
        compiler_params=ROOM,
        cost_estimate=pl.CostEstimate(flops=2**22, bytes_accessed=2**21, transcendentals=0),
        name="first_inside",
    )(grid, layers, beyond)


def last_sections(wide, halves, first, first_beyond, beyond, halves_beyond, above, below, sides):
    def kernel(wide, halves, first_in, beyond_in, beyond, halves_beyond, above, below, *refs):
        ins, (out, edges, first, first_beyond, around, fs, fbs) = refs[: len(sides)], refs[len(sides) :]
        factors = [TIME_STEP * c for c in DIFFUSION]
        row = lax.broadcasted_iota(jnp.int32, (EDGE, LANES), 0)

        def side_edge(side):
            packed = ins[0 if len(ins) == 1 else side][...]
            fields = [
                pltpu.roll(packed, LANES - 1 - 2 * side_place(side, f), 1) for f in range(FIELDS)
            ]
            return fields, half_conductance(fields[0])

        edge = jnp.where(
            row < EDGE // 2,
            pltpu.roll(below[pl.ds(ROWS, EDGE), :], 1, 0),
            pltpu.roll(above[pl.ds(ROWS, EDGE), :], EDGE - 1, 0),
        )
        for f in range(FIELDS):
            for x in range(NX):
                edges[pl.ds((f * NX + x) * EDGE, EDGE), :] = pltpu.roll(
                    edge, LANES - 1 - 2 * (f * NX + x), 1
                )

        def at(ref, s, x):
            return [ref[f, x] for f in range(FIELDS)], s[x]

        for side, x in ((1, 0), (0, NX + 1)):
            here = at(wide, halves, x + 1)
            beside = [at(wide, halves, x), at(wide, halves, x + 2)]
            beside += y_beside(here) + z_beside(here, side_edge(side))
            for f, v in enumerate(step(here[0], rates(*here, beside))):
                first[pl.ds((f * NEAR_X + x) * NY, NY), :] = v
        for f in range(FIELDS):
            for x in range(NX):
                first[pl.ds((f * NEAR_X + x + 1) * NY, NY), :] = first_in[f, x]

        wide_rows = wide.reshape(FIELDS * WIDE_X * NY, LANES)
        half_rows = halves.reshape(WIDE_X * NY, LANES)

        def sent(ref, depth, f, x, count):
            return ref[pl.ds(row_of(f, x) + depth, count, stride=HALO), :]

        for ref, depth, y, tile_row in ((below, 1, 0, 7), (above, 0, NY - 1, 0)):
            for x, count in ((0, 8), (8, 8), (16, 2)):
                s = half_rows[pl.ds((x + 1) * NY + y, count, stride=NY), :]
                mean = s + half_conductance(sent(ref, depth, 0, x, count))
                for f in range(FIELDS):
                    v = wide_rows[pl.ds((f * WIDE_X + x + 1) * NY + y, count, stride=NY), :]
                    rows = pl.ds((f * NEAR_X + x) * NY + y, count, stride=NY)
                    more = mean * (sent(ref, depth, f, x, count) - v)
                    first[rows, :] = first[rows, :] + factors[f] * more
            for x in (0, 8):

                def line(depth, shift):
                    fields = [sent(ref, depth, f, x + 1 + shift, 8) for f in range(FIELDS)]
                    return fields, half_conductance(fields[0])

                here = line(depth, 0)
                inner = (
                    [
                        wide_rows[pl.ds((f * WIDE_X + x + HALO) * NY + y, 8, stride=NY), :]
                        for f in range(FIELDS)
                    ],
                    half_rows[pl.ds((x + HALO) * NY + y, 8, stride=NY), :],
                )
                over = [
                    edges[pl.ds((f * NX + x) * EDGE + 7 - tile_row, 8, stride=EDGE), :]
                    for f in range(FIELDS)
                ]
                beside = [line(1 - depth, 0), inner, line(depth, -1), line(depth, 1)]
                beside += z_beside(here, (over, half_conductance(over[0])))
                for f, v in enumerate(step(here[0], rates(*here, beside))):
                    around[pl.ds((f * NX + x) * EDGE + tile_row, 8, stride=EDGE), :] = v

        for x in range(NX):
            s = halves_beyond[x]
            near = half_conductance(edges[pl.ds(x * EDGE, EDGE), :])
            for f in range(FIELDS):
                tile = edges[pl.ds((f * NX + x) * EDGE, EDGE), :]
                v, fresh = beyond[f, x], beyond_in[f, x]
                more = [
                    jnp.where(row == at_row, (near + s[n * EDGE :][:EDGE]) * (tile - v[n * EDGE :][:EDGE]), 0.0)
                    for n, at_row in enumerate((0, EDGE - 1))
                ]
                first_beyond[f, x] = fresh + factors[f] * jnp.concatenate(more, 0)
        for side, x in ((1, 0), (0, NX - 1)):
            fields, s = side_edge(side)
            for f in range(FIELDS):
                more = (s + halves_beyond[x]) * (fields[f] - beyond[f, x])
                first_beyond[f, x] = first_beyond[f, x] + factors[f] * more

        def near(x):
            return [
                first[pl.ds(pl.multiple_of((f * NEAR_X + x) * NY, NY), NY), :] for f in range(FIELDS)
            ]

        def conductances(x, carry):
            fs[x] = half_conductance(near(x)[0])
            return carry

        lax.fori_loop(0, NEAR_X, conductances, 0, unroll=6)

        def conductances_beyond(x, carry):
            fbs[x] = half_conductance(first_beyond[0, x])
            return carry

        lax.fori_loop(0, NX, conductances_beyond, 0, unroll=4)

        def second(x, carry):
            here = near(x + 1), fs[x + 1]
            tiles = [
                around[pl.ds(pl.multiple_of((f * NX + x) * EDGE, EDGE), EDGE), :]
                for f in range(FIELDS)
            ]
            ring_of = each(
                lambda v, tile: jnp.concatenate([v, tile], 0), here, (tiles, half_conductance(tiles[0]))
            )
            beside = [(near(x), fs[x]), (near(x + 2), fs[x + 2])]
            beside += [
                each(lambda v: pltpu.roll(v, WIDE_Y - 1, 0)[:NY], ring_of),
                each(lambda v: pltpu.roll(v, 1, 0)[:NY], ring_of),
            ]
            beside += z_beside(here, at(first_beyond, fbs, x))
            for f, v in enumerate(step(here[0], rates(*here, beside))):
                out[f, x] = 0.5 * wide[f, x + HALO] + 0.5 * v
            return carry

        lax.fori_loop(0, NX, second, 0, unroll=4)

    def scratch(*shape):
        return pltpu.VMEM(shape + (LANES,), jnp.float32)

    return pl.pallas_call(
        kernel,
        out_shape=jax.ShapeDtypeStruct((FIELDS, NX, NY, LANES), jnp.float32),
        in_specs=[VMEM] * (8 + len(sides)),
        out_specs=VMEM,
        scratch_shapes=[
            scratch(FIELDS * NX * EDGE),
            scratch(FIELDS * NEAR_X * NY),
            scratch(FIELDS, NX, NY),
            scratch(FIELDS * NX * EDGE),
            scratch(NEAR_X, NY),
            scratch(NX, NY),
        ],
        compiler_params=ROOM,
        name="last_sections",
    )(wide, halves, first, first_beyond, beyond, halves_beyond, above, below, *sides)


def body(old_fields, new_owner, old_owner):
    across, along = lax.axis_size("gx"), lax.axis_size("gz")
    group_size = across * along
    box_count = new_owner.shape[0]
    capacity = 2 * (box_count // group_size)
    split = group_size <= 8
    joined = across == 2
    me = (lax.axis_index("gx") * along + lax.axis_index("gz")).reshape(1)
    departing = pack_boxes(old_fields, new_owner, me, group_size, capacity, split)
    table = position_table(old_owner, group_size, capacity)
    if split:
        arrived = [departing[0]] + [
            lax.ppermute(departing[k], ("gx", "gz"), [(i, i ^ k) for i in range(group_size)])
            for k in range(1, group_size)
        ]
    else:
        arrived = [
            lax.all_to_all(departing[0], ("gx", "gz"), split_axis=0, concat_axis=0, tiled=True)
        ]
    held, low, high, *faces = boxes_in_place(
        arrived, table, me, box_count, capacity, split, joined
    )

    def along_x(sides):
        if joined:
            return [lax.ppermute(sides[0], "gx", ring(across, 1))]
        return [lax.ppermute(side, "gx", ring(across, step)) for side, step in zip(sides, (-1, 1))]

    faces = along_x(faces)
    above = lax.ppermute(low, "gz", ring(along, -1))
    below = lax.ppermute(high, "gz", ring(along, 1))
    grid = grid_from_boxes(held)
    layers, beyond, low, high, *sides = faces_and_rows(grid, faces, above, below, joined)
    rows = lax.axis_size("gy")
    above = lax.ppermute(low, "gy", ring(rows, -1))
    below = lax.ppermute(high, "gy", ring(rows, 1))
    sides = along_x(sides)
    wide, halves, first, first_beyond, halves_beyond = first_inside(grid, layers, beyond)
    return last_sections(
        wide, halves, first, first_beyond, beyond, halves_beyond, above, below, sides
    )


def solution(mesh):
    return jax.shard_map(
        body,
        mesh=mesh,
        in_specs=(P(("gx", "gy", "gz"), None, None), P(("gx", "gy", "gz")), P(("gx", "gy", "gz"))),
        out_specs=P(None, "gx", "gy", "gz"),
        check_vma=False,
    )
```

```python
import jax
import jax.numpy as jnp
from jax import lax
from jax.experimental import pallas as pl
from jax.experimental.pallas import tpu as pltpu
from jax.sharding import PartitionSpec as P

EDGE = 8
FIELDS = 4
BRICK_X = 2
BRICK_Y = 2
BRICK_Z = 16
CELLS = EDGE**3
LANES = 128
TILES = CELLS // LANES
BOX = (TILES // 2, 2 * FIELDS, LANES)


DIFFUSION = (1.0, 3.3, 0.9, 1.2)
TIME_STEP = 0.012

VMEM = pl.BlockSpec(memory_space=pltpu.VMEM)
SMEM = pl.BlockSpec(memory_space=pltpu.SMEM)
ROOM = pltpu.CompilerParams(vmem_limit_bytes=16 * 2**20)


def rank_table(owner, table, counts, group, capacity, boxes, empty):
    def clear(i, carry):
        table[i] = empty
        return carry

    lax.fori_loop(0, group * capacity, clear, 0, unroll=16)
    for g in range(group):
        counts[g] = g * capacity

    def place(b, carry):
        o = owner[b]
        slot = counts[o]
        table[slot] = b
        counts[o] = slot + 1
        return carry

    lax.fori_loop(0, boxes, place, 0, unroll=8)


def pack_boxes(old_fields, new_owner, me, group, capacity, split):
    boxes = new_owner.shape[0]
    pieces = group if split else 1
    rows = group * capacity // pieces

    def kernel(me_ref, owner, fields, *refs):
        outs, (table, counts) = refs[:pieces], refs[pieces:]
        rank_table(owner, table, counts, group, capacity, boxes, 0)
        for k, out in enumerate(outs):
            base = (me_ref[0] ^ k) * capacity if split else 0

            def copy(r, carry, out=out, base=base):
                box = table[base + r]
                for t in range(TILES):
                    out[r, t // 2, pl.ds(t % 2 * FIELDS, FIELDS), :] = fields[
                        box, :, pl.ds(t * LANES, LANES)
                    ]
                return carry

            lax.fori_loop(0, rows, copy, 0, unroll=8)

    return pl.pallas_call(
        kernel,
        out_shape=[jax.ShapeDtypeStruct((rows,) + BOX, jnp.float32)] * pieces,
        in_specs=[SMEM, SMEM, VMEM],
        out_specs=[VMEM] * pieces,
        scratch_shapes=[
            pltpu.SMEM((group * capacity,), jnp.int32),
            pltpu.SMEM((group,), jnp.int32),
        ],
        compiler_params=ROOM,
        name="pack_boxes",
    )(me, new_owner, old_fields)


def position_table(old_owner, group, capacity):
    boxes = old_owner.shape[0]

    def kernel(owner, table, counts):
        rank_table(owner, table, counts, group, capacity, boxes, boxes)

    return pl.pallas_call(
        kernel,
        out_shape=jax.ShapeDtypeStruct((group * capacity,), jnp.int32),
        in_specs=[SMEM],
        out_specs=SMEM,
        scratch_shapes=[pltpu.SMEM((group,), jnp.int32)],
        compiler_params=ROOM,
        cost_estimate=pl.CostEstimate(flops=0, bytes_accessed=2**22, transcendentals=0),
        name="position_table",
    )(old_owner)


def swap_boxes(columns):
    lane = lax.broadcasted_iota(jnp.int32, columns[0].shape, 1)
    for bit in range(4):
        width = EDGE << bit
        upper = (lane & width) != 0
        fresh = list(columns)
        for low in range(16):
            if low >> bit & 1:
                continue
            high = low | 1 << bit
            a, b = columns[low], columns[high]
            fresh[low] = jnp.where(upper, pltpu.roll(b, width, 1), a)
            fresh[high] = jnp.where(upper, b, pltpu.roll(a, LANES - width, 1))
        columns = fresh
    return columns


def ring(count, step):
    return [(i, (i + step) % count) for i in range(count)]


def with_both_sides(axis, first, second):
    count = lax.axis_size(axis)
    pairs = [(i, i ^ 1) for i in range(count)], [((i + 1) % count, ((i ^ 1) + 1) % count) for i in range(count)]
    return [lax.ppermute(x, axis, p) for x, p in zip((first, second), pairs)]


def by_parity(odd, low, high):
    return jnp.where(odd, low, high), jnp.where(odd, high, low)


def boxes_in_place(arrived, table, me, boxes, capacity, split, joined):
    pieces = len(arrived)
    rows = table.shape[0] // pieces
    half = boxes // BRICK_X
    face = (BRICK_Z, BRICK_Y * FIELDS, LANES)
    faces = [jax.ShapeDtypeStruct((2,) + face if joined else face, jnp.float32)] * (2 - joined)
    end = jax.ShapeDtypeStruct((2, 2 * FIELDS, LANES), jnp.float32)

    def kernel(me_ref, table, *refs):
        ins, refs = refs[:pieces], refs[pieces:]
        held, low, high, *outs = refs
        odd = me_ref[2] != 0
        for k, rows_in in enumerate(ins):
            base = (me_ref[0] ^ k) * capacity if split else 0

            def scatter(r, carry, rows_in=rows_in, base=base):
                held[table[base + r]] = rows_in[r]
                return carry

            lax.fori_loop(0, rows, scatter, 0, unroll=8)
        for side in range(2):
            out = outs[0].at[side] if joined else outs[side]
            for by in range(BRICK_Y):
                for bz in range(BRICK_Z):
                    p = side * half + by * BRICK_Z + bz
                    out[bz, pl.ds(by * FIELDS, FIELDS), :] = held[
                        p, side, pl.ds(side * FIELDS, FIELDS), :
                    ]
        pair = lax.broadcasted_iota(jnp.int32, (2 * FIELDS, LANES), 1) % EDGE // HALO
        for group in range(2):
            ends = []
            for bz, first in ((0, 0), (BRICK_Z - 1, EDGE - HALO)):
                packed = jnp.zeros((2 * FIELDS, LANES), jnp.float32)
                for n in range(4):
                    b, part = divmod(group * 4 + n, 2)
                    cells = held[b * BRICK_Z + bz, part]
                    shift = (n * HALO - first) % LANES
                    packed = jnp.where(pair == n, pltpu.roll(cells, shift, 1) if shift else cells, packed)
                ends.append(packed)
            low[group], high[group] = by_parity(odd, *ends)

    return pl.pallas_call(
        kernel,
        out_shape=[jax.ShapeDtypeStruct((boxes + 1,) + BOX, jnp.float32), end, end] + faces,
        in_specs=[SMEM, SMEM] + [VMEM] * pieces,
        out_specs=[VMEM] * (3 + len(faces)),
        compiler_params=ROOM,
        name="boxes_in_place",
    )(me, table, *arrived)


HALO = 2
NX = BRICK_X * EDGE
NY = BRICK_Y * EDGE
WIDE_X = NX + 2 * HALO
WIDE_Y = NY + EDGE
NEAR_X = NX + 2


def lay_out(columns, turned, store):
    for r in range(16):
        turned[pl.ds(r * 8, 8), :] = columns[r]
    for a in range(2):
        for i in range(2):
            for f in range(FIELDS):
                store(a, i, f, turned[pl.ds(i * 64 + a * FIELDS + f, 8, stride=8), :])


def grid_from_boxes(held):
    def kernel(held, grid, turned):
        for bx in range(BRICK_X):
            for by in range(BRICK_Y):
                first = (bx * BRICK_Y + by) * BRICK_Z
                for half in range(TILES // 2):

                    def store(t, i, f, rows, x=bx * EDGE + half * 4, by=by):
                        grid[f, x + t * 2 + i, pl.ds(by * EDGE, EDGE), :] = rows

                    columns = swap_boxes([held[first + bz, half] for bz in range(BRICK_Z)])
                    lay_out(columns, turned, store)

    return pl.pallas_call(
        kernel,
        out_shape=jax.ShapeDtypeStruct((FIELDS, NX, NY, LANES), jnp.float32),
        in_specs=[VMEM],
        out_specs=VMEM,
        scratch_shapes=[pltpu.VMEM((LANES, LANES), jnp.float32)],
        cost_estimate=pl.CostEstimate(flops=2**22, bytes_accessed=2**21, transcendentals=0),
        compiler_params=ROOM,
        name="grid_from_boxes",
    )(held)


ROWS = FIELDS * NEAR_X * HALO
EDGES = ROWS + EDGE


def row_of(f, x):
    return (f * NEAR_X + x) * HALO


def side_place(side, f):
    return side * FIELDS + f


def faces_and_rows(grid, faces, me, ends, joined):
    sides = [jax.ShapeDtypeStruct((NY, LANES), jnp.float32)] * (2 - joined)

    def kernel(me_ref, grid, near, other, *refs):
        ins, refs = refs[: len(faces)], refs[len(faces) :]
        (layers, beyond, near_rows, other_rows), refs = refs[:4], refs[4:]
        outs, (turned, low, high) = refs[: len(sides)], refs[len(sides) :]
        for side in range(2):
            face = ins[0].at[side] if joined else ins[side]

            def store(by, i, f, rows, first=0 if side else HALO):
                layers[f, first + i, pl.ds(by * EDGE, EDGE), :] = rows

            lay_out(swap_boxes([face[bz] for bz in range(BRICK_Z)]), turned, store)
        lane = lax.broadcasted_iota(jnp.int32, (EDGE, LANES), 1)
        for bx in range(BRICK_X):
            for by in range(BRICK_Y):
                for half in range(TILES // 2):
                    group, n = divmod((bx * BRICK_Y + by) * 2 + half, 4)
                    before, after = by_parity(me_ref[2] != 0, near[group], other[group])
                    columns = [
                        jnp.where(
                            lane < LANES // 2,
                            pltpu.roll(after, (LANES - EDGE * r - HALO * n) % LANES, 1),
                            pltpu.roll(before, (2 * LANES - HALO - EDGE * r - HALO * n) % LANES, 1),
                        )
                        for r in range(16)
                    ]

                    def store(t, i, f, rows, x=bx * EDGE + half * 4, by=by):
                        beyond[f, x + t * 2 + i, pl.ds(by * EDGE, EDGE), :] = rows

                    lay_out(columns, turned, store)
        for f in range(FIELDS):
            for x in range(NEAR_X):
                cells = layers.at[f, 2 if x else 1] if x % (NX + 1) == 0 else grid.at[f, x - 1]
                low[pl.ds(row_of(f, x), HALO), :] = cells[pl.ds(0, HALO), :]
                high[pl.ds(row_of(f, x), HALO), :] = cells[pl.ds(NY - HALO, HALO), :]
        pair = lane // 2
        for first, out in ((0, low), (NY - EDGE, high)):
            edge = jnp.zeros((EDGE, LANES), jnp.float32)
            for f in range(FIELDS):
                for x in range(NX):
                    place = f * NX + x
                    moved = pltpu.roll(beyond[f, x, pl.ds(first, EDGE), :], 2 * place + 1, 1)
                    edge = jnp.where(pair == place, moved, edge)
            out[pl.ds(ROWS, EDGE), :] = edge
        near_rows[...], other_rows[...] = by_parity(me_ref[1] != 0, low[...], high[...])
        pair = lax.broadcasted_iota(jnp.int32, (NY, LANES), 1) // 2
        edges = [jnp.zeros((NY, LANES), jnp.float32)] * 2
        for side in range(2):
            for f in range(FIELDS):
                moved = pltpu.roll(beyond[f, side * (NX - 1)], 2 * side_place(side, f) + 1, 1)
                edges[side] = jnp.where(pair == side_place(side, f), moved, edges[side])
        if joined:
            outs[0][...] = jnp.where(pair < FIELDS, edges[0], edges[1])
        else:
            for out, edge in zip(outs, edges):
                out[...] = edge

    rows = jax.ShapeDtypeStruct((EDGES, LANES), jnp.float32)
    return pl.pallas_call(
        kernel,
        out_shape=[
            jax.ShapeDtypeStruct((FIELDS, 2 * HALO, NY, LANES), jnp.float32),
            jax.ShapeDtypeStruct((FIELDS, NX, NY, LANES), jnp.float32),
            rows,
            rows,
        ]
        + sides,
        in_specs=[SMEM] + [VMEM] * (3 + len(faces)),
        out_specs=[VMEM] * (4 + len(sides)),
        scratch_shapes=[pltpu.VMEM((LANES, LANES), jnp.float32)]
        + [pltpu.VMEM((EDGES, LANES), jnp.float32)] * 2,
        compiler_params=ROOM,
        name="faces_and_rows",
    )(me, grid, *ends, *faces)


def half_conductance(v):
    return 0.5 * (v * jnp.sqrt(v))


def step(cells, rates):
    return [v + (TIME_STEP * c) * r for v, c, r in zip(cells, DIFFUSION, rates)]


def rates(cells, s, beside):
    means = [s + n for _, n in beside]
    sums = []
    for f, v in enumerate(cells):
        terms = [m * (fields[f] - v) for m, (fields, _) in zip(means, beside)]
        sums.append(sum(terms[1:], terms[0]))
    return sums


def each(function, cells, *others):
    fields, s = cells
    columns = zip(fields, *[other[0] for other in others])
    return [function(*c) for c in columns], function(s, *[other[1] for other in others])


def z_beside(cells, across):
    lane = lax.broadcasted_iota(jnp.int32, cells[1].shape, 1)

    def after(v, other):
        return pltpu.roll(jnp.where(lane == 0, other, v), LANES - 1, 1)

    def before(v, other):
        return pltpu.roll(jnp.where(lane == LANES - 1, other, v), 1, 1)

    return [each(after, cells, across), each(before, cells, across)]


def y_beside(cells):
    row = lax.broadcasted_iota(jnp.int32, (NY, LANES), 0)

    def after(v):
        return jnp.where(row == NY - 1, v, pltpu.roll(v, NY - 1, 0))

    def before(v):
        return jnp.where(row == 0, v, pltpu.roll(v, 1, 0))

    return [each(after, cells), each(before, cells)]


def first_inside(grid, layers, beyond):
    def kernel(grid, layers, beyond, wide, halves, first, first_beyond, halves_beyond):
        for f in range(FIELDS):
            for x in range(HALO):
                wide[f, x] = layers[f, x]
                wide[f, HALO + NX + x] = layers[f, HALO + x]
        for x in range(HALO):
            halves[x] = half_conductance(layers[0, x])
            halves[HALO + NX + x] = half_conductance(layers[0, HALO + x])

        def prepare(x, carry):
            for f in range(FIELDS):
                wide[f, x + HALO] = grid[f, x]
            halves[x + HALO] = half_conductance(grid[0, x])
            halves_beyond[x] = half_conductance(beyond[0, x])
            return carry

        lax.fori_loop(0, NX, prepare, 0, unroll=4)

        def at(ref, s, x):
            return [ref[f, x] for f in range(FIELDS)], s[x]

        def inside(x, carry):
            here, over = at(wide, halves, x + HALO), at(beyond, halves_beyond, x)
            beside = [at(wide, halves, x + HALO - 1), at(wide, halves, x + HALO + 1)]
            beside += y_beside(here) + z_beside(here, over)
            for f, v in enumerate(step(here[0], rates(*here, beside))):
                first[f, x] = v
            left, right = jnp.maximum(x - 1, 0), jnp.minimum(x + 1, NX - 1)
            beside = [at(beyond, halves_beyond, left), at(beyond, halves_beyond, right)]
            beside += y_beside(over) + z_beside(over, here)
            for f, v in enumerate(step(over[0], rates(*over, beside))):
                first_beyond[f, x] = v
            return carry

        lax.fori_loop(0, NX, inside, 0, unroll=2)

    def shape(*sizes):
        return jax.ShapeDtypeStruct(sizes + (NY, LANES), jnp.float32)

    return pl.pallas_call(
        kernel,
        out_shape=[
            shape(FIELDS, WIDE_X),
            shape(WIDE_X),
            shape(FIELDS, NX),
            shape(FIELDS, NX),
            shape(NX),
        ],
        in_specs=[VMEM] * 3,
        out_specs=[VMEM] * 5,
        compiler_params=ROOM,
        cost_estimate=pl.CostEstimate(flops=2**22, bytes_accessed=2**21, transcendentals=0),
        name="first_inside",
    )(grid, layers, beyond)


def last_sections(me, wide, halves, first, first_beyond, beyond, halves_beyond, near, other, sides):
    def kernel(
        me_ref, wide, halves, first_in, beyond_in, beyond, halves_beyond, near_rows, other_rows, *refs
    ):
        ins, (out, *refs) = refs[: len(sides)], refs[len(sides) :]
        edges, first, first_beyond, around, fs, fbs, above, below = refs
        below[...], above[...] = by_parity(me_ref[1] != 0, near_rows[...], other_rows[...])
        factors = [TIME_STEP * c for c in DIFFUSION]
        row = lax.broadcasted_iota(jnp.int32, (EDGE, LANES), 0)

        def side_edge(side):
            packed = ins[0 if len(ins) == 1 else side][...]
            fields = [
                pltpu.roll(packed, LANES - 1 - 2 * side_place(side, f), 1) for f in range(FIELDS)
            ]
            return fields, half_conductance(fields[0])

        edge = jnp.where(
            row < EDGE // 2,
            pltpu.roll(below[pl.ds(ROWS, EDGE), :], 1, 0),
            pltpu.roll(above[pl.ds(ROWS, EDGE), :], EDGE - 1, 0),
        )
        for f in range(FIELDS):
            for x in range(NX):
                edges[pl.ds((f * NX + x) * EDGE, EDGE), :] = pltpu.roll(
                    edge, LANES - 1 - 2 * (f * NX + x), 1
                )

        def at(ref, s, x):
            return [ref[f, x] for f in range(FIELDS)], s[x]

        for side, x in ((1, 0), (0, NX + 1)):
            here = at(wide, halves, x + 1)
            beside = [at(wide, halves, x), at(wide, halves, x + 2)]
            beside += y_beside(here) + z_beside(here, side_edge(side))
            for f, v in enumerate(step(here[0], rates(*here, beside))):
                first[pl.ds((f * NEAR_X + x) * NY, NY), :] = v
        for f in range(FIELDS):
            for x in range(NX):
                first[pl.ds((f * NEAR_X + x + 1) * NY, NY), :] = first_in[f, x]

        wide_rows = wide.reshape(FIELDS * WIDE_X * NY, LANES)
        half_rows = halves.reshape(WIDE_X * NY, LANES)

        def sent(ref, depth, f, x, count):
            return ref[pl.ds(row_of(f, x) + depth, count, stride=HALO), :]

        for ref, depth, y, tile_row in ((below, 1, 0, 7), (above, 0, NY - 1, 0)):
            for x, count in ((0, 8), (8, 8), (16, 2)):
                s = half_rows[pl.ds((x + 1) * NY + y, count, stride=NY), :]
                mean = s + half_conductance(sent(ref, depth, 0, x, count))
                for f in range(FIELDS):
                    v = wide_rows[pl.ds((f * WIDE_X + x + 1) * NY + y, count, stride=NY), :]
                    rows = pl.ds((f * NEAR_X + x) * NY + y, count, stride=NY)
                    more = mean * (sent(ref, depth, f, x, count) - v)
                    first[rows, :] = first[rows, :] + factors[f] * more
            for x in (0, 8):

                def line(depth, shift):
                    fields = [sent(ref, depth, f, x + 1 + shift, 8) for f in range(FIELDS)]
                    return fields, half_conductance(fields[0])

                here = line(depth, 0)
                inner = (
                    [
                        wide_rows[pl.ds((f * WIDE_X + x + HALO) * NY + y, 8, stride=NY), :]
                        for f in range(FIELDS)
                    ],
                    half_rows[pl.ds((x + HALO) * NY + y, 8, stride=NY), :],
                )
                over = [
                    edges[pl.ds((f * NX + x) * EDGE + 7 - tile_row, 8, stride=EDGE), :]
                    for f in range(FIELDS)
                ]
                beside = [line(1 - depth, 0), inner, line(depth, -1), line(depth, 1)]
                beside += z_beside(here, (over, half_conductance(over[0])))
                for f, v in enumerate(step(here[0], rates(*here, beside))):
                    around[pl.ds((f * NX + x) * EDGE + tile_row, 8, stride=EDGE), :] = v

        for x in range(NX):
            s = halves_beyond[x]
            near = half_conductance(edges[pl.ds(x * EDGE, EDGE), :])
            for f in range(FIELDS):
                tile = edges[pl.ds((f * NX + x) * EDGE, EDGE), :]
                v, fresh = beyond[f, x], beyond_in[f, x]
                more = [
                    jnp.where(row == at_row, (near + s[n * EDGE :][:EDGE]) * (tile - v[n * EDGE :][:EDGE]), 0.0)
                    for n, at_row in enumerate((0, EDGE - 1))
                ]
                first_beyond[f, x] = fresh + factors[f] * jnp.concatenate(more, 0)
        for side, x in ((1, 0), (0, NX - 1)):
            fields, s = side_edge(side)
            for f in range(FIELDS):
                more = (s + halves_beyond[x]) * (fields[f] - beyond[f, x])
                first_beyond[f, x] = first_beyond[f, x] + factors[f] * more

        def near(x):
            return [
                first[pl.ds(pl.multiple_of((f * NEAR_X + x) * NY, NY), NY), :] for f in range(FIELDS)
            ]

        def conductances(x, carry):
            fs[x] = half_conductance(near(x)[0])
            return carry

        lax.fori_loop(0, NEAR_X, conductances, 0, unroll=6)

        def conductances_beyond(x, carry):
            fbs[x] = half_conductance(first_beyond[0, x])
            return carry

        lax.fori_loop(0, NX, conductances_beyond, 0, unroll=4)

        def second(x, carry):
            here = near(x + 1), fs[x + 1]
            tiles = [
                around[pl.ds(pl.multiple_of((f * NX + x) * EDGE, EDGE), EDGE), :]
                for f in range(FIELDS)
            ]
            ring_of = each(
                lambda v, tile: jnp.concatenate([v, tile], 0), here, (tiles, half_conductance(tiles[0]))
            )
            beside = [(near(x), fs[x]), (near(x + 2), fs[x + 2])]
            beside += [
                each(lambda v: pltpu.roll(v, WIDE_Y - 1, 0)[:NY], ring_of),
                each(lambda v: pltpu.roll(v, 1, 0)[:NY], ring_of),
            ]
            beside += z_beside(here, at(first_beyond, fbs, x))
            for f, v in enumerate(step(here[0], rates(*here, beside))):
                out[f, x] = 0.5 * wide[f, x + HALO] + 0.5 * v
            return carry

        lax.fori_loop(0, NX, second, 0, unroll=4)

    def scratch(*shape):
        return pltpu.VMEM(shape + (LANES,), jnp.float32)

    return pl.pallas_call(
        kernel,
        out_shape=jax.ShapeDtypeStruct((FIELDS, NX, NY, LANES), jnp.float32),
        in_specs=[SMEM] + [VMEM] * (8 + len(sides)),
        out_specs=VMEM,
        scratch_shapes=[
            scratch(FIELDS * NX * EDGE),
            scratch(FIELDS * NEAR_X * NY),
            scratch(FIELDS, NX, NY),
            scratch(FIELDS * NX * EDGE),
            scratch(NEAR_X, NY),
            scratch(NX, NY),
            scratch(EDGES),
            scratch(EDGES),
        ],
        compiler_params=ROOM,
        name="last_sections",
    )(me, wide, halves, first, first_beyond, beyond, halves_beyond, near, other, *sides)


def body(old_fields, new_owner, old_owner):
    across, along = lax.axis_size("gx"), lax.axis_size("gz")
    group_size = across * along
    box_count = new_owner.shape[0]
    capacity = 2 * (box_count // group_size)
    split = group_size <= 8
    joined = across == 2
    place = lax.axis_index("gx") * along + lax.axis_index("gz")
    me = jnp.stack([place, lax.axis_index("gy") & 1, lax.axis_index("gz") & 1])
    departing = pack_boxes(old_fields, new_owner, me, group_size, capacity, split)
    table = position_table(old_owner, group_size, capacity)
    if split:
        arrived = [departing[0]] + [
            lax.ppermute(departing[k], ("gx", "gz"), [(i, i ^ k) for i in range(group_size)])
            for k in range(1, group_size)
        ]
    else:
        arrived = [
            lax.all_to_all(departing[0], ("gx", "gz"), split_axis=0, concat_axis=0, tiled=True)
        ]
    held, near, other, *faces = boxes_in_place(
        arrived, table, me, box_count, capacity, split, joined
    )

    def along_x(sides):
        if joined:
            return [lax.ppermute(sides[0], "gx", ring(across, 1))]
        return [lax.ppermute(side, "gx", ring(across, step)) for side, step in zip(sides, (-1, 1))]

    faces = along_x(faces)
    ends = with_both_sides("gz", near, other)
    grid = grid_from_boxes(held)
    layers, beyond, near, other, *sides = faces_and_rows(grid, faces, me, ends, joined)
    near, other = with_both_sides("gy", near, other)
    sides = along_x(sides)
    wide, halves, first, first_beyond, halves_beyond = first_inside(grid, layers, beyond)
    return last_sections(
        me, wide, halves, first, first_beyond, beyond, halves_beyond, near, other, sides
    )


def solution(mesh):
    return jax.shard_map(
        body,
        mesh=mesh,
        in_specs=(P(("gx", "gy", "gz"), None, None), P(("gx", "gy", "gz")), P(("gx", "gy", "gz"))),
        out_specs=P(None, "gx", "gy", "gz"),
        check_vma=False,
    )
```

```python
import jax
import jax.numpy as jnp
from jax import lax
from jax.experimental import pallas as pl
from jax.experimental.pallas import tpu as pltpu
from jax.sharding import PartitionSpec as P

EDGE = 8
FIELDS = 4
BRICK_X = 2
BRICK_Y = 2
BRICK_Z = 16
CELLS = EDGE**3
LANES = 128
TILES = CELLS // LANES
BOX = (TILES // 2, 2 * FIELDS, LANES)


DIFFUSION = (1.0, 3.3, 0.9, 1.2)
TIME_STEP = 0.012

VMEM = pl.BlockSpec(memory_space=pltpu.VMEM)
SMEM = pl.BlockSpec(memory_space=pltpu.SMEM)
ROOM = pltpu.CompilerParams(vmem_limit_bytes=16 * 2**20)


def rank_table(owner, table, counts, group, capacity, boxes, empty):
    def clear(i, carry):
        table[i] = empty
        return carry

    lax.fori_loop(0, group * capacity, clear, 0, unroll=16)
    for g in range(group):
        counts[g] = g * capacity

    def place(b, carry):
        o = owner[b]
        slot = counts[o]
        table[slot] = b
        counts[o] = slot + 1
        return carry

    lax.fori_loop(0, boxes, place, 0, unroll=8)


def pack_boxes(old_fields, new_owner, me, group, capacity, split):
    boxes = new_owner.shape[0]
    pieces = group if split else 1
    rows = group * capacity // pieces

    def kernel(me_ref, owner, fields, *refs):
        outs, (table, counts) = refs[:pieces], refs[pieces:]
        rank_table(owner, table, counts, group, capacity, boxes, 0)
        for k, out in enumerate(outs):
            base = (me_ref[0] ^ k) * capacity if split else 0

            def copy(r, carry, out=out, base=base):
                box = table[base + r]
                for t in range(TILES):
                    out[r, t // 2, pl.ds(t % 2 * FIELDS, FIELDS), :] = fields[
                        box, :, pl.ds(t * LANES, LANES)
                    ]
                return carry

            lax.fori_loop(0, rows, copy, 0, unroll=8)

    return pl.pallas_call(
        kernel,
        out_shape=[jax.ShapeDtypeStruct((rows,) + BOX, jnp.float32)] * pieces,
        in_specs=[SMEM, SMEM, VMEM],
        out_specs=[VMEM] * pieces,
        scratch_shapes=[
            pltpu.SMEM((group * capacity,), jnp.int32),
            pltpu.SMEM((group,), jnp.int32),
        ],
        compiler_params=ROOM,
        name="pack_boxes",
    )(me, new_owner, old_fields)


def position_table(old_owner, group, capacity):
    boxes = old_owner.shape[0]

    def kernel(owner, table, counts):
        rank_table(owner, table, counts, group, capacity, boxes, boxes)

    return pl.pallas_call(
        kernel,
        out_shape=jax.ShapeDtypeStruct((group * capacity,), jnp.int32),
        in_specs=[SMEM],
        out_specs=SMEM,
        scratch_shapes=[pltpu.SMEM((group,), jnp.int32)],
        compiler_params=ROOM,
        cost_estimate=pl.CostEstimate(flops=0, bytes_accessed=2**22, transcendentals=0),
        name="position_table",
    )(old_owner)


def swap_boxes(columns):
    lane = lax.broadcasted_iota(jnp.int32, columns[0].shape, 1)
    for bit in range(4):
        width = EDGE << bit
        upper = (lane & width) != 0
        fresh = list(columns)
        for low in range(16):
            if low >> bit & 1:
                continue
            high = low | 1 << bit
            a, b = columns[low], columns[high]
            fresh[low] = jnp.where(upper, pltpu.roll(b, width, 1), a)
            fresh[high] = jnp.where(upper, b, pltpu.roll(a, LANES - width, 1))
        columns = fresh
    return columns


def ring(count, step):
    return [(i, (i + step) % count) for i in range(count)]


def pairs(count, first):
    return [((i + first) % count, ((i ^ 1) + first) % count) for i in range(count)]


def boxes_in_place(arrived, table, me, boxes, capacity, split, joined):
    pieces = len(arrived)
    rows = table.shape[0] // pieces
    half = boxes // BRICK_X
    face = (BRICK_Z, BRICK_Y * FIELDS, LANES)
    faces = [jax.ShapeDtypeStruct((2,) + face if joined else face, jnp.float32)] * (2 - joined)
    end = jax.ShapeDtypeStruct((2, 2 * FIELDS, LANES), jnp.float32)

    def kernel(me_ref, table, *refs):
        ins, refs = refs[:pieces], refs[pieces:]
        held, odd_pairs, even_pairs, *outs = refs
        odd = me_ref[1] != 0
        for k, rows_in in enumerate(ins):
            base = (me_ref[0] ^ k) * capacity if split else 0

            def scatter(r, carry, rows_in=rows_in, base=base):
                held[table[base + r]] = rows_in[r]
                return carry

            lax.fori_loop(0, rows, scatter, 0, unroll=8)
        for side in range(2):
            out = outs[0].at[side] if joined else outs[side]
            for by in range(BRICK_Y):
                for bz in range(BRICK_Z):
                    p = side * half + by * BRICK_Z + bz
                    out[bz, pl.ds(by * FIELDS, FIELDS), :] = held[
                        p, side, pl.ds(side * FIELDS, FIELDS), :
                    ]
        pair = lax.broadcasted_iota(jnp.int32, (2 * FIELDS, LANES), 1) % EDGE // HALO
        for group in range(2):
            ends = []
            for bz, first in ((0, 0), (BRICK_Z - 1, EDGE - HALO)):
                packed = jnp.zeros((2 * FIELDS, LANES), jnp.float32)
                for n in range(4):
                    b, part = divmod(group * 4 + n, 2)
                    cells = held[b * BRICK_Z + bz, part]
                    shift = (n * HALO - first) % LANES
                    packed = jnp.where(pair == n, pltpu.roll(cells, shift, 1) if shift else cells, packed)
                ends.append(packed)
            odd_pairs[group] = jnp.where(odd, ends[1], ends[0])
            even_pairs[group] = jnp.where(odd, ends[0], ends[1])

    return pl.pallas_call(
        kernel,
        out_shape=[jax.ShapeDtypeStruct((boxes + 1,) + BOX, jnp.float32), end, end] + faces,
        in_specs=[SMEM, SMEM] + [VMEM] * pieces,
        out_specs=[VMEM] * (3 + len(faces)),
        compiler_params=ROOM,
        name="boxes_in_place",
    )(me, table, *arrived)


HALO = 2
NX = BRICK_X * EDGE
NY = BRICK_Y * EDGE
WIDE_X = NX + 2 * HALO
WIDE_Y = NY + EDGE
NEAR_X = NX + 2


def lay_out(columns, turned, store):
    for r in range(16):
        turned[pl.ds(r * 8, 8), :] = columns[r]
    for a in range(2):
        for i in range(2):
            for f in range(FIELDS):
                store(a, i, f, turned[pl.ds(i * 64 + a * FIELDS + f, 8, stride=8), :])


def grid_from_boxes(held):
    def kernel(held, grid, turned):
        for bx in range(BRICK_X):
            for by in range(BRICK_Y):
                first = (bx * BRICK_Y + by) * BRICK_Z
                for half in range(TILES // 2):

                    def store(t, i, f, rows, x=bx * EDGE + half * 4, by=by):
                        grid[f, x + t * 2 + i, pl.ds(by * EDGE, EDGE), :] = rows

                    columns = swap_boxes([held[first + bz, half] for bz in range(BRICK_Z)])
                    lay_out(columns, turned, store)

    return pl.pallas_call(
        kernel,
        out_shape=jax.ShapeDtypeStruct((FIELDS, NX, NY, LANES), jnp.float32),
        in_specs=[VMEM],
        out_specs=VMEM,
        scratch_shapes=[pltpu.VMEM((LANES, LANES), jnp.float32)],
        cost_estimate=pl.CostEstimate(flops=2**22, bytes_accessed=2**21, transcendentals=0),
        compiler_params=ROOM,
        name="grid_from_boxes",
    )(held)


ROWS = FIELDS * NEAR_X * HALO
EDGES = ROWS + EDGE


def row_of(f, x):
    return (f * NEAR_X + x) * HALO


def side_place(side, f):
    return side * FIELDS + f


def faces_and_rows(grid, faces, me, odd_pairs, even_pairs, joined):
    sides = [jax.ShapeDtypeStruct((NY, LANES), jnp.float32)] * (2 - joined)

    def kernel(me_ref, grid, odd_pairs, even_pairs, *refs):
        ins, refs = refs[: len(faces)], refs[len(faces) :]
        (layers, beyond, low, high), refs = refs[:4], refs[4:]
        outs, (turned, ends) = refs[: len(sides)], refs[len(sides) :]
        ends[me_ref[1]] = even_pairs[...]
        ends[1 - me_ref[1]] = odd_pairs[...]
        for side in range(2):
            face = ins[0].at[side] if joined else ins[side]

            def store(by, i, f, rows, first=0 if side else HALO):
                layers[f, first + i, pl.ds(by * EDGE, EDGE), :] = rows

            lay_out(swap_boxes([face[bz] for bz in range(BRICK_Z)]), turned, store)
        lane = lax.broadcasted_iota(jnp.int32, (EDGE, LANES), 1)
        for bx in range(BRICK_X):
            for by in range(BRICK_Y):
                for half in range(TILES // 2):
                    group, n = divmod((bx * BRICK_Y + by) * 2 + half, 4)
                    after, before = ends[0, group], ends[1, group]
                    columns = [
                        jnp.where(
                            lane < LANES // 2,
                            pltpu.roll(after, (LANES - EDGE * r - HALO * n) % LANES, 1),
                            pltpu.roll(before, (2 * LANES - HALO - EDGE * r - HALO * n) % LANES, 1),
                        )
                        for r in range(16)
                    ]

                    def store(t, i, f, rows, x=bx * EDGE + half * 4, by=by):
                        beyond[f, x + t * 2 + i, pl.ds(by * EDGE, EDGE), :] = rows

                    lay_out(columns, turned, store)
        for f in range(FIELDS):
            for x in range(NEAR_X):
                cells = layers.at[f, 2 if x else 1] if x % (NX + 1) == 0 else grid.at[f, x - 1]
                low[pl.ds(row_of(f, x), HALO), :] = cells[pl.ds(0, HALO), :]
                high[pl.ds(row_of(f, x), HALO), :] = cells[pl.ds(NY - HALO, HALO), :]
        pair = lane // 2
        for first, out in ((0, low), (NY - EDGE, high)):
            edge = jnp.zeros((EDGE, LANES), jnp.float32)
            for f in range(FIELDS):
                for x in range(NX):
                    place = f * NX + x
                    moved = pltpu.roll(beyond[f, x, pl.ds(first, EDGE), :], 2 * place + 1, 1)
                    edge = jnp.where(pair == place, moved, edge)
            out[pl.ds(ROWS, EDGE), :] = edge
        pair = lax.broadcasted_iota(jnp.int32, (NY, LANES), 1) // 2
        edges = [jnp.zeros((NY, LANES), jnp.float32)] * 2
        for side in range(2):
            for f in range(FIELDS):
                moved = pltpu.roll(beyond[f, side * (NX - 1)], 2 * side_place(side, f) + 1, 1)
                edges[side] = jnp.where(pair == side_place(side, f), moved, edges[side])
        if joined:
            outs[0][...] = jnp.where(pair < FIELDS, edges[0], edges[1])
        else:
            for out, edge in zip(outs, edges):
                out[...] = edge

    rows = jax.ShapeDtypeStruct((EDGES, LANES), jnp.float32)
    return pl.pallas_call(
        kernel,
        out_shape=[
            jax.ShapeDtypeStruct((FIELDS, 2 * HALO, NY, LANES), jnp.float32),
            jax.ShapeDtypeStruct((FIELDS, NX, NY, LANES), jnp.float32),
            rows,
            rows,
        ]
        + sides,
        in_specs=[SMEM] + [VMEM] * (3 + len(faces)),
        out_specs=[VMEM] * (4 + len(sides)),
        scratch_shapes=[
            pltpu.VMEM((LANES, LANES), jnp.float32),
            pltpu.VMEM((2, 2, 2 * FIELDS, LANES), jnp.float32),
        ],
        compiler_params=ROOM,
        name="faces_and_rows",
    )(me, grid, odd_pairs, even_pairs, *faces)


def half_conductance(v):
    return 0.5 * (v * jnp.sqrt(v))


def step(cells, rates):
    return [v + (TIME_STEP * c) * r for v, c, r in zip(cells, DIFFUSION, rates)]


def rates(cells, s, beside):
    means = [s + n for _, n in beside]
    sums = []
    for f, v in enumerate(cells):
        terms = [m * (fields[f] - v) for m, (fields, _) in zip(means, beside)]
        sums.append(sum(terms[1:], terms[0]))
    return sums


def each(function, cells, *others):
    fields, s = cells
    columns = zip(fields, *[other[0] for other in others])
    return [function(*c) for c in columns], function(s, *[other[1] for other in others])


def z_beside(cells, across):
    lane = lax.broadcasted_iota(jnp.int32, cells[1].shape, 1)

    def after(v, other):
        return pltpu.roll(jnp.where(lane == 0, other, v), LANES - 1, 1)

    def before(v, other):
        return pltpu.roll(jnp.where(lane == LANES - 1, other, v), 1, 1)

    return [each(after, cells, across), each(before, cells, across)]


def y_beside(cells):
    row = lax.broadcasted_iota(jnp.int32, (NY, LANES), 0)

    def after(v):
        return jnp.where(row == NY - 1, v, pltpu.roll(v, NY - 1, 0))

    def before(v):
        return jnp.where(row == 0, v, pltpu.roll(v, 1, 0))

    return [each(after, cells), each(before, cells)]


def first_inside(grid, layers, beyond):
    def kernel(grid, layers, beyond, wide, halves, first, first_beyond, halves_beyond):
        for f in range(FIELDS):
            for x in range(HALO):
                wide[f, x] = layers[f, x]
                wide[f, HALO + NX + x] = layers[f, HALO + x]
        for x in range(HALO):
            halves[x] = half_conductance(layers[0, x])
            halves[HALO + NX + x] = half_conductance(layers[0, HALO + x])

        def prepare(x, carry):
            for f in range(FIELDS):
                wide[f, x + HALO] = grid[f, x]
            halves[x + HALO] = half_conductance(grid[0, x])
            halves_beyond[x] = half_conductance(beyond[0, x])
            return carry

        lax.fori_loop(0, NX, prepare, 0, unroll=4)

        def at(ref, s, x):
            return [ref[f, x] for f in range(FIELDS)], s[x]

        def inside(x, carry):
            here, over = at(wide, halves, x + HALO), at(beyond, halves_beyond, x)
            beside = [at(wide, halves, x + HALO - 1), at(wide, halves, x + HALO + 1)]
            beside += y_beside(here) + z_beside(here, over)
            for f, v in enumerate(step(here[0], rates(*here, beside))):
                first[f, x] = v
            left, right = jnp.maximum(x - 1, 0), jnp.minimum(x + 1, NX - 1)
            beside = [at(beyond, halves_beyond, left), at(beyond, halves_beyond, right)]
            beside += y_beside(over) + z_beside(over, here)
            for f, v in enumerate(step(over[0], rates(*over, beside))):
                first_beyond[f, x] = v
            return carry

        lax.fori_loop(0, NX, inside, 0, unroll=2)

    def shape(*sizes):
        return jax.ShapeDtypeStruct(sizes + (NY, LANES), jnp.float32)

    return pl.pallas_call(
        kernel,
        out_shape=[
            shape(FIELDS, WIDE_X),
            shape(WIDE_X),
            shape(FIELDS, NX),
            shape(FIELDS, NX),
            shape(NX),
        ],
        in_specs=[VMEM] * 3,
        out_specs=[VMEM] * 5,
        compiler_params=ROOM,
        cost_estimate=pl.CostEstimate(flops=2**22, bytes_accessed=2**21, transcendentals=0),
        name="first_inside",
    )(grid, layers, beyond)


def last_sections(wide, halves, first, first_beyond, beyond, halves_beyond, above, below, sides):
    def kernel(wide, halves, first_in, beyond_in, beyond, halves_beyond, above, below, *refs):
        ins, (out, edges, first, first_beyond, around, fs, fbs) = refs[: len(sides)], refs[len(sides) :]
        factors = [TIME_STEP * c for c in DIFFUSION]
        row = lax.broadcasted_iota(jnp.int32, (EDGE, LANES), 0)

        def side_edge(side):
            packed = ins[0 if len(ins) == 1 else side][...]
            fields = [
                pltpu.roll(packed, LANES - 1 - 2 * side_place(side, f), 1) for f in range(FIELDS)
            ]
            return fields, half_conductance(fields[0])

        edge = jnp.where(
            row < EDGE // 2,
            pltpu.roll(below[pl.ds(ROWS, EDGE), :], 1, 0),
            pltpu.roll(above[pl.ds(ROWS, EDGE), :], EDGE - 1, 0),
        )
        for f in range(FIELDS):
            for x in range(NX):
                edges[pl.ds((f * NX + x) * EDGE, EDGE), :] = pltpu.roll(
                    edge, LANES - 1 - 2 * (f * NX + x), 1
                )

        def at(ref, s, x):
            return [ref[f, x] for f in range(FIELDS)], s[x]

        for side, x in ((1, 0), (0, NX + 1)):
            here = at(wide, halves, x + 1)
            beside = [at(wide, halves, x), at(wide, halves, x + 2)]
            beside += y_beside(here) + z_beside(here, side_edge(side))
            for f, v in enumerate(step(here[0], rates(*here, beside))):
                first[pl.ds((f * NEAR_X + x) * NY, NY), :] = v
        for f in range(FIELDS):
            for x in range(NX):
                first[pl.ds((f * NEAR_X + x + 1) * NY, NY), :] = first_in[f, x]

        wide_rows = wide.reshape(FIELDS * WIDE_X * NY, LANES)
        half_rows = halves.reshape(WIDE_X * NY, LANES)

        def sent(ref, depth, f, x, count):
            return ref[pl.ds(row_of(f, x) + depth, count, stride=HALO), :]

        for ref, depth, y, tile_row in ((below, 1, 0, 7), (above, 0, NY - 1, 0)):
            for x, count in ((0, 8), (8, 8), (16, 2)):
                s = half_rows[pl.ds((x + 1) * NY + y, count, stride=NY), :]
                mean = s + half_conductance(sent(ref, depth, 0, x, count))
                for f in range(FIELDS):
                    v = wide_rows[pl.ds((f * WIDE_X + x + 1) * NY + y, count, stride=NY), :]
                    rows = pl.ds((f * NEAR_X + x) * NY + y, count, stride=NY)
                    more = mean * (sent(ref, depth, f, x, count) - v)
                    first[rows, :] = first[rows, :] + factors[f] * more
            for x in (0, 8):

                def line(depth, shift):
                    fields = [sent(ref, depth, f, x + 1 + shift, 8) for f in range(FIELDS)]
                    return fields, half_conductance(fields[0])

                here = line(depth, 0)
                inner = (
                    [
                        wide_rows[pl.ds((f * WIDE_X + x + HALO) * NY + y, 8, stride=NY), :]
                        for f in range(FIELDS)
                    ],
                    half_rows[pl.ds((x + HALO) * NY + y, 8, stride=NY), :],
                )
                over = [
                    edges[pl.ds((f * NX + x) * EDGE + 7 - tile_row, 8, stride=EDGE), :]
                    for f in range(FIELDS)
                ]
                beside = [line(1 - depth, 0), inner, line(depth, -1), line(depth, 1)]
                beside += z_beside(here, (over, half_conductance(over[0])))
                for f, v in enumerate(step(here[0], rates(*here, beside))):
                    around[pl.ds((f * NX + x) * EDGE + tile_row, 8, stride=EDGE), :] = v

        for x in range(NX):
            s = halves_beyond[x]
            near = half_conductance(edges[pl.ds(x * EDGE, EDGE), :])
            for f in range(FIELDS):
                tile = edges[pl.ds((f * NX + x) * EDGE, EDGE), :]
                v, fresh = beyond[f, x], beyond_in[f, x]
                more = [
                    jnp.where(row == at_row, (near + s[n * EDGE :][:EDGE]) * (tile - v[n * EDGE :][:EDGE]), 0.0)
                    for n, at_row in enumerate((0, EDGE - 1))
                ]
                first_beyond[f, x] = fresh + factors[f] * jnp.concatenate(more, 0)
        for side, x in ((1, 0), (0, NX - 1)):
            fields, s = side_edge(side)
            for f in range(FIELDS):
                more = (s + halves_beyond[x]) * (fields[f] - beyond[f, x])
                first_beyond[f, x] = first_beyond[f, x] + factors[f] * more

        def near(x):
            return [
                first[pl.ds(pl.multiple_of((f * NEAR_X + x) * NY, NY), NY), :] for f in range(FIELDS)
            ]

        def conductances(x, carry):
            fs[x] = half_conductance(near(x)[0])
            return carry

        lax.fori_loop(0, NEAR_X, conductances, 0, unroll=6)

        def conductances_beyond(x, carry):
            fbs[x] = half_conductance(first_beyond[0, x])
            return carry

        lax.fori_loop(0, NX, conductances_beyond, 0, unroll=4)

        def second(x, carry):
            here = near(x + 1), fs[x + 1]
            tiles = [
                around[pl.ds(pl.multiple_of((f * NX + x) * EDGE, EDGE), EDGE), :]
                for f in range(FIELDS)
            ]
            ring_of = each(
                lambda v, tile: jnp.concatenate([v, tile], 0), here, (tiles, half_conductance(tiles[0]))
            )
            beside = [(near(x), fs[x]), (near(x + 2), fs[x + 2])]
            beside += [
                each(lambda v: pltpu.roll(v, WIDE_Y - 1, 0)[:NY], ring_of),
                each(lambda v: pltpu.roll(v, 1, 0)[:NY], ring_of),
            ]
            beside += z_beside(here, at(first_beyond, fbs, x))
            for f, v in enumerate(step(here[0], rates(*here, beside))):
                out[f, x] = 0.5 * wide[f, x + HALO] + 0.5 * v
            return carry

        lax.fori_loop(0, NX, second, 0, unroll=4)

    def scratch(*shape):
        return pltpu.VMEM(shape + (LANES,), jnp.float32)

    return pl.pallas_call(
        kernel,
        out_shape=jax.ShapeDtypeStruct((FIELDS, NX, NY, LANES), jnp.float32),
        in_specs=[VMEM] * (8 + len(sides)),
        out_specs=VMEM,
        scratch_shapes=[
            scratch(FIELDS * NX * EDGE),
            scratch(FIELDS * NEAR_X * NY),
            scratch(FIELDS, NX, NY),
            scratch(FIELDS * NX * EDGE),
            scratch(NEAR_X, NY),
            scratch(NX, NY),
        ],
        compiler_params=ROOM,
        name="last_sections",
    )(wide, halves, first, first_beyond, beyond, halves_beyond, above, below, *sides)


def body(old_fields, new_owner, old_owner):
    across, along = lax.axis_size("gx"), lax.axis_size("gz")
    group_size = across * along
    box_count = new_owner.shape[0]
    capacity = 2 * (box_count // group_size)
    split = group_size <= 8
    joined = across == 2
    place = lax.axis_index("gx") * along + lax.axis_index("gz")
    me = jnp.stack([place, lax.axis_index("gz") & 1])
    departing = pack_boxes(old_fields, new_owner, me, group_size, capacity, split)
    table = position_table(old_owner, group_size, capacity)
    if split:
        arrived = [departing[0]] + [
            lax.ppermute(departing[k], ("gx", "gz"), [(i, i ^ k) for i in range(group_size)])
            for k in range(1, group_size)
        ]
    else:
        arrived = [
            lax.all_to_all(departing[0], ("gx", "gz"), split_axis=0, concat_axis=0, tiled=True)
        ]
    held, odd_pairs, even_pairs, *faces = boxes_in_place(
        arrived, table, me, box_count, capacity, split, joined
    )

    def along_x(sides):
        if joined:
            return [lax.ppermute(sides[0], "gx", ring(across, 1))]
        return [lax.ppermute(side, "gx", ring(across, step)) for side, step in zip(sides, (-1, 1))]

    faces = along_x(faces)
    odd_pairs = lax.ppermute(odd_pairs, "gz", pairs(along, 1))
    even_pairs = lax.ppermute(even_pairs, "gz", pairs(along, 0))
    grid = grid_from_boxes(held)
    layers, beyond, low, high, *sides = faces_and_rows(
        grid, faces, me, odd_pairs, even_pairs, joined
    )
    rows = lax.axis_size("gy")
    above = lax.ppermute(low, "gy", ring(rows, -1))
    below = lax.ppermute(high, "gy", ring(rows, 1))
    sides = along_x(sides)
    wide, halves, first, first_beyond, halves_beyond = first_inside(grid, layers, beyond)
    return last_sections(
        wide, halves, first, first_beyond, beyond, halves_beyond, above, below, sides
    )


def solution(mesh):
    return jax.shard_map(
        body,
        mesh=mesh,
        in_specs=(P(("gx", "gy", "gz"), None, None), P(("gx", "gy", "gz")), P(("gx", "gy", "gz"))),
        out_specs=P(None, "gx", "gy", "gz"),
        check_vma=False,
    )
```

```python
import jax
import jax.numpy as jnp
from jax import lax
from jax.experimental import pallas as pl
from jax.experimental.pallas import tpu as pltpu
from jax.sharding import PartitionSpec as P

EDGE = 8
FIELDS = 4
BRICK_X = 2
BRICK_Y = 2
BRICK_Z = 16
CELLS = EDGE**3
LANES = 128
TILES = CELLS // LANES
BOX = (TILES // 2, 2 * FIELDS, LANES)


DIFFUSION = (1.0, 3.3, 0.9, 1.2)
TIME_STEP = 0.012

VMEM = pl.BlockSpec(memory_space=pltpu.VMEM)
SMEM = pl.BlockSpec(memory_space=pltpu.SMEM)
HBM = pl.BlockSpec(memory_space=pltpu.HBM)
ROOM = pltpu.CompilerParams(vmem_limit_bytes=16 * 2**20)


def in_hbm(array):
    return pltpu.with_memory_space_constraint(array, pltpu.HBM)


def group_place():
    return lax.axis_index("gx") * lax.axis_size("gz") + lax.axis_index("gz")


def rank_table(owner, table, counts, group, capacity, boxes, empty):
    def clear(i, carry):
        table[i] = empty
        return carry

    lax.fori_loop(0, group * capacity, clear, 0, unroll=16)
    for g in range(group):
        counts[g] = g * capacity

    def place(b, carry):
        o = owner[b]
        slot = counts[o]
        table[slot] = b
        counts[o] = slot + 1
        return carry

    lax.fori_loop(0, boxes, place, 0, unroll=8)


def pack_boxes(old_fields, new_owner, group, capacity, split):
    boxes = new_owner.shape[0]
    pieces = group if split else 1
    rows = group * capacity // pieces

    def kernel(owner_hbm, fields_hbm, *refs):
        outs, (owner, fields, table, counts, sems) = refs[:pieces], refs[pieces:]
        fetch_owner = pltpu.make_async_copy(owner_hbm, owner, sems.at[0])
        fetch_fields = pltpu.make_async_copy(fields_hbm, fields, sems.at[1])
        fetch_owner.start()
        fetch_fields.start()
        fetch_owner.wait()
        rank_table(owner, table, counts, group, capacity, boxes, 0)
        fetch_fields.wait()
        for k, out in enumerate(outs):
            base = (group_place() ^ k) * capacity if split else 0

            def copy(r, carry, out=out, base=base):
                box = table[base + r]
                for t in range(TILES):
                    out[r, t // 2, pl.ds(t % 2 * FIELDS, FIELDS), :] = fields[
                        box, :, pl.ds(t * LANES, LANES)
                    ]
                return carry

            lax.fori_loop(0, rows, copy, 0, unroll=8)

    return pl.pallas_call(
        kernel,
        out_shape=[jax.ShapeDtypeStruct((rows,) + BOX, jnp.float32)] * pieces,
        in_specs=[HBM, HBM],
        out_specs=[VMEM] * pieces,
        scratch_shapes=[
            pltpu.SMEM((boxes,), jnp.int32),
            pltpu.VMEM(old_fields.shape, jnp.float32),
            pltpu.SMEM((group * capacity,), jnp.int32),
            pltpu.SMEM((group,), jnp.int32),
            pltpu.SemaphoreType.DMA((2,)),
        ],
        compiler_params=ROOM,
        name="pack_boxes",
    )(in_hbm(new_owner), in_hbm(old_fields))


def position_table(old_owner, group, capacity):
    boxes = old_owner.shape[0]

    def kernel(owner, table, counts):
        rank_table(owner, table, counts, group, capacity, boxes, boxes)

    return pl.pallas_call(
        kernel,
        out_shape=pltpu.SMEM((group * capacity,), jnp.int32),
        in_specs=[SMEM],
        out_specs=SMEM,
        scratch_shapes=[pltpu.SMEM((group,), jnp.int32)],
        compiler_params=ROOM,
        cost_estimate=pl.CostEstimate(flops=0, bytes_accessed=2**22, transcendentals=0),
        name="position_table",
    )(old_owner)


def swap_boxes(columns):
    lane = lax.broadcasted_iota(jnp.int32, columns[0].shape, 1)
    for bit in range(4):
        width = EDGE << bit
        upper = (lane & width) != 0
        fresh = list(columns)
        for low in range(16):
            if low >> bit & 1:
                continue
            high = low | 1 << bit
            a, b = columns[low], columns[high]
            fresh[low] = jnp.where(upper, pltpu.roll(b, width, 1), a)
            fresh[high] = jnp.where(upper, b, pltpu.roll(a, LANES - width, 1))
        columns = fresh
    return columns


def ring(count, step):
    return [(i, (i + step) % count) for i in range(count)]


def pairs(count, first):
    return [((i + first) % count, ((i ^ 1) + first) % count) for i in range(count)]


def boxes_in_place(arrived, table, boxes, capacity, split, joined):
    pieces = len(arrived)
    rows = table.shape[0] // pieces
    half = boxes // BRICK_X
    face = (BRICK_Z, BRICK_Y * FIELDS, LANES)
    faces = [jax.ShapeDtypeStruct((2,) + face if joined else face, jnp.float32)] * (2 - joined)
    end = jax.ShapeDtypeStruct((2, 2 * FIELDS, LANES), jnp.float32)

    def kernel(table, *refs):
        ins, refs = refs[:pieces], refs[pieces:]
        held, odd_pairs, even_pairs, *outs = refs
        odd = lax.axis_index("gz") & 1 != 0
        for k, rows_in in enumerate(ins):
            base = (group_place() ^ k) * capacity if split else 0

            def scatter(r, carry, rows_in=rows_in, base=base):
                held[table[base + r]] = rows_in[r]
                return carry

            lax.fori_loop(0, rows, scatter, 0, unroll=8)
        for side in range(2):
            out = outs[0].at[side] if joined else outs[side]
            for by in range(BRICK_Y):
                for bz in range(BRICK_Z):
                    p = side * half + by * BRICK_Z + bz
                    out[bz, pl.ds(by * FIELDS, FIELDS), :] = held[
                        p, side, pl.ds(side * FIELDS, FIELDS), :
                    ]
        pair = lax.broadcasted_iota(jnp.int32, (2 * FIELDS, LANES), 1) % EDGE // HALO
        for group in range(2):
            ends = []
            for bz, first in ((0, 0), (BRICK_Z - 1, EDGE - HALO)):
                packed = jnp.zeros((2 * FIELDS, LANES), jnp.float32)
                for n in range(4):
                    b, part = divmod(group * 4 + n, 2)
                    cells = held[b * BRICK_Z + bz, part]
                    shift = (n * HALO - first) % LANES
                    packed = jnp.where(pair == n, pltpu.roll(cells, shift, 1) if shift else cells, packed)
                ends.append(packed)
            odd_pairs[group] = jnp.where(odd, ends[1], ends[0])
            even_pairs[group] = jnp.where(odd, ends[0], ends[1])

    return pl.pallas_call(
        kernel,
        out_shape=[jax.ShapeDtypeStruct((boxes + 1,) + BOX, jnp.float32), end, end] + faces,
        in_specs=[SMEM] + [VMEM] * pieces,
        out_specs=[VMEM] * (3 + len(faces)),
        compiler_params=ROOM,
        name="boxes_in_place",
    )(pltpu.with_memory_space_constraint(table, pltpu.SMEM), *arrived)


HALO = 2
NX = BRICK_X * EDGE
NY = BRICK_Y * EDGE
WIDE_X = NX + 2 * HALO
WIDE_Y = NY + EDGE
NEAR_X = NX + 2


def lay_out(columns, turned, store):
    for r in range(16):
        turned[pl.ds(r * 8, 8), :] = columns[r]
    for a in range(2):
        for i in range(2):
            for f in range(FIELDS):
                store(a, i, f, turned[pl.ds(i * 64 + a * FIELDS + f, 8, stride=8), :])


def grid_from_boxes(held):
    def kernel(held, grid, turned):
        for bx in range(BRICK_X):
            for by in range(BRICK_Y):
                first = (bx * BRICK_Y + by) * BRICK_Z
                for half in range(TILES // 2):

                    def store(t, i, f, rows, x=bx * EDGE + half * 4, by=by):
                        grid[f, x + t * 2 + i, pl.ds(by * EDGE, EDGE), :] = rows

                    columns = swap_boxes([held[first + bz, half] for bz in range(BRICK_Z)])
                    lay_out(columns, turned, store)

    return pl.pallas_call(
        kernel,
        out_shape=jax.ShapeDtypeStruct((FIELDS, NX, NY, LANES), jnp.float32),
        in_specs=[VMEM],
        out_specs=VMEM,
        scratch_shapes=[pltpu.VMEM((LANES, LANES), jnp.float32)],
        cost_estimate=pl.CostEstimate(flops=2**22, bytes_accessed=2**21, transcendentals=0),
        compiler_params=ROOM,
        name="grid_from_boxes",
    )(held)


ROWS = FIELDS * NEAR_X * HALO
EDGES = ROWS + EDGE


def row_of(f, x):
    return (f * NEAR_X + x) * HALO


def side_place(side, f):
    return side * FIELDS + f


def faces_and_rows(grid, faces, odd_pairs, even_pairs, joined):
    sides = [jax.ShapeDtypeStruct((NY, LANES), jnp.float32)] * (2 - joined)

    def kernel(grid, odd_pairs, even_pairs, *refs):
        ins, refs = refs[: len(faces)], refs[len(faces) :]
        (layers, beyond, low, high), refs = refs[:4], refs[4:]
        outs, (turned, ends) = refs[: len(sides)], refs[len(sides) :]
        odd = lax.axis_index("gz") & 1
        ends[odd] = even_pairs[...]
        ends[1 - odd] = odd_pairs[...]
        for side in range(2):
            face = ins[0].at[side] if joined else ins[side]

            def store(by, i, f, rows, first=0 if side else HALO):
                layers[f, first + i, pl.ds(by * EDGE, EDGE), :] = rows

            lay_out(swap_boxes([face[bz] for bz in range(BRICK_Z)]), turned, store)
        lane = lax.broadcasted_iota(jnp.int32, (EDGE, LANES), 1)
        for bx in range(BRICK_X):
            for by in range(BRICK_Y):
                for half in range(TILES // 2):
                    group, n = divmod((bx * BRICK_Y + by) * 2 + half, 4)
                    after, before = ends[0, group], ends[1, group]
                    columns = [
                        jnp.where(
                            lane < LANES // 2,
                            pltpu.roll(after, (LANES - EDGE * r - HALO * n) % LANES, 1),
                            pltpu.roll(before, (2 * LANES - HALO - EDGE * r - HALO * n) % LANES, 1),
                        )
                        for r in range(16)
                    ]

                    def store(t, i, f, rows, x=bx * EDGE + half * 4, by=by):
                        beyond[f, x + t * 2 + i, pl.ds(by * EDGE, EDGE), :] = rows

                    lay_out(columns, turned, store)
        for f in range(FIELDS):
            for x in range(NEAR_X):
                cells = layers.at[f, 2 if x else 1] if x % (NX + 1) == 0 else grid.at[f, x - 1]
                low[pl.ds(row_of(f, x), HALO), :] = cells[pl.ds(0, HALO), :]
                high[pl.ds(row_of(f, x), HALO), :] = cells[pl.ds(NY - HALO, HALO), :]
        pair = lane // 2
        for first, out in ((0, low), (NY - EDGE, high)):
            edge = jnp.zeros((EDGE, LANES), jnp.float32)
            for f in range(FIELDS):
                for x in range(NX):
                    place = f * NX + x
                    moved = pltpu.roll(beyond[f, x, pl.ds(first, EDGE), :], 2 * place + 1, 1)
                    edge = jnp.where(pair == place, moved, edge)
            out[pl.ds(ROWS, EDGE), :] = edge
        pair = lax.broadcasted_iota(jnp.int32, (NY, LANES), 1) // 2
        edges = [jnp.zeros((NY, LANES), jnp.float32)] * 2
        for side in range(2):
            for f in range(FIELDS):
                moved = pltpu.roll(beyond[f, side * (NX - 1)], 2 * side_place(side, f) + 1, 1)
                edges[side] = jnp.where(pair == side_place(side, f), moved, edges[side])
        if joined:
            outs[0][...] = jnp.where(pair < FIELDS, edges[0], edges[1])
        else:
            for out, edge in zip(outs, edges):
                out[...] = edge

    rows = jax.ShapeDtypeStruct((EDGES, LANES), jnp.float32)
    return pl.pallas_call(
        kernel,
        out_shape=[
            jax.ShapeDtypeStruct((FIELDS, 2 * HALO, NY, LANES), jnp.float32),
            jax.ShapeDtypeStruct((FIELDS, NX, NY, LANES), jnp.float32),
            rows,
            rows,
        ]
        + sides,
        in_specs=[VMEM] * (3 + len(faces)),
        out_specs=[VMEM] * (4 + len(sides)),
        scratch_shapes=[
            pltpu.VMEM((LANES, LANES), jnp.float32),
            pltpu.VMEM((2, 2, 2 * FIELDS, LANES), jnp.float32),
        ],
        compiler_params=ROOM,
        name="faces_and_rows",
    )(grid, odd_pairs, even_pairs, *faces)


def half_conductance(v):
    return 0.5 * (v * jnp.sqrt(v))


def step(cells, rates):
    return [v + (TIME_STEP * c) * r for v, c, r in zip(cells, DIFFUSION, rates)]


def rates(cells, s, beside):
    means = [s + n for _, n in beside]
    sums = []
    for f, v in enumerate(cells):
        terms = [m * (fields[f] - v) for m, (fields, _) in zip(means, beside)]
        sums.append(sum(terms[1:], terms[0]))
    return sums


def each(function, cells, *others):
    fields, s = cells
    columns = zip(fields, *[other[0] for other in others])
    return [function(*c) for c in columns], function(s, *[other[1] for other in others])


def z_beside(cells, across):
    lane = lax.broadcasted_iota(jnp.int32, cells[1].shape, 1)

    def after(v, other):
        return pltpu.roll(jnp.where(lane == 0, other, v), LANES - 1, 1)

    def before(v, other):
        return pltpu.roll(jnp.where(lane == LANES - 1, other, v), 1, 1)

    return [each(after, cells, across), each(before, cells, across)]


def y_beside(cells):
    row = lax.broadcasted_iota(jnp.int32, (NY, LANES), 0)

    def after(v):
        return jnp.where(row == NY - 1, v, pltpu.roll(v, NY - 1, 0))

    def before(v):
        return jnp.where(row == 0, v, pltpu.roll(v, 1, 0))

    return [each(after, cells), each(before, cells)]


def first_inside(grid, layers, beyond):
    def kernel(grid, layers, beyond, wide, halves, first, first_beyond, halves_beyond):
        for f in range(FIELDS):
            for x in range(HALO):
                wide[f, x] = layers[f, x]
                wide[f, HALO + NX + x] = layers[f, HALO + x]
        for x in range(HALO):
            halves[x] = half_conductance(layers[0, x])
            halves[HALO + NX + x] = half_conductance(layers[0, HALO + x])

        def prepare(x, carry):
            for f in range(FIELDS):
                wide[f, x + HALO] = grid[f, x]
            halves[x + HALO] = half_conductance(grid[0, x])
            halves_beyond[x] = half_conductance(beyond[0, x])
            return carry

        lax.fori_loop(0, NX, prepare, 0, unroll=4)

        def at(ref, s, x):
            return [ref[f, x] for f in range(FIELDS)], s[x]

        def inside(x, carry):
            here, over = at(wide, halves, x + HALO), at(beyond, halves_beyond, x)
            beside = [at(wide, halves, x + HALO - 1), at(wide, halves, x + HALO + 1)]
            beside += y_beside(here) + z_beside(here, over)
            for f, v in enumerate(step(here[0], rates(*here, beside))):
                first[f, x] = v
            left, right = jnp.maximum(x - 1, 0), jnp.minimum(x + 1, NX - 1)
            beside = [at(beyond, halves_beyond, left), at(beyond, halves_beyond, right)]
            beside += y_beside(over) + z_beside(over, here)
            for f, v in enumerate(step(over[0], rates(*over, beside))):
                first_beyond[f, x] = v
            return carry

        lax.fori_loop(0, NX, inside, 0, unroll=2)

    def shape(*sizes):
        return jax.ShapeDtypeStruct(sizes + (NY, LANES), jnp.float32)

    return pl.pallas_call(
        kernel,
        out_shape=[
            shape(FIELDS, WIDE_X),
            shape(WIDE_X),
            shape(FIELDS, NX),
            shape(FIELDS, NX),
            shape(NX),
        ],
        in_specs=[VMEM] * 3,
        out_specs=[VMEM] * 5,
        compiler_params=ROOM,
        cost_estimate=pl.CostEstimate(flops=2**22, bytes_accessed=2**21, transcendentals=0),
        name="first_inside",
    )(grid, layers, beyond)


def last_sections(wide, halves, first, first_beyond, beyond, halves_beyond, above, below, sides):
    def kernel(wide, halves, first_in, beyond_in, beyond, halves_beyond, above, below, *refs):
        ins, (out, edges, first, first_beyond, around, fs, fbs) = refs[: len(sides)], refs[len(sides) :]
        factors = [TIME_STEP * c for c in DIFFUSION]
        row = lax.broadcasted_iota(jnp.int32, (EDGE, LANES), 0)

        def side_edge(side):
            packed = ins[0 if len(ins) == 1 else side][...]
            fields = [
                pltpu.roll(packed, LANES - 1 - 2 * side_place(side, f), 1) for f in range(FIELDS)
            ]
            return fields, half_conductance(fields[0])

        edge = jnp.where(
            row < EDGE // 2,
            pltpu.roll(below[pl.ds(ROWS, EDGE), :], 1, 0),
            pltpu.roll(above[pl.ds(ROWS, EDGE), :], EDGE - 1, 0),
        )
        for f in range(FIELDS):
            for x in range(NX):
                edges[pl.ds((f * NX + x) * EDGE, EDGE), :] = pltpu.roll(
                    edge, LANES - 1 - 2 * (f * NX + x), 1
                )

        def at(ref, s, x):
            return [ref[f, x] for f in range(FIELDS)], s[x]

        for side, x in ((1, 0), (0, NX + 1)):
            here = at(wide, halves, x + 1)
            beside = [at(wide, halves, x), at(wide, halves, x + 2)]
            beside += y_beside(here) + z_beside(here, side_edge(side))
            for f, v in enumerate(step(here[0], rates(*here, beside))):
                first[pl.ds((f * NEAR_X + x) * NY, NY), :] = v
        for f in range(FIELDS):
            for x in range(NX):
                first[pl.ds((f * NEAR_X + x + 1) * NY, NY), :] = first_in[f, x]

        wide_rows = wide.reshape(FIELDS * WIDE_X * NY, LANES)
        half_rows = halves.reshape(WIDE_X * NY, LANES)

        def sent(ref, depth, f, x, count):
            return ref[pl.ds(row_of(f, x) + depth, count, stride=HALO), :]

        for ref, depth, y, tile_row in ((below, 1, 0, 7), (above, 0, NY - 1, 0)):
            for x, count in ((0, 8), (8, 8), (16, 2)):
                s = half_rows[pl.ds((x + 1) * NY + y, count, stride=NY), :]
                mean = s + half_conductance(sent(ref, depth, 0, x, count))
                for f in range(FIELDS):
                    v = wide_rows[pl.ds((f * WIDE_X + x + 1) * NY + y, count, stride=NY), :]
                    rows = pl.ds((f * NEAR_X + x) * NY + y, count, stride=NY)
                    more = mean * (sent(ref, depth, f, x, count) - v)
                    first[rows, :] = first[rows, :] + factors[f] * more
            for x in (0, 8):

                def line(depth, shift):
                    fields = [sent(ref, depth, f, x + 1 + shift, 8) for f in range(FIELDS)]
                    return fields, half_conductance(fields[0])

                here = line(depth, 0)
                inner = (
                    [
                        wide_rows[pl.ds((f * WIDE_X + x + HALO) * NY + y, 8, stride=NY), :]
                        for f in range(FIELDS)
                    ],
                    half_rows[pl.ds((x + HALO) * NY + y, 8, stride=NY), :],
                )
                over = [
                    edges[pl.ds((f * NX + x) * EDGE + 7 - tile_row, 8, stride=EDGE), :]
                    for f in range(FIELDS)
                ]
                beside = [line(1 - depth, 0), inner, line(depth, -1), line(depth, 1)]
                beside += z_beside(here, (over, half_conductance(over[0])))
                for f, v in enumerate(step(here[0], rates(*here, beside))):
                    around[pl.ds((f * NX + x) * EDGE + tile_row, 8, stride=EDGE), :] = v

        for x in range(NX):
            s = halves_beyond[x]
            near = half_conductance(edges[pl.ds(x * EDGE, EDGE), :])
            for f in range(FIELDS):
                tile = edges[pl.ds((f * NX + x) * EDGE, EDGE), :]
                v, fresh = beyond[f, x], beyond_in[f, x]
                more = [
                    jnp.where(row == at_row, (near + s[n * EDGE :][:EDGE]) * (tile - v[n * EDGE :][:EDGE]), 0.0)
                    for n, at_row in enumerate((0, EDGE - 1))
                ]
                first_beyond[f, x] = fresh + factors[f] * jnp.concatenate(more, 0)
        for side, x in ((1, 0), (0, NX - 1)):
            fields, s = side_edge(side)
            for f in range(FIELDS):
                more = (s + halves_beyond[x]) * (fields[f] - beyond[f, x])
                first_beyond[f, x] = first_beyond[f, x] + factors[f] * more

        def near(x):
            return [
                first[pl.ds(pl.multiple_of((f * NEAR_X + x) * NY, NY), NY), :] for f in range(FIELDS)
            ]

        def conductances(x, carry):
            fs[x] = half_conductance(near(x)[0])
            return carry

        lax.fori_loop(0, NEAR_X, conductances, 0, unroll=6)

        def conductances_beyond(x, carry):
            fbs[x] = half_conductance(first_beyond[0, x])
            return carry

        lax.fori_loop(0, NX, conductances_beyond, 0, unroll=4)

        def second(x, carry):
            here = near(x + 1), fs[x + 1]
            tiles = [
                around[pl.ds(pl.multiple_of((f * NX + x) * EDGE, EDGE), EDGE), :]
                for f in range(FIELDS)
            ]
            ring_of = each(
                lambda v, tile: jnp.concatenate([v, tile], 0), here, (tiles, half_conductance(tiles[0]))
            )
            beside = [(near(x), fs[x]), (near(x + 2), fs[x + 2])]
            beside += [
                each(lambda v: pltpu.roll(v, WIDE_Y - 1, 0)[:NY], ring_of),
                each(lambda v: pltpu.roll(v, 1, 0)[:NY], ring_of),
            ]
            beside += z_beside(here, at(first_beyond, fbs, x))
            for f, v in enumerate(step(here[0], rates(*here, beside))):
                out[f, x] = 0.5 * wide[f, x + HALO] + 0.5 * v
            return carry

        lax.fori_loop(0, NX, second, 0, unroll=4)

    def scratch(*shape):
        return pltpu.VMEM(shape + (LANES,), jnp.float32)

    return pl.pallas_call(
        kernel,
        out_shape=jax.ShapeDtypeStruct((FIELDS, NX, NY, LANES), jnp.float32),
        in_specs=[VMEM] * (8 + len(sides)),
        out_specs=VMEM,
        scratch_shapes=[
            scratch(FIELDS * NX * EDGE),
            scratch(FIELDS * NEAR_X * NY),
            scratch(FIELDS, NX, NY),
            scratch(FIELDS * NX * EDGE),
            scratch(NEAR_X, NY),
            scratch(NX, NY),
        ],
        compiler_params=ROOM,
        name="last_sections",
    )(wide, halves, first, first_beyond, beyond, halves_beyond, above, below, *sides)


def body(old_fields, new_owner, old_owner):
    across, along = lax.axis_size("gx"), lax.axis_size("gz")
    group_size = across * along
    box_count = new_owner.shape[0]
    capacity = 2 * (box_count // group_size)
    split = group_size <= 8
    joined = across == 2
    departing = pack_boxes(old_fields, new_owner, group_size, capacity, split)
    table = position_table(old_owner, group_size, capacity)
    if split:
        arrived = [departing[0]] + [
            lax.ppermute(departing[k], ("gx", "gz"), [(i, i ^ k) for i in range(group_size)])
            for k in range(1, group_size)
        ]
    else:
        arrived = [
            lax.all_to_all(departing[0], ("gx", "gz"), split_axis=0, concat_axis=0, tiled=True)
        ]
    held, odd_pairs, even_pairs, *faces = boxes_in_place(
        arrived, table, box_count, capacity, split, joined
    )

    def along_x(sides):
        if joined:
            return [lax.ppermute(sides[0], "gx", ring(across, 1))]
        return [lax.ppermute(side, "gx", ring(across, step)) for side, step in zip(sides, (-1, 1))]

    faces = along_x(faces)
    odd_pairs = lax.ppermute(odd_pairs, "gz", pairs(along, 1))
    even_pairs = lax.ppermute(even_pairs, "gz", pairs(along, 0))
    grid = grid_from_boxes(held)
    layers, beyond, low, high, *sides = faces_and_rows(
        grid, faces, odd_pairs, even_pairs, joined
    )
    rows = lax.axis_size("gy")
    above = lax.ppermute(low, "gy", ring(rows, -1))
    below = lax.ppermute(high, "gy", ring(rows, 1))
    sides = along_x(sides)
    wide, halves, first, first_beyond, halves_beyond = first_inside(grid, layers, beyond)
    return last_sections(
        wide, halves, first, first_beyond, beyond, halves_beyond, above, below, sides
    )


def solution(mesh):
    return jax.shard_map(
        body,
        mesh=mesh,
        in_specs=(P(("gx", "gy", "gz"), None, None), P(("gx", "gy", "gz")), P(("gx", "gy", "gz"))),
        out_specs=P(None, "gx", "gy", "gz"),
        check_vma=False,
    )
```

```python
import jax
import jax.numpy as jnp
from jax import lax
from jax.experimental import pallas as pl
from jax.experimental.pallas import tpu as pltpu
from jax.sharding import PartitionSpec as P

EDGE = 8
FIELDS = 4
BRICK_X = 2
BRICK_Y = 2
BRICK_Z = 16
CELLS = EDGE**3
LANES = 128
TILES = CELLS // LANES
BOX = (TILES // 2, 2 * FIELDS, LANES)


DIFFUSION = (1.0, 3.3, 0.9, 1.2)
TIME_STEP = 0.012

VMEM = pl.BlockSpec(memory_space=pltpu.VMEM)
SMEM = pl.BlockSpec(memory_space=pltpu.SMEM)
HBM = pl.BlockSpec(memory_space=pltpu.HBM)
ROOM = pltpu.CompilerParams(vmem_limit_bytes=16 * 2**20)


def in_hbm(array):
    return pltpu.with_memory_space_constraint(array, pltpu.HBM)


def group_place():
    return lax.axis_index("gx") * lax.axis_size("gz") + lax.axis_index("gz")


def rank_table(owner, table, counts, group, capacity, boxes, empty):
    def clear(i, carry):
        table[i] = empty
        return carry

    lax.fori_loop(0, group * capacity, clear, 0, unroll=16)
    for g in range(group):
        counts[g] = g * capacity

    def place(b, carry):
        o = owner[b]
        slot = counts[o]
        table[slot] = b
        counts[o] = slot + 1
        return carry

    lax.fori_loop(0, boxes, place, 0, unroll=8)


def pack_boxes(old_fields, new_owner, group, capacity, split):
    boxes = new_owner.shape[0]
    pieces = group if split else 1
    rows = group * capacity // pieces

    def kernel(owner_hbm, fields_hbm, *refs):
        outs, (owner, fields, table, counts, sems) = refs[:pieces], refs[pieces:]
        fetch_owner = pltpu.make_async_copy(owner_hbm, owner, sems.at[0])
        fetch_fields = pltpu.make_async_copy(fields_hbm, fields, sems.at[1])
        fetch_owner.start()
        fetch_fields.start()
        fetch_owner.wait()
        rank_table(owner, table, counts, group, capacity, boxes, 0)
        fetch_fields.wait()
        for k, out in enumerate(outs):
            base = (group_place() ^ k) * capacity if split else 0

            def copy(r, carry, out=out, base=base):
                box = table[base + r]
                for t in range(TILES):
                    out[r, t // 2, pl.ds(t % 2 * FIELDS, FIELDS), :] = fields[
                        box, :, pl.ds(t * LANES, LANES)
                    ]
                return carry

            lax.fori_loop(0, rows, copy, 0, unroll=8)

    return pl.pallas_call(
        kernel,
        out_shape=[jax.ShapeDtypeStruct((rows,) + BOX, jnp.float32)] * pieces,
        in_specs=[HBM, HBM],
        out_specs=[VMEM] * pieces,
        scratch_shapes=[
            pltpu.SMEM((boxes,), jnp.int32),
            pltpu.VMEM(old_fields.shape, jnp.float32),
            pltpu.SMEM((group * capacity,), jnp.int32),
            pltpu.SMEM((group,), jnp.int32),
            pltpu.SemaphoreType.DMA((2,)),
        ],
        compiler_params=ROOM,
        name="pack_boxes",
    )(in_hbm(new_owner), in_hbm(old_fields))


def position_table(old_owner, group, capacity):
    boxes = old_owner.shape[0]

    def kernel(owner, table, counts):
        rank_table(owner, table, counts, group, capacity, boxes, boxes)

    return pl.pallas_call(
        kernel,
        out_shape=pltpu.SMEM((group * capacity,), jnp.int32),
        in_specs=[SMEM],
        out_specs=SMEM,
        scratch_shapes=[pltpu.SMEM((group,), jnp.int32)],
        compiler_params=ROOM,
        cost_estimate=pl.CostEstimate(flops=0, bytes_accessed=2**22, transcendentals=0),
        name="position_table",
    )(old_owner)


def swap_boxes(columns):
    lane = lax.broadcasted_iota(jnp.int32, columns[0].shape, 1)
    for bit in range(4):
        width = EDGE << bit
        upper = (lane & width) != 0
        fresh = list(columns)
        for low in range(16):
            if low >> bit & 1:
                continue
            high = low | 1 << bit
            a, b = columns[low], columns[high]
            fresh[low] = jnp.where(upper, pltpu.roll(b, width, 1), a)
            fresh[high] = jnp.where(upper, b, pltpu.roll(a, LANES - width, 1))
        columns = fresh
    return columns


def ring(count, step):
    return [(i, (i + step) % count) for i in range(count)]


def pairs(count, first):
    return [((i + first) % count, ((i ^ 1) + first) % count) for i in range(count)]


def boxes_in_place(arrived, order, table, boxes, capacity, split, joined):
    pieces = len(arrived)
    rows = table.shape[0] // pieces
    half = boxes // BRICK_X
    face = (BRICK_Z, BRICK_Y * FIELDS, LANES)
    faces = [jax.ShapeDtypeStruct((2,) + face if joined else face, jnp.float32)] * (2 - joined)
    end = jax.ShapeDtypeStruct((2, 2 * FIELDS, LANES), jnp.float32)

    def kernel(table, *refs):
        ins, refs = refs[:pieces], refs[pieces:]
        held, odd_pairs, even_pairs, *outs = refs
        odd = lax.axis_index("gz") & 1 != 0
        for k, rows_in in zip(order, ins):
            base = (group_place() ^ k) * capacity if split else 0

            def scatter(r, carry, rows_in=rows_in, base=base):
                held[table[base + r]] = rows_in[r]
                return carry

            lax.fori_loop(0, rows, scatter, 0, unroll=8)
        for side in range(2):
            out = outs[0].at[side] if joined else outs[side]
            for by in range(BRICK_Y):
                for bz in range(BRICK_Z):
                    p = side * half + by * BRICK_Z + bz
                    out[bz, pl.ds(by * FIELDS, FIELDS), :] = held[
                        p, side, pl.ds(side * FIELDS, FIELDS), :
                    ]
        pair = lax.broadcasted_iota(jnp.int32, (2 * FIELDS, LANES), 1) % EDGE // HALO
        for group in range(2):
            ends = []
            for bz, first in ((0, 0), (BRICK_Z - 1, EDGE - HALO)):
                packed = jnp.zeros((2 * FIELDS, LANES), jnp.float32)
                for n in range(4):
                    b, part = divmod(group * 4 + n, 2)
                    cells = held[b * BRICK_Z + bz, part]
                    shift = (n * HALO - first) % LANES
                    packed = jnp.where(pair == n, pltpu.roll(cells, shift, 1) if shift else cells, packed)
                ends.append(packed)
            odd_pairs[group] = jnp.where(odd, ends[1], ends[0])
            even_pairs[group] = jnp.where(odd, ends[0], ends[1])

    return pl.pallas_call(
        kernel,
        out_shape=[jax.ShapeDtypeStruct((boxes + 1,) + BOX, jnp.float32), end, end] + faces,
        in_specs=[SMEM] + [VMEM] * pieces,
        out_specs=[VMEM] * (3 + len(faces)),
        compiler_params=ROOM,
        name="boxes_in_place",
    )(pltpu.with_memory_space_constraint(table, pltpu.SMEM), *arrived)


HALO = 2
NX = BRICK_X * EDGE
NY = BRICK_Y * EDGE
WIDE_X = NX + 2 * HALO
WIDE_Y = NY + EDGE
NEAR_X = NX + 2


def lay_out(columns, turned, store):
    for r in range(16):
        turned[pl.ds(r * 8, 8), :] = columns[r]
    for a in range(2):
        for i in range(2):
            for f in range(FIELDS):
                store(a, i, f, turned[pl.ds(i * 64 + a * FIELDS + f, 8, stride=8), :])


def grid_from_boxes(held):
    def kernel(held, grid, turned):
        for bx in range(BRICK_X):
            for by in range(BRICK_Y):
                first = (bx * BRICK_Y + by) * BRICK_Z
                for half in range(TILES // 2):

                    def store(t, i, f, rows, x=bx * EDGE + half * 4, by=by):
                        grid[f, x + t * 2 + i, pl.ds(by * EDGE, EDGE), :] = rows

                    columns = swap_boxes([held[first + bz, half] for bz in range(BRICK_Z)])
                    lay_out(columns, turned, store)

    return pl.pallas_call(
        kernel,
        out_shape=jax.ShapeDtypeStruct((FIELDS, NX, NY, LANES), jnp.float32),
        in_specs=[VMEM],
        out_specs=VMEM,
        scratch_shapes=[pltpu.VMEM((LANES, LANES), jnp.float32)],
        cost_estimate=pl.CostEstimate(flops=2**22, bytes_accessed=2**21, transcendentals=0),
        compiler_params=ROOM,
        name="grid_from_boxes",
    )(held)


ROWS = FIELDS * NEAR_X * HALO
EDGES = ROWS + EDGE


def row_of(f, x):
    return (f * NEAR_X + x) * HALO


def side_place(side, f):
    return side * FIELDS + f


def faces_and_rows(grid, faces, odd_pairs, even_pairs, joined):
    sides = [jax.ShapeDtypeStruct((NY, LANES), jnp.float32)] * (2 - joined)

    def kernel(grid, odd_pairs, even_pairs, *refs):
        ins, refs = refs[: len(faces)], refs[len(faces) :]
        (layers, beyond, low, high), refs = refs[:4], refs[4:]
        outs, (turned, ends) = refs[: len(sides)], refs[len(sides) :]
        odd = lax.axis_index("gz") & 1
        ends[odd] = even_pairs[...]
        ends[1 - odd] = odd_pairs[...]
        for side in range(2):
            face = ins[0].at[side] if joined else ins[side]

            def store(by, i, f, rows, first=0 if side else HALO):
                layers[f, first + i, pl.ds(by * EDGE, EDGE), :] = rows

            lay_out(swap_boxes([face[bz] for bz in range(BRICK_Z)]), turned, store)
        lane = lax.broadcasted_iota(jnp.int32, (EDGE, LANES), 1)
        for bx in range(BRICK_X):
            for by in range(BRICK_Y):
                for half in range(TILES // 2):
                    group, n = divmod((bx * BRICK_Y + by) * 2 + half, 4)
                    after, before = ends[0, group], ends[1, group]
                    columns = [
                        jnp.where(
                            lane < LANES // 2,
                            pltpu.roll(after, (LANES - EDGE * r - HALO * n) % LANES, 1),
                            pltpu.roll(before, (2 * LANES - HALO - EDGE * r - HALO * n) % LANES, 1),
                        )
                        for r in range(16)
                    ]

                    def store(t, i, f, rows, x=bx * EDGE + half * 4, by=by):
                        beyond[f, x + t * 2 + i, pl.ds(by * EDGE, EDGE), :] = rows

                    lay_out(columns, turned, store)
        for f in range(FIELDS):
            for x in range(NEAR_X):
                cells = layers.at[f, 2 if x else 1] if x % (NX + 1) == 0 else grid.at[f, x - 1]
                low[pl.ds(row_of(f, x), HALO), :] = cells[pl.ds(0, HALO), :]
                high[pl.ds(row_of(f, x), HALO), :] = cells[pl.ds(NY - HALO, HALO), :]
        pair = lane // 2
        for first, out in ((0, low), (NY - EDGE, high)):
            edge = jnp.zeros((EDGE, LANES), jnp.float32)
            for f in range(FIELDS):
                for x in range(NX):
                    place = f * NX + x
                    moved = pltpu.roll(beyond[f, x, pl.ds(first, EDGE), :], 2 * place + 1, 1)
                    edge = jnp.where(pair == place, moved, edge)
            out[pl.ds(ROWS, EDGE), :] = edge
        pair = lax.broadcasted_iota(jnp.int32, (NY, LANES), 1) // 2
        edges = [jnp.zeros((NY, LANES), jnp.float32)] * 2
        for side in range(2):
            for f in range(FIELDS):
                moved = pltpu.roll(beyond[f, side * (NX - 1)], 2 * side_place(side, f) + 1, 1)
                edges[side] = jnp.where(pair == side_place(side, f), moved, edges[side])
        if joined:
            outs[0][...] = jnp.where(pair < FIELDS, edges[0], edges[1])
        else:
            for out, edge in zip(outs, edges):
                out[...] = edge

    rows = jax.ShapeDtypeStruct((EDGES, LANES), jnp.float32)
    return pl.pallas_call(
        kernel,
        out_shape=[
            jax.ShapeDtypeStruct((FIELDS, 2 * HALO, NY, LANES), jnp.float32),
            jax.ShapeDtypeStruct((FIELDS, NX, NY, LANES), jnp.float32),
            rows,
            rows,
        ]
        + sides,
        in_specs=[VMEM] * (3 + len(faces)),
        out_specs=[VMEM] * (4 + len(sides)),
        scratch_shapes=[
            pltpu.VMEM((LANES, LANES), jnp.float32),
            pltpu.VMEM((2, 2, 2 * FIELDS, LANES), jnp.float32),
        ],
        compiler_params=ROOM,
        name="faces_and_rows",
    )(grid, odd_pairs, even_pairs, *faces)


def half_conductance(v):
    return 0.5 * (v * jnp.sqrt(v))


def step(cells, rates):
    return [v + (TIME_STEP * c) * r for v, c, r in zip(cells, DIFFUSION, rates)]


def rates(cells, s, beside):
    means = [s + n for _, n in beside]
    sums = []
    for f, v in enumerate(cells):
        terms = [m * (fields[f] - v) for m, (fields, _) in zip(means, beside)]
        sums.append(sum(terms[1:], terms[0]))
    return sums


def each(function, cells, *others):
    fields, s = cells
    columns = zip(fields, *[other[0] for other in others])
    return [function(*c) for c in columns], function(s, *[other[1] for other in others])


def z_beside(cells, across):
    lane = lax.broadcasted_iota(jnp.int32, cells[1].shape, 1)

    def after(v, other):
        return pltpu.roll(jnp.where(lane == 0, other, v), LANES - 1, 1)

    def before(v, other):
        return pltpu.roll(jnp.where(lane == LANES - 1, other, v), 1, 1)

    return [each(after, cells, across), each(before, cells, across)]


def y_beside(cells):
    row = lax.broadcasted_iota(jnp.int32, (NY, LANES), 0)

    def after(v):
        return jnp.where(row == NY - 1, v, pltpu.roll(v, NY - 1, 0))

    def before(v):
        return jnp.where(row == 0, v, pltpu.roll(v, 1, 0))

    return [each(after, cells), each(before, cells)]


def first_inside(grid, layers, beyond):
    def kernel(grid, layers, beyond, wide, halves, first, first_beyond, halves_beyond):
        for f in range(FIELDS):
            for x in range(HALO):
                wide[f, x] = layers[f, x]
                wide[f, HALO + NX + x] = layers[f, HALO + x]
        for x in range(HALO):
            halves[x] = half_conductance(layers[0, x])
            halves[HALO + NX + x] = half_conductance(layers[0, HALO + x])

        def prepare(x, carry):
            for f in range(FIELDS):
                wide[f, x + HALO] = grid[f, x]
            halves[x + HALO] = half_conductance(grid[0, x])
            halves_beyond[x] = half_conductance(beyond[0, x])
            return carry

        lax.fori_loop(0, NX, prepare, 0, unroll=4)

        def at(ref, s, x):
            return [ref[f, x] for f in range(FIELDS)], s[x]

        def inside(x, carry):
            here, over = at(wide, halves, x + HALO), at(beyond, halves_beyond, x)
            beside = [at(wide, halves, x + HALO - 1), at(wide, halves, x + HALO + 1)]
            beside += y_beside(here) + z_beside(here, over)
            for f, v in enumerate(step(here[0], rates(*here, beside))):
                first[f, x] = v
            left, right = jnp.maximum(x - 1, 0), jnp.minimum(x + 1, NX - 1)
            beside = [at(beyond, halves_beyond, left), at(beyond, halves_beyond, right)]
            beside += y_beside(over) + z_beside(over, here)
            for f, v in enumerate(step(over[0], rates(*over, beside))):
                first_beyond[f, x] = v
            return carry

        lax.fori_loop(0, NX, inside, 0, unroll=2)

    def shape(*sizes):
        return jax.ShapeDtypeStruct(sizes + (NY, LANES), jnp.float32)

    return pl.pallas_call(
        kernel,
        out_shape=[
            shape(FIELDS, WIDE_X),
            shape(WIDE_X),
            shape(FIELDS, NX),
            shape(FIELDS, NX),
            shape(NX),
        ],
        in_specs=[VMEM] * 3,
        out_specs=[VMEM] * 5,
        compiler_params=ROOM,
        cost_estimate=pl.CostEstimate(flops=2**22, bytes_accessed=2**21, transcendentals=0),
        name="first_inside",
    )(grid, layers, beyond)


PARTS = 4


def last_sections(wide, halves, first, first_beyond, beyond, halves_beyond, above, below, sides):
    def kernel(wide, halves, first_in, beyond_in, beyond, halves_beyond, above, below, *refs):
        ins, (out, *refs) = refs[: len(sides)], refs[len(sides) :]
        edges, first, first_beyond, around, fs, fbs, result, sems = refs
        factors = [TIME_STEP * c for c in DIFFUSION]
        row = lax.broadcasted_iota(jnp.int32, (EDGE, LANES), 0)

        def side_edge(side):
            packed = ins[0 if len(ins) == 1 else side][...]
            fields = [
                pltpu.roll(packed, LANES - 1 - 2 * side_place(side, f), 1) for f in range(FIELDS)
            ]
            return fields, half_conductance(fields[0])

        edge = jnp.where(
            row < EDGE // 2,
            pltpu.roll(below[pl.ds(ROWS, EDGE), :], 1, 0),
            pltpu.roll(above[pl.ds(ROWS, EDGE), :], EDGE - 1, 0),
        )
        for f in range(FIELDS):
            for x in range(NX):
                edges[pl.ds((f * NX + x) * EDGE, EDGE), :] = pltpu.roll(
                    edge, LANES - 1 - 2 * (f * NX + x), 1
                )

        def at(ref, s, x):
            return [ref[f, x] for f in range(FIELDS)], s[x]

        for side, x in ((1, 0), (0, NX + 1)):
            here = at(wide, halves, x + 1)
            beside = [at(wide, halves, x), at(wide, halves, x + 2)]
            beside += y_beside(here) + z_beside(here, side_edge(side))
            for f, v in enumerate(step(here[0], rates(*here, beside))):
                first[pl.ds((f * NEAR_X + x) * NY, NY), :] = v
        for f in range(FIELDS):
            for x in range(NX):
                first[pl.ds((f * NEAR_X + x + 1) * NY, NY), :] = first_in[f, x]

        wide_rows = wide.reshape(FIELDS * WIDE_X * NY, LANES)
        half_rows = halves.reshape(WIDE_X * NY, LANES)

        def sent(ref, depth, f, x, count):
            return ref[pl.ds(row_of(f, x) + depth, count, stride=HALO), :]

        for ref, depth, y, tile_row in ((below, 1, 0, 7), (above, 0, NY - 1, 0)):
            for x, count in ((0, 8), (8, 8), (16, 2)):
                s = half_rows[pl.ds((x + 1) * NY + y, count, stride=NY), :]
                mean = s + half_conductance(sent(ref, depth, 0, x, count))
                for f in range(FIELDS):
                    v = wide_rows[pl.ds((f * WIDE_X + x + 1) * NY + y, count, stride=NY), :]
                    rows = pl.ds((f * NEAR_X + x) * NY + y, count, stride=NY)
                    more = mean * (sent(ref, depth, f, x, count) - v)
                    first[rows, :] = first[rows, :] + factors[f] * more
            for x in (0, 8):

                def line(depth, shift):
                    fields = [sent(ref, depth, f, x + 1 + shift, 8) for f in range(FIELDS)]
                    return fields, half_conductance(fields[0])

                here = line(depth, 0)
                inner = (
                    [
                        wide_rows[pl.ds((f * WIDE_X + x + HALO) * NY + y, 8, stride=NY), :]
                        for f in range(FIELDS)
                    ],
                    half_rows[pl.ds((x + HALO) * NY + y, 8, stride=NY), :],
                )
                over = [
                    edges[pl.ds((f * NX + x) * EDGE + 7 - tile_row, 8, stride=EDGE), :]
                    for f in range(FIELDS)
                ]
                beside = [line(1 - depth, 0), inner, line(depth, -1), line(depth, 1)]
                beside += z_beside(here, (over, half_conductance(over[0])))
                for f, v in enumerate(step(here[0], rates(*here, beside))):
                    around[pl.ds((f * NX + x) * EDGE + tile_row, 8, stride=EDGE), :] = v

        for x in range(NX):
            s = halves_beyond[x]
            near = half_conductance(edges[pl.ds(x * EDGE, EDGE), :])
            for f in range(FIELDS):
                tile = edges[pl.ds((f * NX + x) * EDGE, EDGE), :]
                v, fresh = beyond[f, x], beyond_in[f, x]
                more = [
                    jnp.where(row == at_row, (near + s[n * EDGE :][:EDGE]) * (tile - v[n * EDGE :][:EDGE]), 0.0)
                    for n, at_row in enumerate((0, EDGE - 1))
                ]
                first_beyond[f, x] = fresh + factors[f] * jnp.concatenate(more, 0)
        for side, x in ((1, 0), (0, NX - 1)):
            fields, s = side_edge(side)
            for f in range(FIELDS):
                more = (s + halves_beyond[x]) * (fields[f] - beyond[f, x])
                first_beyond[f, x] = first_beyond[f, x] + factors[f] * more

        def near(x):
            return [
                first[pl.ds(pl.multiple_of((f * NEAR_X + x) * NY, NY), NY), :] for f in range(FIELDS)
            ]

        def conductances(x, carry):
            fs[x] = half_conductance(near(x)[0])
            return carry

        lax.fori_loop(0, NEAR_X, conductances, 0, unroll=6)

        def conductances_beyond(x, carry):
            fbs[x] = half_conductance(first_beyond[0, x])
            return carry

        lax.fori_loop(0, NX, conductances_beyond, 0, unroll=4)

        def second(x, carry):
            here = near(x + 1), fs[x + 1]
            tiles = [
                around[pl.ds(pl.multiple_of((f * NX + x) * EDGE, EDGE), EDGE), :]
                for f in range(FIELDS)
            ]
            ring_of = each(
                lambda v, tile: jnp.concatenate([v, tile], 0), here, (tiles, half_conductance(tiles[0]))
            )
            beside = [(near(x), fs[x]), (near(x + 2), fs[x + 2])]
            beside += [
                each(lambda v: pltpu.roll(v, WIDE_Y - 1, 0)[:NY], ring_of),
                each(lambda v: pltpu.roll(v, 1, 0)[:NY], ring_of),
            ]
            beside += z_beside(here, at(first_beyond, fbs, x))
            for f, v in enumerate(step(here[0], rates(*here, beside))):
                result[f, x] = 0.5 * wide[f, x + HALO] + 0.5 * v
            return carry

        copies = []
        for part in range(PARTS):
            start = part * (NX // PARTS)
            lax.fori_loop(start, start + NX // PARTS, second, 0, unroll=NX // PARTS)
            layers = pl.ds(start, NX // PARTS)
            copies.append(
                pltpu.make_async_copy(result.at[:, layers], out.at[:, layers], sems.at[part])
            )
            copies[-1].start()
        for copy in copies:
            copy.wait()

    def scratch(*shape):
        return pltpu.VMEM(shape + (LANES,), jnp.float32)

    return pl.pallas_call(
        kernel,
        out_shape=jax.ShapeDtypeStruct((FIELDS, NX, NY, LANES), jnp.float32),
        in_specs=[VMEM] * (8 + len(sides)),
        out_specs=HBM,
        scratch_shapes=[
            scratch(FIELDS * NX * EDGE),
            scratch(FIELDS * NEAR_X * NY),
            scratch(FIELDS, NX, NY),
            scratch(FIELDS * NX * EDGE),
            scratch(NEAR_X, NY),
            scratch(NX, NY),
            scratch(FIELDS, NX, NY),
            pltpu.SemaphoreType.DMA((PARTS,)),
        ],
        compiler_params=ROOM,
        name="last_sections",
    )(wide, halves, first, first_beyond, beyond, halves_beyond, above, below, *sides)


def body(old_fields, new_owner, old_owner):
    across, along = lax.axis_size("gx"), lax.axis_size("gz")
    group_size = across * along
    box_count = new_owner.shape[0]
    capacity = 2 * (box_count // group_size)
    split = group_size <= 8
    joined = across == 2
    departing = pack_boxes(old_fields, new_owner, group_size, capacity, split)
    table = position_table(old_owner, group_size, capacity)
    if split:
        order = (3, 1, 2, 4, 6, 5, 7, 0)
        arrived = [
            lax.ppermute(departing[k], ("gx", "gz"), [(i, i ^ k) for i in range(group_size)])
            if k
            else departing[k]
            for k in order
        ]
    else:
        order = [0]
        arrived = [
            lax.all_to_all(departing[0], ("gx", "gz"), split_axis=0, concat_axis=0, tiled=True)
        ]
    held, odd_pairs, even_pairs, *faces = boxes_in_place(
        arrived, order, table, box_count, capacity, split, joined
    )

    def along_x(sides):
        if joined:
            return [lax.ppermute(sides[0], "gx", ring(across, 1))]
        return [lax.ppermute(side, "gx", ring(across, step)) for side, step in zip(sides, (-1, 1))]

    faces = along_x(faces)
    odd_pairs = lax.ppermute(odd_pairs, "gz", pairs(along, 1))
    even_pairs = lax.ppermute(even_pairs, "gz", pairs(along, 0))
    grid = grid_from_boxes(held)
    layers, beyond, low, high, *sides = faces_and_rows(
        grid, faces, odd_pairs, even_pairs, joined
    )
    rows = lax.axis_size("gy")
    above = lax.ppermute(low, "gy", ring(rows, -1))
    below = lax.ppermute(high, "gy", ring(rows, 1))
    sides = along_x(sides)
    wide, halves, first, first_beyond, halves_beyond = first_inside(grid, layers, beyond)
    return last_sections(
        wide, halves, first, first_beyond, beyond, halves_beyond, above, below, sides
    )


def solution(mesh):
    return jax.shard_map(
        body,
        mesh=mesh,
        in_specs=(P(("gx", "gy", "gz"), None, None), P(("gx", "gy", "gz")), P(("gx", "gy", "gz"))),
        out_specs=P(None, "gx", "gy", "gz"),
        check_vma=False,
    )
```

```python
import jax
import jax.numpy as jnp
from jax import lax
from jax.experimental import pallas as pl
from jax.experimental.pallas import tpu as pltpu
from jax.sharding import PartitionSpec as P

EDGE = 8
FIELDS = 4
BRICK_X = 2
BRICK_Y = 2
BRICK_Z = 16
CELLS = EDGE**3
LANES = 128
TILES = CELLS // LANES
BOX = (TILES // 2, 2 * FIELDS, LANES)


DIFFUSION = (1.0, 3.3, 0.9, 1.2)
TIME_STEP = 0.012

VMEM = pl.BlockSpec(memory_space=pltpu.VMEM)
SMEM = pl.BlockSpec(memory_space=pltpu.SMEM)
HBM = pl.BlockSpec(memory_space=pltpu.HBM)
ROOM = pltpu.CompilerParams(vmem_limit_bytes=16 * 2**20)


def in_hbm(array):
    return pltpu.with_memory_space_constraint(array, pltpu.HBM)


def group_place():
    return lax.axis_index("gx") * lax.axis_size("gz") + lax.axis_index("gz")


def rank_table(owner, table, counts, group, capacity, boxes, empty):
    def clear(i, carry):
        table[i] = empty
        return carry

    lax.fori_loop(0, group * capacity, clear, 0, unroll=16)
    for g in range(group):
        counts[g] = g * capacity

    def place(b, carry):
        o = owner[b]
        slot = counts[o]
        table[slot] = b
        counts[o] = slot + 1
        return carry

    lax.fori_loop(0, boxes, place, 0, unroll=8)


def pack_boxes(old_fields, new_owner, group, capacity, split):
    boxes = new_owner.shape[0]
    pieces = group if split else 1
    rows = group * capacity // pieces

    def kernel(owner_hbm, fields_hbm, *refs):
        outs, (owner, fields, table, counts, sems) = refs[:pieces], refs[pieces:]
        fetch_owner = pltpu.make_async_copy(owner_hbm, owner, sems.at[0])
        fetch_fields = pltpu.make_async_copy(fields_hbm, fields, sems.at[1])
        fetch_owner.start()
        fetch_fields.start()
        fetch_owner.wait()
        rank_table(owner, table, counts, group, capacity, boxes, 0)
        fetch_fields.wait()
        for k, out in enumerate(outs):
            base = (group_place() ^ k) * capacity if split else 0

            def copy(r, carry, out=out, base=base):
                box = table[base + r]
                for t in range(TILES):
                    out[r, t // 2, pl.ds(t % 2 * FIELDS, FIELDS), :] = fields[
                        box, :, pl.ds(t * LANES, LANES)
                    ]
                return carry

            lax.fori_loop(0, rows, copy, 0, unroll=8)

    return pl.pallas_call(
        kernel,
        out_shape=[jax.ShapeDtypeStruct((rows,) + BOX, jnp.float32)] * pieces,
        in_specs=[HBM, HBM],
        out_specs=[VMEM] * pieces,
        scratch_shapes=[
            pltpu.SMEM((boxes,), jnp.int32),
            pltpu.VMEM(old_fields.shape, jnp.float32),
            pltpu.SMEM((group * capacity,), jnp.int32),
            pltpu.SMEM((group,), jnp.int32),
            pltpu.SemaphoreType.DMA((2,)),
        ],
        compiler_params=ROOM,
        name="pack_boxes",
    )(in_hbm(new_owner), in_hbm(old_fields))


def position_table(old_owner, group, capacity):
    boxes = old_owner.shape[0]

    def kernel(owner, table, counts):
        rank_table(owner, table, counts, group, capacity, boxes, boxes)

    return pl.pallas_call(
        kernel,
        out_shape=pltpu.SMEM((group * capacity,), jnp.int32),
        in_specs=[SMEM],
        out_specs=SMEM,
        scratch_shapes=[pltpu.SMEM((group,), jnp.int32)],
        compiler_params=ROOM,
        cost_estimate=pl.CostEstimate(flops=0, bytes_accessed=2**22, transcendentals=0),
        name="position_table",
    )(old_owner)


def swap_boxes(columns):
    lane = lax.broadcasted_iota(jnp.int32, columns[0].shape, 1)
    for bit in range(4):
        width = EDGE << bit
        upper = (lane & width) != 0
        fresh = list(columns)
        for low in range(16):
            if low >> bit & 1:
                continue
            high = low | 1 << bit
            a, b = columns[low], columns[high]
            fresh[low] = jnp.where(upper, pltpu.roll(b, width, 1), a)
            fresh[high] = jnp.where(upper, b, pltpu.roll(a, LANES - width, 1))
        columns = fresh
    return columns


def ring(count, step):
    return [(i, (i + step) % count) for i in range(count)]


def pairs(count, first):
    return [((i + first) % count, ((i ^ 1) + first) % count) for i in range(count)]


def boxes_in_place(arrived, order, table, boxes, capacity, split, joined):
    pieces = len(arrived)
    rows = table.shape[0] // pieces
    half = boxes // BRICK_X
    face = (BRICK_Z, BRICK_Y * FIELDS, LANES)
    faces = [jax.ShapeDtypeStruct((2,) + face if joined else face, jnp.float32)] * (2 - joined)
    end = jax.ShapeDtypeStruct((2, 2 * FIELDS, LANES), jnp.float32)

    def kernel(table, *refs):
        ins, refs = refs[:pieces], refs[pieces:]
        held, odd_pairs, even_pairs, *outs = refs
        odd = lax.axis_index("gz") & 1 != 0
        for k, rows_in in zip(order, ins):
            base = (group_place() ^ k) * capacity if split else 0

            def scatter(r, carry, rows_in=rows_in, base=base):
                held[table[base + r]] = rows_in[r]
                return carry

            lax.fori_loop(0, rows, scatter, 0, unroll=8)
        for side in range(2):
            out = outs[0].at[side] if joined else outs[side]
            for by in range(BRICK_Y):
                for bz in range(BRICK_Z):
                    p = side * half + by * BRICK_Z + bz
                    out[bz, pl.ds(by * FIELDS, FIELDS), :] = held[
                        p, side, pl.ds(side * FIELDS, FIELDS), :
                    ]
        pair = lax.broadcasted_iota(jnp.int32, (2 * FIELDS, LANES), 1) % EDGE // HALO
        for group in range(2):
            ends = []
            for bz, first in ((0, 0), (BRICK_Z - 1, EDGE - HALO)):
                packed = jnp.zeros((2 * FIELDS, LANES), jnp.float32)
                for n in range(4):
                    b, part = divmod(group * 4 + n, 2)
                    cells = held[b * BRICK_Z + bz, part]
                    shift = (n * HALO - first) % LANES
                    packed = jnp.where(pair == n, pltpu.roll(cells, shift, 1) if shift else cells, packed)
                ends.append(packed)
            odd_pairs[group] = jnp.where(odd, ends[1], ends[0])
            even_pairs[group] = jnp.where(odd, ends[0], ends[1])

    return pl.pallas_call(
        kernel,
        out_shape=[jax.ShapeDtypeStruct((boxes + 1,) + BOX, jnp.float32), end, end] + faces,
        in_specs=[SMEM] + [VMEM] * pieces,
        out_specs=[VMEM] * (3 + len(faces)),
        compiler_params=ROOM,
        name="boxes_in_place",
    )(pltpu.with_memory_space_constraint(table, pltpu.SMEM), *arrived)


HALO = 2
NX = BRICK_X * EDGE
NY = BRICK_Y * EDGE
WIDE_X = NX + 2 * HALO
WIDE_Y = NY + EDGE
NEAR_X = NX + 2


def lay_out(columns, turned, store):
    for r in range(16):
        turned[pl.ds(r * 8, 8), :] = columns[r]
    for a in range(2):
        for i in range(2):
            for f in range(FIELDS):
                store(a, i, f, turned[pl.ds(i * 64 + a * FIELDS + f, 8, stride=8), :])


def grid_from_boxes(held):
    def kernel(held, grid, turned):
        for bx in range(BRICK_X):
            for by in range(BRICK_Y):
                first = (bx * BRICK_Y + by) * BRICK_Z
                for half in range(TILES // 2):

                    def store(t, i, f, rows, x=bx * EDGE + half * 4, by=by):
                        grid[f, x + t * 2 + i, pl.ds(by * EDGE, EDGE), :] = rows

                    columns = swap_boxes([held[first + bz, half] for bz in range(BRICK_Z)])
                    lay_out(columns, turned, store)

    return pl.pallas_call(
        kernel,
        out_shape=jax.ShapeDtypeStruct((FIELDS, NX, NY, LANES), jnp.float32),
        in_specs=[VMEM],
        out_specs=VMEM,
        scratch_shapes=[pltpu.VMEM((LANES, LANES), jnp.float32)],
        cost_estimate=pl.CostEstimate(flops=2**22, bytes_accessed=2**21, transcendentals=0),
        compiler_params=ROOM,
        name="grid_from_boxes",
    )(held)


ROWS = FIELDS * NEAR_X * HALO
EDGES = ROWS + EDGE


def row_of(f, x):
    return (f * NEAR_X + x) * HALO


def beyond_ends(ends, bx, by, half, r):
    group, n = divmod((bx * BRICK_Y + by) * 2 + half, 4)
    lane = lax.broadcasted_iota(jnp.int32, (EDGE, LANES), 1)
    first = EDGE * r + HALO * n
    return jnp.where(
        lane < LANES // 2,
        pltpu.roll(ends[0, group], (LANES - first) % LANES, 1),
        pltpu.roll(ends[1, group], (2 * LANES - HALO - first) % LANES, 1),
    )


def edge_place(bx, half, i):
    return (bx * 2 + half) * 2 + i


def side_place(side, f):
    return side * FIELDS + f


def faces_and_rows(grid, faces, odd_pairs, even_pairs, joined):
    sides = [jax.ShapeDtypeStruct((NY, LANES), jnp.float32)] * (2 - joined)

    def kernel(grid, odd_pairs, even_pairs, *refs):
        ins, refs = refs[: len(faces)], refs[len(faces) :]
        (layers, ends, low, high), refs = refs[:4], refs[4:]
        outs, (turned,) = refs[: len(sides)], refs[len(sides) :]
        odd = lax.axis_index("gz") & 1
        ends[odd] = even_pairs[...]
        ends[1 - odd] = odd_pairs[...]
        for side in range(2):
            face = ins[0].at[side] if joined else ins[side]

            def store(by, i, f, rows, first=0 if side else HALO):
                layers[f, first + i, pl.ds(by * EDGE, EDGE), :] = rows

            lay_out(swap_boxes([face[bz] for bz in range(BRICK_Z)]), turned, store)
        for f in range(FIELDS):
            for x in range(NEAR_X):
                cells = layers.at[f, 2 if x else 1] if x % (NX + 1) == 0 else grid.at[f, x - 1]
                low[pl.ds(row_of(f, x), HALO), :] = cells[pl.ds(0, HALO), :]
                high[pl.ds(row_of(f, x), HALO), :] = cells[pl.ds(NY - HALO, HALO), :]
        lane = lax.broadcasted_iota(jnp.int32, (EDGE, LANES), 1)
        for by, j, out in ((0, 0, low), (1, EDGE - 1, high)):
            edge = jnp.zeros((EDGE, LANES), jnp.float32)
            for bx in range(BRICK_X):
                for half in range(TILES // 2):
                    group, n = divmod((bx * BRICK_Y + by) * 2 + half, 4)
                    for i in range(2):
                        place = 2 * edge_place(bx, half, i)
                        lane_in = EDGE * (i * EDGE + j) + HALO * n
                        after = pltpu.roll(ends[0, group], (place + 1 - lane_in) % LANES, 1)
                        before = pltpu.roll(ends[1, group], (place - 1 - lane_in) % LANES, 1)
                        edge = jnp.where(lane == place, before, jnp.where(lane == place + 1, after, edge))
            out[pl.ds(ROWS, EDGE), :] = edge
        pair = lax.broadcasted_iota(jnp.int32, (NY, LANES), 1) // 2
        edges = [jnp.zeros((NY, LANES), jnp.float32)] * 2
        for side in range(2):
            cells = [[], [], [], []]
            for by in range(BRICK_Y):
                for j in range(EDGE):
                    turned[pl.ds(j * EDGE, EDGE), :] = beyond_ends(ends, side, by, side, side * EDGE + j)
                for f in range(FIELDS):
                    cells[f].append(turned[pl.ds(side * FIELDS + f, EDGE, stride=EDGE), :])
            for f in range(FIELDS):
                place = side_place(side, f)
                moved = pltpu.roll(jnp.concatenate(cells[f], 0), 2 * place + 1, 1)
                edges[side] = jnp.where(pair == place, moved, edges[side])
        if joined:
            outs[0][...] = jnp.where(pair < FIELDS, edges[0], edges[1])
        else:
            for out, edge in zip(outs, edges):
                out[...] = edge

    rows = jax.ShapeDtypeStruct((EDGES, LANES), jnp.float32)
    return pl.pallas_call(
        kernel,
        out_shape=[
            jax.ShapeDtypeStruct((FIELDS, 2 * HALO, NY, LANES), jnp.float32),
            jax.ShapeDtypeStruct((2, 2, 2 * FIELDS, LANES), jnp.float32),
            rows,
            rows,
        ]
        + sides,
        in_specs=[VMEM] * (3 + len(faces)),
        out_specs=[VMEM] * (4 + len(sides)),
        scratch_shapes=[pltpu.VMEM((LANES, LANES), jnp.float32)],
        compiler_params=ROOM,
        name="faces_and_rows",
    )(grid, odd_pairs, even_pairs, *faces)


def half_conductance(v):
    return 0.5 * (v * jnp.sqrt(v))


def step(cells, rates):
    return [v + (TIME_STEP * c) * r for v, c, r in zip(cells, DIFFUSION, rates)]


def rates(cells, s, beside):
    means = [s + n for _, n in beside]
    sums = []
    for f, v in enumerate(cells):
        terms = [m * (fields[f] - v) for m, (fields, _) in zip(means, beside)]
        sums.append(sum(terms[1:], terms[0]))
    return sums


def each(function, cells, *others):
    fields, s = cells
    columns = zip(fields, *[other[0] for other in others])
    return [function(*c) for c in columns], function(s, *[other[1] for other in others])


def z_beside(cells, across):
    lane = lax.broadcasted_iota(jnp.int32, cells[1].shape, 1)

    def after(v, other):
        return pltpu.roll(jnp.where(lane == 0, other, v), LANES - 1, 1)

    def before(v, other):
        return pltpu.roll(jnp.where(lane == LANES - 1, other, v), 1, 1)

    return [each(after, cells, across), each(before, cells, across)]


def y_beside(cells):
    row = lax.broadcasted_iota(jnp.int32, (NY, LANES), 0)

    def after(v):
        return jnp.where(row == NY - 1, v, pltpu.roll(v, NY - 1, 0))

    def before(v):
        return jnp.where(row == 0, v, pltpu.roll(v, 1, 0))

    return [each(after, cells), each(before, cells)]


def first_inside(grid, layers, ends):
    def kernel(
        grid, layers, ends, wide, halves, beyond, first, first_beyond, halves_beyond, turned
    ):
        for bx in range(BRICK_X):
            for by in range(BRICK_Y):
                for half in range(TILES // 2):

                    def store(t, i, f, rows, x=bx * EDGE + half * 4, by=by):
                        beyond[f, x + t * 2 + i, pl.ds(by * EDGE, EDGE), :] = rows

                    lay_out([beyond_ends(ends, bx, by, half, r) for r in range(16)], turned, store)
        for f in range(FIELDS):
            for x in range(HALO):
                wide[f, x] = layers[f, x]
                wide[f, HALO + NX + x] = layers[f, HALO + x]
        for x in range(HALO):
            halves[x] = half_conductance(layers[0, x])
            halves[HALO + NX + x] = half_conductance(layers[0, HALO + x])

        def prepare(x, carry):
            for f in range(FIELDS):
                wide[f, x + HALO] = grid[f, x]
            halves[x + HALO] = half_conductance(grid[0, x])
            halves_beyond[x] = half_conductance(beyond[0, x])
            return carry

        lax.fori_loop(0, NX, prepare, 0, unroll=4)

        def at(ref, s, x):
            return [ref[f, x] for f in range(FIELDS)], s[x]

        def inside(x, carry):
            here, over = at(wide, halves, x + HALO), at(beyond, halves_beyond, x)
            beside = [at(wide, halves, x + HALO - 1), at(wide, halves, x + HALO + 1)]
            beside += y_beside(here) + z_beside(here, over)
            for f, v in enumerate(step(here[0], rates(*here, beside))):
                first[f, x] = v
            left, right = jnp.maximum(x - 1, 0), jnp.minimum(x + 1, NX - 1)
            beside = [at(beyond, halves_beyond, left), at(beyond, halves_beyond, right)]
            beside += y_beside(over) + z_beside(over, here)
            for f, v in enumerate(step(over[0], rates(*over, beside))):
                first_beyond[f, x] = v
            return carry

        lax.fori_loop(0, NX, inside, 0, unroll=2)

    def shape(*sizes):
        return jax.ShapeDtypeStruct(sizes + (NY, LANES), jnp.float32)

    return pl.pallas_call(
        kernel,
        out_shape=[
            shape(FIELDS, WIDE_X),
            shape(WIDE_X),
            shape(FIELDS, NX),
            shape(FIELDS, NX),
            shape(FIELDS, NX),
            shape(NX),
        ],
        in_specs=[VMEM] * 3,
        out_specs=[VMEM] * 6,
        scratch_shapes=[pltpu.VMEM((LANES, LANES), jnp.float32)],
        compiler_params=ROOM,
        cost_estimate=pl.CostEstimate(flops=2**22, bytes_accessed=2**21, transcendentals=0),
        name="first_inside",
    )(grid, layers, ends)


PARTS = 4


def last_sections(wide, halves, first, first_beyond, beyond, halves_beyond, above, below, sides):
    def kernel(wide, halves, first_in, beyond_in, beyond, halves_beyond, above, below, *refs):
        ins, (out, *refs) = refs[: len(sides)], refs[len(sides) :]
        edges, first, first_beyond, around, fs, fbs, result, sems = refs
        factors = [TIME_STEP * c for c in DIFFUSION]
        row = lax.broadcasted_iota(jnp.int32, (EDGE, LANES), 0)

        def side_edge(side):
            packed = ins[0 if len(ins) == 1 else side][...]
            fields = [
                pltpu.roll(packed, LANES - 1 - 2 * side_place(side, f), 1) for f in range(FIELDS)
            ]
            return fields, half_conductance(fields[0])

        for sent_edge, at_row in ((below, 0), (above, EDGE - 1)):
            edge = sent_edge[pl.ds(ROWS, EDGE), :]
            for bx in range(BRICK_X):
                for half in range(TILES // 2):
                    for i in range(2):
                        tile = pltpu.roll(edge, LANES - 1 - 2 * edge_place(bx, half, i), 1)
                        for t in range(2):
                            x = bx * EDGE + half * 4 + t * 2 + i
                            rows = pl.ds(x * EDGE + at_row, FIELDS, stride=NX * EDGE)
                            edges[rows, :] = tile[t * FIELDS :][:FIELDS]

        def at(ref, s, x):
            return [ref[f, x] for f in range(FIELDS)], s[x]

        for side, x in ((1, 0), (0, NX + 1)):
            here = at(wide, halves, x + 1)
            beside = [at(wide, halves, x), at(wide, halves, x + 2)]
            beside += y_beside(here) + z_beside(here, side_edge(side))
            for f, v in enumerate(step(here[0], rates(*here, beside))):
                first[pl.ds((f * NEAR_X + x) * NY, NY), :] = v
        for f in range(FIELDS):
            for x in range(NX):
                first[pl.ds((f * NEAR_X + x + 1) * NY, NY), :] = first_in[f, x]

        wide_rows = wide.reshape(FIELDS * WIDE_X * NY, LANES)
        half_rows = halves.reshape(WIDE_X * NY, LANES)

        def sent(ref, depth, f, x, count):
            return ref[pl.ds(row_of(f, x) + depth, count, stride=HALO), :]

        for ref, depth, y, tile_row in ((below, 1, 0, 7), (above, 0, NY - 1, 0)):
            for x, count in ((0, 8), (8, 8), (16, 2)):
                s = half_rows[pl.ds((x + 1) * NY + y, count, stride=NY), :]
                mean = s + half_conductance(sent(ref, depth, 0, x, count))
                for f in range(FIELDS):
                    v = wide_rows[pl.ds((f * WIDE_X + x + 1) * NY + y, count, stride=NY), :]
                    rows = pl.ds((f * NEAR_X + x) * NY + y, count, stride=NY)
                    more = mean * (sent(ref, depth, f, x, count) - v)
                    first[rows, :] = first[rows, :] + factors[f] * more
            for x in (0, 8):

                def line(depth, shift):
                    fields = [sent(ref, depth, f, x + 1 + shift, 8) for f in range(FIELDS)]
                    return fields, half_conductance(fields[0])

                here = line(depth, 0)
                inner = (
                    [
                        wide_rows[pl.ds((f * WIDE_X + x + HALO) * NY + y, 8, stride=NY), :]
                        for f in range(FIELDS)
                    ],
                    half_rows[pl.ds((x + HALO) * NY + y, 8, stride=NY), :],
                )
                over = [
                    edges[pl.ds((f * NX + x) * EDGE + 7 - tile_row, 8, stride=EDGE), :]
                    for f in range(FIELDS)
                ]
                beside = [line(1 - depth, 0), inner, line(depth, -1), line(depth, 1)]
                beside += z_beside(here, (over, half_conductance(over[0])))
                for f, v in enumerate(step(here[0], rates(*here, beside))):
                    around[pl.ds((f * NX + x) * EDGE + tile_row, 8, stride=EDGE), :] = v

        for x in range(NX):
            s = halves_beyond[x]
            near = half_conductance(edges[pl.ds(x * EDGE, EDGE), :])
            for f in range(FIELDS):
                tile = edges[pl.ds((f * NX + x) * EDGE, EDGE), :]
                v, fresh = beyond[f, x], beyond_in[f, x]
                more = [
                    jnp.where(row == at_row, (near + s[n * EDGE :][:EDGE]) * (tile - v[n * EDGE :][:EDGE]), 0.0)
                    for n, at_row in enumerate((0, EDGE - 1))
                ]
                first_beyond[f, x] = fresh + factors[f] * jnp.concatenate(more, 0)
        for side, x in ((1, 0), (0, NX - 1)):
            fields, s = side_edge(side)
            for f in range(FIELDS):
                more = (s + halves_beyond[x]) * (fields[f] - beyond[f, x])
                first_beyond[f, x] = first_beyond[f, x] + factors[f] * more

        def near(x):
            return [
                first[pl.ds(pl.multiple_of((f * NEAR_X + x) * NY, NY), NY), :] for f in range(FIELDS)
            ]

        def conductances(x, carry):
            fs[x] = half_conductance(near(x)[0])
            return carry

        lax.fori_loop(0, NEAR_X, conductances, 0, unroll=6)

        def conductances_beyond(x, carry):
            fbs[x] = half_conductance(first_beyond[0, x])
            return carry

        lax.fori_loop(0, NX, conductances_beyond, 0, unroll=4)

        def second(x, carry):
            here = near(x + 1), fs[x + 1]
            tiles = [
                around[pl.ds(pl.multiple_of((f * NX + x) * EDGE, EDGE), EDGE), :]
                for f in range(FIELDS)
            ]
            ring_of = each(
                lambda v, tile: jnp.concatenate([v, tile], 0), here, (tiles, half_conductance(tiles[0]))
            )
            beside = [(near(x), fs[x]), (near(x + 2), fs[x + 2])]
            beside += [
                each(lambda v: pltpu.roll(v, WIDE_Y - 1, 0)[:NY], ring_of),
                each(lambda v: pltpu.roll(v, 1, 0)[:NY], ring_of),
            ]
            beside += z_beside(here, at(first_beyond, fbs, x))
            for f, v in enumerate(step(here[0], rates(*here, beside))):
                result[f, x] = 0.5 * wide[f, x + HALO] + 0.5 * v
            return carry

        copies = []
        for part in range(PARTS):
            start = part * (NX // PARTS)
            lax.fori_loop(start, start + NX // PARTS, second, 0, unroll=NX // PARTS)
            layers = pl.ds(start, NX // PARTS)
            copies.append(
                pltpu.make_async_copy(result.at[:, layers], out.at[:, layers], sems.at[part])
            )
            copies[-1].start()
        for copy in copies:
            copy.wait()

    def scratch(*shape):
        return pltpu.VMEM(shape + (LANES,), jnp.float32)

    return pl.pallas_call(
        kernel,
        out_shape=jax.ShapeDtypeStruct((FIELDS, NX, NY, LANES), jnp.float32),
        in_specs=[VMEM] * (8 + len(sides)),
        out_specs=HBM,
        scratch_shapes=[
            scratch(FIELDS * NX * EDGE),
            scratch(FIELDS * NEAR_X * NY),
            scratch(FIELDS, NX, NY),
            scratch(FIELDS * NX * EDGE),
            scratch(NEAR_X, NY),
            scratch(NX, NY),
            scratch(FIELDS, NX, NY),
            pltpu.SemaphoreType.DMA((PARTS,)),
        ],
        compiler_params=ROOM,
        name="last_sections",
    )(wide, halves, first, first_beyond, beyond, halves_beyond, above, below, *sides)


def body(old_fields, new_owner, old_owner):
    across, along = lax.axis_size("gx"), lax.axis_size("gz")
    group_size = across * along
    box_count = new_owner.shape[0]
    capacity = 2 * (box_count // group_size)
    split = group_size <= 8
    joined = across == 2
    departing = pack_boxes(old_fields, new_owner, group_size, capacity, split)
    table = position_table(old_owner, group_size, capacity)
    if split:
        order = (3, 1, 2, 4, 6, 5, 7, 0)
        arrived = [
            lax.ppermute(departing[k], ("gx", "gz"), [(i, i ^ k) for i in range(group_size)])
            if k
            else departing[k]
            for k in order
        ]
    else:
        order = [0]
        arrived = [
            lax.all_to_all(departing[0], ("gx", "gz"), split_axis=0, concat_axis=0, tiled=True)
        ]
    held, odd_pairs, even_pairs, *faces = boxes_in_place(
        arrived, order, table, box_count, capacity, split, joined
    )

    def along_x(sides):
        if joined:
            return [lax.ppermute(sides[0], "gx", ring(across, 1))]
        return [lax.ppermute(side, "gx", ring(across, step)) for side, step in zip(sides, (-1, 1))]

    faces = along_x(faces)
    odd_pairs = lax.ppermute(odd_pairs, "gz", pairs(along, 1))
    even_pairs = lax.ppermute(even_pairs, "gz", pairs(along, 0))
    grid = grid_from_boxes(held)
    layers, ends, low, high, *sides = faces_and_rows(
        grid, faces, odd_pairs, even_pairs, joined
    )
    rows = lax.axis_size("gy")
    above = lax.ppermute(low, "gy", ring(rows, -1))
    below = lax.ppermute(high, "gy", ring(rows, 1))
    sides = along_x(sides)
    wide, halves, beyond, first, first_beyond, halves_beyond = first_inside(grid, layers, ends)
    return last_sections(
        wide, halves, first, first_beyond, beyond, halves_beyond, above, below, sides
    )


def solution(mesh):
    return jax.shard_map(
        body,
        mesh=mesh,
        in_specs=(P(("gx", "gy", "gz"), None, None), P(("gx", "gy", "gz")), P(("gx", "gy", "gz"))),
        out_specs=P(None, "gx", "gy", "gz"),
        check_vma=False,
    )
```

```python
import jax
import jax.numpy as jnp
from jax import lax
from jax.experimental import pallas as pl
from jax.experimental.pallas import tpu as pltpu
from jax.sharding import PartitionSpec as P

EDGE = 8
FIELDS = 4
BRICK_X = 2
BRICK_Y = 2
BRICK_Z = 16
CELLS = EDGE**3
LANES = 128
TILES = CELLS // LANES
BOX = (TILES // 2, 2 * FIELDS, LANES)


DIFFUSION = (1.0, 3.3, 0.9, 1.2)
TIME_STEP = 0.012

VMEM = pl.BlockSpec(memory_space=pltpu.VMEM)
SMEM = pl.BlockSpec(memory_space=pltpu.SMEM)
HBM = pl.BlockSpec(memory_space=pltpu.HBM)
ROOM = pltpu.CompilerParams(vmem_limit_bytes=16 * 2**20)


def in_hbm(array):
    return pltpu.with_memory_space_constraint(array, pltpu.HBM)


def group_place():
    return lax.axis_index("gx") * lax.axis_size("gz") + lax.axis_index("gz")


def rank_table(owner, table, counts, group, capacity, boxes, empty):
    def clear(i, carry):
        table[i] = empty
        return carry

    lax.fori_loop(0, group * capacity, clear, 0, unroll=16)
    for g in range(group):
        counts[g] = g * capacity

    def place(b, carry):
        o = owner[b]
        slot = counts[o]
        table[slot] = b
        counts[o] = slot + 1
        return carry

    lax.fori_loop(0, boxes, place, 0, unroll=8)


def pack_boxes(old_fields, new_owner, group, capacity, split):
    boxes = new_owner.shape[0]
    pieces = group if split else 1
    rows = group * capacity // pieces

    def kernel(owner_hbm, fields_hbm, *refs):
        outs, (owner, fields, table, counts, sems) = refs[:pieces], refs[pieces:]
        fetch_owner = pltpu.make_async_copy(owner_hbm, owner, sems.at[0])
        fetch_fields = pltpu.make_async_copy(fields_hbm, fields, sems.at[1])
        fetch_owner.start()
        fetch_fields.start()
        fetch_owner.wait()
        rank_table(owner, table, counts, group, capacity, boxes, 0)
        fetch_fields.wait()
        for k, out in enumerate(outs):
            base = (group_place() ^ k) * capacity if split else 0

            def copy(r, carry, out=out, base=base):
                box = table[base + r]
                for t in range(TILES):
                    out[r, t // 2, pl.ds(t % 2 * FIELDS, FIELDS), :] = fields[
                        box, :, pl.ds(t * LANES, LANES)
                    ]
                return carry

            lax.fori_loop(0, rows, copy, 0, unroll=8)

    return pl.pallas_call(
        kernel,
        out_shape=[jax.ShapeDtypeStruct((rows,) + BOX, jnp.float32)] * pieces,
        in_specs=[HBM, HBM],
        out_specs=[VMEM] * pieces,
        scratch_shapes=[
            pltpu.SMEM((boxes,), jnp.int32),
            pltpu.VMEM(old_fields.shape, jnp.float32),
            pltpu.SMEM((group * capacity,), jnp.int32),
            pltpu.SMEM((group,), jnp.int32),
            pltpu.SemaphoreType.DMA((2,)),
        ],
        compiler_params=ROOM,
        name="pack_boxes",
    )(in_hbm(new_owner), in_hbm(old_fields))


def position_table(old_owner, group, capacity):
    boxes = old_owner.shape[0]

    def kernel(owner, table, counts):
        rank_table(owner, table, counts, group, capacity, boxes, boxes)

    return pl.pallas_call(
        kernel,
        out_shape=pltpu.SMEM((group * capacity,), jnp.int32),
        in_specs=[SMEM],
        out_specs=SMEM,
        scratch_shapes=[pltpu.SMEM((group,), jnp.int32)],
        compiler_params=ROOM,
        cost_estimate=pl.CostEstimate(flops=0, bytes_accessed=2**22, transcendentals=0),
        name="position_table",
    )(old_owner)


def swap_boxes(columns):
    lane = lax.broadcasted_iota(jnp.int32, columns[0].shape, 1)
    for bit in range(4):
        width = EDGE << bit
        upper = (lane & width) != 0
        fresh = list(columns)
        for low in range(16):
            if low >> bit & 1:
                continue
            high = low | 1 << bit
            a, b = columns[low], columns[high]
            fresh[low] = jnp.where(upper, pltpu.roll(b, width, 1), a)
            fresh[high] = jnp.where(upper, b, pltpu.roll(a, LANES - width, 1))
        columns = fresh
    return columns


def ring(count, step):
    return [(i, (i + step) % count) for i in range(count)]


def pairs(count, first):
    return [((i + first) % count, ((i ^ 1) + first) % count) for i in range(count)]


def boxes_in_place(arrived, order, table, boxes, capacity, split, joined):
    pieces = len(arrived)
    rows = table.shape[0] // pieces
    half = boxes // BRICK_X
    face = (BRICK_Z, BRICK_Y * FIELDS, LANES)
    faces = [jax.ShapeDtypeStruct((2,) + face if joined else face, jnp.float32)] * (2 - joined)
    end = jax.ShapeDtypeStruct((2, 2 * FIELDS, LANES), jnp.float32)

    def kernel(table, *refs):
        ins, refs = refs[:pieces], refs[pieces:]
        held, odd_pairs, even_pairs, *outs = refs
        odd = lax.axis_index("gz") & 1 != 0
        for k, rows_in in zip(order, ins):
            base = (group_place() ^ k) * capacity if split else 0

            def scatter(r, carry, rows_in=rows_in, base=base):
                held[table[base + r]] = rows_in[r]
                return carry

            lax.fori_loop(0, rows, scatter, 0, unroll=8)
        for side in range(2):
            out = outs[0].at[side] if joined else outs[side]
            for by in range(BRICK_Y):
                for bz in range(BRICK_Z):
                    p = side * half + by * BRICK_Z + bz
                    out[bz, pl.ds(by * FIELDS, FIELDS), :] = held[
                        p, side, pl.ds(side * FIELDS, FIELDS), :
                    ]
        pair = lax.broadcasted_iota(jnp.int32, (2 * FIELDS, LANES), 1) % EDGE // HALO
        for group in range(2):
            ends = []
            for bz, first in ((0, 0), (BRICK_Z - 1, EDGE - HALO)):
                packed = jnp.zeros((2 * FIELDS, LANES), jnp.float32)
                for n in range(4):
                    b, part = divmod(group * 4 + n, 2)
                    cells = held[b * BRICK_Z + bz, part]
                    shift = (n * HALO - first) % LANES
                    packed = jnp.where(pair == n, pltpu.roll(cells, shift, 1) if shift else cells, packed)
                ends.append(packed)
            odd_pairs[group] = jnp.where(odd, ends[1], ends[0])
            even_pairs[group] = jnp.where(odd, ends[0], ends[1])

    return pl.pallas_call(
        kernel,
        out_shape=[jax.ShapeDtypeStruct((boxes + 1,) + BOX, jnp.float32), end, end] + faces,
        in_specs=[SMEM] + [VMEM] * pieces,
        out_specs=[VMEM] * (3 + len(faces)),
        compiler_params=ROOM,
        name="boxes_in_place",
    )(pltpu.with_memory_space_constraint(table, pltpu.SMEM), *arrived)


HALO = 2
NX = BRICK_X * EDGE
NY = BRICK_Y * EDGE
WIDE_X = NX + 2 * HALO
WIDE_Y = NY + EDGE
NEAR_X = NX + 2


def lay_out(columns, turned, store):
    for r in range(16):
        turned[pl.ds(r * 8, 8), :] = columns[r]
    for a in range(2):
        for i in range(2):
            for f in range(FIELDS):
                store(a, i, f, turned[pl.ds(i * 64 + a * FIELDS + f, 8, stride=8), :])


def grid_from_boxes(held):
    def kernel(held, grid, turned):
        for bx in range(BRICK_X):
            for by in range(BRICK_Y):
                first = (bx * BRICK_Y + by) * BRICK_Z
                for half in range(TILES // 2):

                    def store(t, i, f, rows, x=bx * EDGE + half * 4, by=by):
                        grid[f, x + t * 2 + i, pl.ds(by * EDGE, EDGE), :] = rows

                    columns = swap_boxes([held[first + bz, half] for bz in range(BRICK_Z)])
                    lay_out(columns, turned, store)

    return pl.pallas_call(
        kernel,
        out_shape=jax.ShapeDtypeStruct((FIELDS, NX, NY, LANES), jnp.float32),
        in_specs=[VMEM],
        out_specs=VMEM,
        scratch_shapes=[pltpu.VMEM((LANES, LANES), jnp.float32)],
        cost_estimate=pl.CostEstimate(flops=2**22, bytes_accessed=2**21, transcendentals=0),
        compiler_params=ROOM,
        name="grid_from_boxes",
    )(held)


ROWS = FIELDS * NEAR_X * HALO
EDGES = ROWS + EDGE


def row_of(f, x):
    return (f * NEAR_X + x) * HALO


def beyond_ends(ends, bx, by, half, r):
    group, n = divmod((bx * BRICK_Y + by) * 2 + half, 4)
    lane = lax.broadcasted_iota(jnp.int32, (EDGE, LANES), 1)
    first = EDGE * r + HALO * n
    return jnp.where(
        lane < LANES // 2,
        pltpu.roll(ends[0, group], (LANES - first) % LANES, 1),
        pltpu.roll(ends[1, group], (2 * LANES - HALO - first) % LANES, 1),
    )


def edge_place(bx, half, i):
    return (bx * 2 + half) * 2 + i


def side_place(side, f):
    return side * FIELDS + f


def faces_and_rows(grid, faces, odd_pairs, even_pairs, joined):
    sides = [jax.ShapeDtypeStruct((NY, LANES), jnp.float32)] * (2 - joined)

    def kernel(grid, odd_pairs, even_pairs, *refs):
        ins, refs = refs[: len(faces)], refs[len(faces) :]
        (layers, ends, low, high), refs = refs[:4], refs[4:]
        outs, (turned,) = refs[: len(sides)], refs[len(sides) :]
        odd = lax.axis_index("gz") & 1
        ends[odd] = even_pairs[...]
        ends[1 - odd] = odd_pairs[...]
        for side in range(2):
            face = ins[0].at[side] if joined else ins[side]

            def store(by, i, f, rows, first=0 if side else HALO):
                layers[f, first + i, pl.ds(by * EDGE, EDGE), :] = rows

            lay_out(swap_boxes([face[bz] for bz in range(BRICK_Z)]), turned, store)
        for f in range(FIELDS):
            for x in range(NEAR_X):
                cells = layers.at[f, 2 if x else 1] if x % (NX + 1) == 0 else grid.at[f, x - 1]
                low[pl.ds(row_of(f, x), HALO), :] = cells[pl.ds(0, HALO), :]
                high[pl.ds(row_of(f, x), HALO), :] = cells[pl.ds(NY - HALO, HALO), :]
        lane = lax.broadcasted_iota(jnp.int32, (EDGE, LANES), 1)
        for by, j, out in ((0, 0, low), (1, EDGE - 1, high)):
            edge = jnp.zeros((EDGE, LANES), jnp.float32)
            for bx in range(BRICK_X):
                for half in range(TILES // 2):
                    group, n = divmod((bx * BRICK_Y + by) * 2 + half, 4)
                    for i in range(2):
                        place = 2 * edge_place(bx, half, i)
                        lane_in = EDGE * (i * EDGE + j) + HALO * n
                        after = pltpu.roll(ends[0, group], (place + 1 - lane_in) % LANES, 1)
                        before = pltpu.roll(ends[1, group], (place - 1 - lane_in) % LANES, 1)
                        edge = jnp.where(lane == place, before, jnp.where(lane == place + 1, after, edge))
            out[pl.ds(ROWS, EDGE), :] = edge
        pair = lax.broadcasted_iota(jnp.int32, (NY, LANES), 1) // 2
        edges = [jnp.zeros((NY, LANES), jnp.float32)] * 2
        for side in range(2):
            cells = [[], [], [], []]
            for by in range(BRICK_Y):
                for j in range(EDGE):
                    turned[pl.ds(j * EDGE, EDGE), :] = beyond_ends(ends, side, by, side, side * EDGE + j)
                for f in range(FIELDS):
                    cells[f].append(turned[pl.ds(side * FIELDS + f, EDGE, stride=EDGE), :])
            for f in range(FIELDS):
                place = side_place(side, f)
                moved = pltpu.roll(jnp.concatenate(cells[f], 0), 2 * place + 1, 1)
                edges[side] = jnp.where(pair == place, moved, edges[side])
        if joined:
            outs[0][...] = jnp.where(pair < FIELDS, edges[0], edges[1])
        else:
            for out, edge in zip(outs, edges):
                out[...] = edge

    rows = jax.ShapeDtypeStruct((EDGES, LANES), jnp.float32)
    return pl.pallas_call(
        kernel,
        out_shape=[
            jax.ShapeDtypeStruct((FIELDS, 2 * HALO, NY, LANES), jnp.float32),
            jax.ShapeDtypeStruct((2, 2, 2 * FIELDS, LANES), jnp.float32),
            rows,
            rows,
        ]
        + sides,
        in_specs=[VMEM] * (3 + len(faces)),
        out_specs=[VMEM] * (4 + len(sides)),
        scratch_shapes=[pltpu.VMEM((LANES, LANES), jnp.float32)],
        compiler_params=ROOM,
        name="faces_and_rows",
    )(grid, odd_pairs, even_pairs, *faces)


def half_conductance(v):
    return 0.5 * (v * jnp.sqrt(v))


def step(cells, rates):
    return [v + (TIME_STEP * c) * r for v, c, r in zip(cells, DIFFUSION, rates)]


def rates(cells, s, beside):
    means = [s + n for _, n in beside]
    total = sum(means[1:], means[0])
    sums = []
    for f, v in enumerate(cells):
        terms = [m * fields[f] for m, (fields, _) in zip(means, beside)]
        sums.append(sum(terms[1:], terms[0]) - v * total)
    return sums


def each(function, cells, *others):
    fields, s = cells
    columns = zip(fields, *[other[0] for other in others])
    return [function(*c) for c in columns], function(s, *[other[1] for other in others])


def z_beside(cells, across):
    lane = lax.broadcasted_iota(jnp.int32, cells[1].shape, 1)

    def after(v, other):
        return pltpu.roll(jnp.where(lane == 0, other, v), LANES - 1, 1)

    def before(v, other):
        return pltpu.roll(jnp.where(lane == LANES - 1, other, v), 1, 1)

    return [each(after, cells, across), each(before, cells, across)]


def y_beside(cells):
    row = lax.broadcasted_iota(jnp.int32, (NY, LANES), 0)

    def after(v):
        return jnp.where(row == NY - 1, v, pltpu.roll(v, NY - 1, 0))

    def before(v):
        return jnp.where(row == 0, v, pltpu.roll(v, 1, 0))

    return [each(after, cells), each(before, cells)]


def first_inside(grid, layers, ends):
    def kernel(
        grid, layers, ends, wide, halves, beyond, first, first_beyond, halves_beyond, turned
    ):
        for bx in range(BRICK_X):
            for by in range(BRICK_Y):
                for half in range(TILES // 2):

                    def store(t, i, f, rows, x=bx * EDGE + half * 4, by=by):
                        beyond[f, x + t * 2 + i, pl.ds(by * EDGE, EDGE), :] = rows

                    lay_out([beyond_ends(ends, bx, by, half, r) for r in range(16)], turned, store)
        for f in range(FIELDS):
            for x in range(HALO):
                wide[f, x] = layers[f, x]
                wide[f, HALO + NX + x] = layers[f, HALO + x]
        for x in range(HALO):
            halves[x] = half_conductance(layers[0, x])
            halves[HALO + NX + x] = half_conductance(layers[0, HALO + x])

        def prepare(x, carry):
            for f in range(FIELDS):
                wide[f, x + HALO] = grid[f, x]
            halves[x + HALO] = half_conductance(grid[0, x])
            halves_beyond[x] = half_conductance(beyond[0, x])
            return carry

        lax.fori_loop(0, NX, prepare, 0, unroll=4)

        def at(ref, s, x):
            return [ref[f, x] for f in range(FIELDS)], s[x]

        def inside(x, carry):
            here, over = at(wide, halves, x + HALO), at(beyond, halves_beyond, x)
            beside = [at(wide, halves, x + HALO - 1), at(wide, halves, x + HALO + 1)]
            beside += y_beside(here) + z_beside(here, over)
            for f, v in enumerate(step(here[0], rates(*here, beside))):
                first[f, x] = v
            left, right = jnp.maximum(x - 1, 0), jnp.minimum(x + 1, NX - 1)
            beside = [at(beyond, halves_beyond, left), at(beyond, halves_beyond, right)]
            beside += y_beside(over) + z_beside(over, here)
            for f, v in enumerate(step(over[0], rates(*over, beside))):
                first_beyond[f, x] = v
            return carry

        lax.fori_loop(0, NX, inside, 0, unroll=2)

    def shape(*sizes):
        return jax.ShapeDtypeStruct(sizes + (NY, LANES), jnp.float32)

    return pl.pallas_call(
        kernel,
        out_shape=[
            shape(FIELDS, WIDE_X),
            shape(WIDE_X),
            shape(FIELDS, NX),
            shape(FIELDS, NX),
            shape(FIELDS, NX),
            shape(NX),
        ],
        in_specs=[VMEM] * 3,
        out_specs=[VMEM] * 6,
        scratch_shapes=[pltpu.VMEM((LANES, LANES), jnp.float32)],
        compiler_params=ROOM,
        cost_estimate=pl.CostEstimate(flops=2**22, bytes_accessed=2**21, transcendentals=0),
        name="first_inside",
    )(grid, layers, ends)


PARTS = 8


def last_sections(wide, halves, first, first_beyond, beyond, halves_beyond, above, below, sides):
    def kernel(wide, halves, first_in, beyond_in, beyond, halves_beyond, above, below, *refs):
        ins, (out, *refs) = refs[: len(sides)], refs[len(sides) :]
        edges, first, first_beyond, around, fs, fbs, below_halves, above_halves, result, sems = refs
        factors = [TIME_STEP * c for c in DIFFUSION]
        row = lax.broadcasted_iota(jnp.int32, (EDGE, LANES), 0)

        def side_edge(side):
            packed = ins[0 if len(ins) == 1 else side][...]
            fields = [
                pltpu.roll(packed, LANES - 1 - 2 * side_place(side, f), 1) for f in range(FIELDS)
            ]
            return fields, half_conductance(fields[0])

        for sent_edge, at_row in ((below, 0), (above, EDGE - 1)):
            edge = sent_edge[pl.ds(ROWS, EDGE), :]
            for bx in range(BRICK_X):
                for half in range(TILES // 2):
                    for i in range(2):
                        tile = pltpu.roll(edge, LANES - 1 - 2 * edge_place(bx, half, i), 1)
                        for t in range(2):
                            x = bx * EDGE + half * 4 + t * 2 + i
                            rows = pl.ds(x * EDGE + at_row, FIELDS, stride=NX * EDGE)
                            edges[rows, :] = tile[t * FIELDS :][:FIELDS]

        def at(ref, s, x):
            return [ref[f, x] for f in range(FIELDS)], s[x]

        for side, x in ((1, 0), (0, NX + 1)):
            here = at(wide, halves, x + 1)
            beside = [at(wide, halves, x), at(wide, halves, x + 2)]
            beside += y_beside(here) + z_beside(here, side_edge(side))
            for f, v in enumerate(step(here[0], rates(*here, beside))):
                first[pl.ds((f * NEAR_X + x) * NY, NY), :] = v
        for f in range(FIELDS):
            for x in range(NX):
                first[pl.ds((f * NEAR_X + x + 1) * NY, NY), :] = first_in[f, x]

        wide_rows = wide.reshape(FIELDS * WIDE_X * NY, LANES)
        half_rows = halves.reshape(WIDE_X * NY, LANES)

        for ref, sent_halves in ((below, below_halves), (above, above_halves)):
            sent_halves[...] = half_conductance(ref[pl.ds(0, sent_halves.shape[0]), :])

        def sent(ref, depth, f, x, count):
            return ref[pl.ds(row_of(f, x) + depth, count, stride=HALO), :]

        for ref, ref_halves, depth, y, tile_row in (
            (below, below_halves, 1, 0, 7),
            (above, above_halves, 0, NY - 1, 0),
        ):
            for x, count in ((0, 8), (8, 8), (16, 2)):
                s = half_rows[pl.ds((x + 1) * NY + y, count, stride=NY), :]
                mean = s + sent(ref_halves, depth, 0, x, count)
                for f in range(FIELDS):
                    v = wide_rows[pl.ds((f * WIDE_X + x + 1) * NY + y, count, stride=NY), :]
                    rows = pl.ds((f * NEAR_X + x) * NY + y, count, stride=NY)
                    more = mean * (sent(ref, depth, f, x, count) - v)
                    first[rows, :] = first[rows, :] + factors[f] * more
            for x in (0, 8):

                def line(depth, shift):
                    fields = [sent(ref, depth, f, x + 1 + shift, 8) for f in range(FIELDS)]
                    return fields, sent(ref_halves, depth, 0, x + 1 + shift, 8)

                here = line(depth, 0)
                inner = (
                    [
                        wide_rows[pl.ds((f * WIDE_X + x + HALO) * NY + y, 8, stride=NY), :]
                        for f in range(FIELDS)
                    ],
                    half_rows[pl.ds((x + HALO) * NY + y, 8, stride=NY), :],
                )
                over = [
                    edges[pl.ds((f * NX + x) * EDGE + 7 - tile_row, 8, stride=EDGE), :]
                    for f in range(FIELDS)
                ]
                beside = [line(1 - depth, 0), inner, line(depth, -1), line(depth, 1)]
                beside += z_beside(here, (over, half_conductance(over[0])))
                for f, v in enumerate(step(here[0], rates(*here, beside))):
                    around[pl.ds((f * NX + x) * EDGE + tile_row, 8, stride=EDGE), :] = v

        for x in range(NX):
            s = halves_beyond[x]
            near = half_conductance(edges[pl.ds(x * EDGE, EDGE), :])
            for f in range(FIELDS):
                tile = edges[pl.ds((f * NX + x) * EDGE, EDGE), :]
                v, fresh = beyond[f, x], beyond_in[f, x]
                more = [
                    jnp.where(row == at_row, (near + s[n * EDGE :][:EDGE]) * (tile - v[n * EDGE :][:EDGE]), 0.0)
                    for n, at_row in enumerate((0, EDGE - 1))
                ]
                first_beyond[f, x] = fresh + factors[f] * jnp.concatenate(more, 0)
        for side, x in ((1, 0), (0, NX - 1)):
            fields, s = side_edge(side)
            for f in range(FIELDS):
                more = (s + halves_beyond[x]) * (fields[f] - beyond[f, x])
                first_beyond[f, x] = first_beyond[f, x] + factors[f] * more

        def near(x):
            return [
                first[pl.ds(pl.multiple_of((f * NEAR_X + x) * NY, NY), NY), :] for f in range(FIELDS)
            ]

        def conductances(x, carry):
            fs[x] = half_conductance(near(x)[0])
            return carry

        lax.fori_loop(0, NEAR_X, conductances, 0, unroll=6)

        def conductances_beyond(x, carry):
            fbs[x] = half_conductance(first_beyond[0, x])
            return carry

        lax.fori_loop(0, NX, conductances_beyond, 0, unroll=4)

        def second(x, carry):
            here = near(x + 1), fs[x + 1]
            tiles = [
                around[pl.ds(pl.multiple_of((f * NX + x) * EDGE, EDGE), EDGE), :]
                for f in range(FIELDS)
            ]
            ring_of = each(
                lambda v, tile: jnp.concatenate([v, tile], 0), here, (tiles, half_conductance(tiles[0]))
            )
            beside = [(near(x), fs[x]), (near(x + 2), fs[x + 2])]
            beside += [
                each(lambda v: pltpu.roll(v, WIDE_Y - 1, 0)[:NY], ring_of),
                each(lambda v: pltpu.roll(v, 1, 0)[:NY], ring_of),
            ]
            beside += z_beside(here, at(first_beyond, fbs, x))
            for f, v in enumerate(step(here[0], rates(*here, beside))):
                result[f, x] = 0.5 * wide[f, x + HALO] + 0.5 * v
            return carry

        copies = []
        for part in range(PARTS):
            start = part * (NX // PARTS)
            lax.fori_loop(start, start + NX // PARTS, second, 0, unroll=NX // PARTS)
            layers = pl.ds(start, NX // PARTS)
            copies.append(
                pltpu.make_async_copy(result.at[:, layers], out.at[:, layers], sems.at[part])
            )
            copies[-1].start()
        for copy in copies:
            copy.wait()

    def scratch(*shape):
        return pltpu.VMEM(shape + (LANES,), jnp.float32)

    return pl.pallas_call(
        kernel,
        out_shape=jax.ShapeDtypeStruct((FIELDS, NX, NY, LANES), jnp.float32),
        in_specs=[VMEM] * (8 + len(sides)),
        out_specs=HBM,
        scratch_shapes=[
            scratch(FIELDS * NX * EDGE),
            scratch(FIELDS * NEAR_X * NY),
            scratch(FIELDS, NX, NY),
            scratch(FIELDS * NX * EDGE),
            scratch(NEAR_X, NY),
            scratch(NX, NY),
            scratch(5 * EDGE),
            scratch(5 * EDGE),
            scratch(FIELDS, NX, NY),
            pltpu.SemaphoreType.DMA((PARTS,)),
        ],
        compiler_params=ROOM,
        name="last_sections",
    )(wide, halves, first, first_beyond, beyond, halves_beyond, above, below, *sides)


def body(old_fields, new_owner, old_owner):
    across, along = lax.axis_size("gx"), lax.axis_size("gz")
    group_size = across * along
    box_count = new_owner.shape[0]
    capacity = 2 * (box_count // group_size)
    split = group_size <= 8
    joined = across == 2
    departing = pack_boxes(old_fields, new_owner, group_size, capacity, split)
    table = position_table(old_owner, group_size, capacity)
    if split:
        order = (3, 1, 2, 4, 6, 5, 7, 0)
        arrived = [
            lax.ppermute(departing[k], ("gx", "gz"), [(i, i ^ k) for i in range(group_size)])
            if k
            else departing[k]
            for k in order
        ]
    else:
        order = [0]
        arrived = [
            lax.all_to_all(departing[0], ("gx", "gz"), split_axis=0, concat_axis=0, tiled=True)
        ]
    held, odd_pairs, even_pairs, *faces = boxes_in_place(
        arrived, order, table, box_count, capacity, split, joined
    )

    def along_x(sides):
        if joined:
            return [lax.ppermute(sides[0], "gx", ring(across, 1))]
        return [lax.ppermute(side, "gx", ring(across, step)) for side, step in zip(sides, (-1, 1))]

    faces = along_x(faces)
    odd_pairs = lax.ppermute(odd_pairs, "gz", pairs(along, 1))
    even_pairs = lax.ppermute(even_pairs, "gz", pairs(along, 0))
    grid = grid_from_boxes(held)
    layers, ends, low, high, *sides = faces_and_rows(
        grid, faces, odd_pairs, even_pairs, joined
    )
    rows = lax.axis_size("gy")
    above = lax.ppermute(low, "gy", ring(rows, -1))
    below = lax.ppermute(high, "gy", ring(rows, 1))
    sides = along_x(sides)
    wide, halves, beyond, first, first_beyond, halves_beyond = first_inside(grid, layers, ends)
    return last_sections(
        wide, halves, first, first_beyond, beyond, halves_beyond, above, below, sides
    )


def solution(mesh):
    return jax.shard_map(
        body,
        mesh=mesh,
        in_specs=(P(("gx", "gy", "gz"), None, None), P(("gx", "gy", "gz")), P(("gx", "gy", "gz"))),
        out_specs=P(None, "gx", "gy", "gz"),
        check_vma=False,
    )
```

```python
import jax
import jax.numpy as jnp
from jax import lax
from jax.experimental import pallas as pl
from jax.experimental.pallas import tpu as pltpu
from jax.sharding import PartitionSpec as P

EDGE = 8
FIELDS = 4
BRICK_X = 2
BRICK_Y = 2
BRICK_Z = 16
CELLS = EDGE**3
LANES = 128
TILES = CELLS // LANES
BOX = (TILES // 2, 2 * FIELDS, LANES)


DIFFUSION = (1.0, 3.3, 0.9, 1.2)
TIME_STEP = 0.012

VMEM = pl.BlockSpec(memory_space=pltpu.VMEM)
SMEM = pl.BlockSpec(memory_space=pltpu.SMEM)
HBM = pl.BlockSpec(memory_space=pltpu.HBM)
ROOM = pltpu.CompilerParams(vmem_limit_bytes=16 * 2**20)


def in_hbm(array):
    return pltpu.with_memory_space_constraint(array, pltpu.HBM)


def group_place():
    return lax.axis_index("gx") * lax.axis_size("gz") + lax.axis_index("gz")


def rank_table(owner, table, counts, group, capacity, boxes, empty):
    def clear(i, carry):
        table[i] = empty
        return carry

    lax.fori_loop(0, group * capacity, clear, 0, unroll=16)
    for g in range(group):
        counts[g] = g * capacity

    def place(b, carry):
        o = owner[b]
        slot = counts[o]
        table[slot] = b
        counts[o] = slot + 1
        return carry

    lax.fori_loop(0, boxes, place, 0, unroll=8)


def pack_boxes(old_fields, new_owner, group, capacity, split):
    boxes = new_owner.shape[0]
    pieces = group if split else 1
    rows = group * capacity // pieces

    def kernel(owner_hbm, fields_hbm, *refs):
        outs, (owner, fields, table, counts, sems) = refs[:pieces], refs[pieces:]
        fetch_owner = pltpu.make_async_copy(owner_hbm, owner, sems.at[0])
        fetch_fields = pltpu.make_async_copy(fields_hbm, fields, sems.at[1])
        fetch_owner.start()
        fetch_fields.start()
        fetch_owner.wait()
        rank_table(owner, table, counts, group, capacity, boxes, 0)
        fetch_fields.wait()
        for k, out in enumerate(outs):
            base = (group_place() ^ k) * capacity if split else 0

            def copy(r, carry, out=out, base=base):
                box = table[base + r]
                for t in range(TILES):
                    out[r, t // 2, pl.ds(t % 2 * FIELDS, FIELDS), :] = fields[
                        box, :, pl.ds(t * LANES, LANES)
                    ]
                return carry

            lax.fori_loop(0, rows, copy, 0, unroll=8)

    return pl.pallas_call(
        kernel,
        out_shape=[jax.ShapeDtypeStruct((rows,) + BOX, jnp.float32)] * pieces,
        in_specs=[HBM, HBM],
        out_specs=[VMEM] * pieces,
        scratch_shapes=[
            pltpu.SMEM((boxes,), jnp.int32),
            pltpu.VMEM(old_fields.shape, jnp.float32),
            pltpu.SMEM((group * capacity,), jnp.int32),
            pltpu.SMEM((group,), jnp.int32),
            pltpu.SemaphoreType.DMA((2,)),
        ],
        compiler_params=ROOM,
        name="pack_boxes",
    )(in_hbm(new_owner), in_hbm(old_fields))


def position_table(old_owner, group, capacity):
    boxes = old_owner.shape[0]

    def kernel(owner, table, counts):
        rank_table(owner, table, counts, group, capacity, boxes, boxes)

    return pl.pallas_call(
        kernel,
        out_shape=pltpu.SMEM((group * capacity,), jnp.int32),
        in_specs=[SMEM],
        out_specs=SMEM,
        scratch_shapes=[pltpu.SMEM((group,), jnp.int32)],
        compiler_params=ROOM,
        cost_estimate=pl.CostEstimate(flops=0, bytes_accessed=2**22, transcendentals=0),
        name="position_table",
    )(old_owner)


def swap_boxes(columns):
    lane = lax.broadcasted_iota(jnp.int32, columns[0].shape, 1)
    for bit in range(4):
        width = EDGE << bit
        upper = (lane & width) != 0
        fresh = list(columns)
        for low in range(16):
            if low >> bit & 1:
                continue
            high = low | 1 << bit
            a, b = columns[low], columns[high]
            fresh[low] = jnp.where(upper, pltpu.roll(b, width, 1), a)
            fresh[high] = jnp.where(upper, b, pltpu.roll(a, LANES - width, 1))
        columns = fresh
    return columns


def ring(count, step):
    return [(i, (i + step) % count) for i in range(count)]


def pairs(count, first):
    return [((i + first) % count, ((i ^ 1) + first) % count) for i in range(count)]


def boxes_in_place(arrived, order, table, boxes, capacity, split, joined):
    pieces = len(arrived)
    rows = table.shape[0] // pieces
    half = boxes // BRICK_X
    face = (BRICK_Z, BRICK_Y * FIELDS, LANES)
    faces = [jax.ShapeDtypeStruct((2,) + face if joined else face, jnp.float32)] * (2 - joined)
    end = jax.ShapeDtypeStruct((2, 2 * FIELDS, LANES), jnp.float32)

    def kernel(table, *refs):
        ins, refs = refs[:pieces], refs[pieces:]
        held, odd_pairs, even_pairs, *outs = refs
        odd = lax.axis_index("gz") & 1 != 0
        for k, rows_in in zip(order, ins):
            base = (group_place() ^ k) * capacity if split else 0

            def scatter(r, carry, rows_in=rows_in, base=base):
                held[table[base + r]] = rows_in[r]
                return carry

            lax.fori_loop(0, rows, scatter, 0, unroll=8)
        for side in range(2):
            out = outs[0].at[side] if joined else outs[side]
            for by in range(BRICK_Y):
                for bz in range(BRICK_Z):
                    p = side * half + by * BRICK_Z + bz
                    out[bz, pl.ds(by * FIELDS, FIELDS), :] = held[
                        p, side, pl.ds(side * FIELDS, FIELDS), :
                    ]
        pair = lax.broadcasted_iota(jnp.int32, (2 * FIELDS, LANES), 1) % EDGE // HALO
        for group in range(2):
            ends = []
            for bz, first in ((0, 0), (BRICK_Z - 1, EDGE - HALO)):
                packed = jnp.zeros((2 * FIELDS, LANES), jnp.float32)
                for n in range(4):
                    b, part = divmod(group * 4 + n, 2)
                    cells = held[b * BRICK_Z + bz, part]
                    shift = (n * HALO - first) % LANES
                    packed = jnp.where(pair == n, pltpu.roll(cells, shift, 1) if shift else cells, packed)
                ends.append(packed)
            odd_pairs[group] = jnp.where(odd, ends[1], ends[0])
            even_pairs[group] = jnp.where(odd, ends[0], ends[1])

    return pl.pallas_call(
        kernel,
        out_shape=[jax.ShapeDtypeStruct((boxes + 1,) + BOX, jnp.float32), end, end] + faces,
        in_specs=[SMEM] + [VMEM] * pieces,
        out_specs=[VMEM] * (3 + len(faces)),
        compiler_params=ROOM,
        name="boxes_in_place",
    )(pltpu.with_memory_space_constraint(table, pltpu.SMEM), *arrived)


HALO = 2
NX = BRICK_X * EDGE
NY = BRICK_Y * EDGE
WIDE_X = NX + 2 * HALO
WIDE_Y = NY + EDGE
NEAR_X = NX + 2


def lay_out(columns, turned, store):
    for r in range(16):
        turned[pl.ds(r * 8, 8), :] = columns[r]
    for a in range(2):
        for i in range(2):
            for f in range(FIELDS):
                store(a, i, f, turned[pl.ds(i * 64 + a * FIELDS + f, 8, stride=8), :])


def grid_from_boxes(held):
    def kernel(held, grid, turned):
        for bx in range(BRICK_X):
            for by in range(BRICK_Y):
                first = (bx * BRICK_Y + by) * BRICK_Z
                for half in range(TILES // 2):

                    def store(t, i, f, rows, x=bx * EDGE + half * 4, by=by):
                        grid[f, x + t * 2 + i, pl.ds(by * EDGE, EDGE), :] = rows

                    columns = swap_boxes([held[first + bz, half] for bz in range(BRICK_Z)])
                    lay_out(columns, turned, store)

    return pl.pallas_call(
        kernel,
        out_shape=jax.ShapeDtypeStruct((FIELDS, NX, NY, LANES), jnp.float32),
        in_specs=[VMEM],
        out_specs=VMEM,
        scratch_shapes=[pltpu.VMEM((LANES, LANES), jnp.float32)],
        cost_estimate=pl.CostEstimate(flops=2**22, bytes_accessed=2**21, transcendentals=0),
        compiler_params=ROOM,
        name="grid_from_boxes",
    )(held)


ROWS = FIELDS * NEAR_X * HALO
EDGES = ROWS + EDGE


def row_of(f, x):
    return (f * NEAR_X + x) * HALO


def beyond_ends(ends, bx, by, half, r):
    group, n = divmod((bx * BRICK_Y + by) * 2 + half, 4)
    lane = lax.broadcasted_iota(jnp.int32, (EDGE, LANES), 1)
    first = EDGE * r + HALO * n
    return jnp.where(
        lane < LANES // 2,
        pltpu.roll(ends[0, group], (LANES - first) % LANES, 1),
        pltpu.roll(ends[1, group], (2 * LANES - HALO - first) % LANES, 1),
    )


def edge_place(bx, half, i):
    return (bx * 2 + half) * 2 + i


def side_place(side, f):
    return side * FIELDS + f


def faces_and_rows(grid, faces, odd_pairs, even_pairs, joined):
    sides = [jax.ShapeDtypeStruct((NY, LANES), jnp.float32)] * (2 - joined)

    def kernel(grid, odd_pairs, even_pairs, *refs):
        ins, refs = refs[: len(faces)], refs[len(faces) :]
        (layers, ends, low, high), refs = refs[:4], refs[4:]
        outs, (turned,) = refs[: len(sides)], refs[len(sides) :]
        odd = lax.axis_index("gz") & 1
        ends[odd] = even_pairs[...]
        ends[1 - odd] = odd_pairs[...]
        for side in range(2):
            face = ins[0].at[side] if joined else ins[side]

            def store(by, i, f, rows, first=0 if side else HALO):
                layers[f, first + i, pl.ds(by * EDGE, EDGE), :] = rows

            lay_out(swap_boxes([face[bz] for bz in range(BRICK_Z)]), turned, store)
        for f in range(FIELDS):
            for x in range(NEAR_X):
                cells = layers.at[f, 2 if x else 1] if x % (NX + 1) == 0 else grid.at[f, x - 1]
                low[pl.ds(row_of(f, x), HALO), :] = cells[pl.ds(0, HALO), :]
                high[pl.ds(row_of(f, x), HALO), :] = cells[pl.ds(NY - HALO, HALO), :]
        lane = lax.broadcasted_iota(jnp.int32, (EDGE, LANES), 1)
        for by, j, out in ((0, 0, low), (1, EDGE - 1, high)):
            edge = jnp.zeros((EDGE, LANES), jnp.float32)
            for bx in range(BRICK_X):
                for half in range(TILES // 2):
                    group, n = divmod((bx * BRICK_Y + by) * 2 + half, 4)
                    for i in range(2):
                        place = 2 * edge_place(bx, half, i)
                        lane_in = EDGE * (i * EDGE + j) + HALO * n
                        after = pltpu.roll(ends[0, group], (place + 1 - lane_in) % LANES, 1)
                        before = pltpu.roll(ends[1, group], (place - 1 - lane_in) % LANES, 1)
                        edge = jnp.where(lane == place, before, jnp.where(lane == place + 1, after, edge))
            out[pl.ds(ROWS, EDGE), :] = edge
        pair = lax.broadcasted_iota(jnp.int32, (NY, LANES), 1) // 2
        edges = [jnp.zeros((NY, LANES), jnp.float32)] * 2
        for side in range(2):
            cells = [[], [], [], []]
            for by in range(BRICK_Y):
                for j in range(EDGE):
                    turned[pl.ds(j * EDGE, EDGE), :] = beyond_ends(ends, side, by, side, side * EDGE + j)
                for f in range(FIELDS):
                    cells[f].append(turned[pl.ds(side * FIELDS + f, EDGE, stride=EDGE), :])
            for f in range(FIELDS):
                place = side_place(side, f)
                moved = pltpu.roll(jnp.concatenate(cells[f], 0), 2 * place + 1, 1)
                edges[side] = jnp.where(pair == place, moved, edges[side])
        if joined:
            outs[0][...] = jnp.where(pair < FIELDS, edges[0], edges[1])
        else:
            for out, edge in zip(outs, edges):
                out[...] = edge

    rows = jax.ShapeDtypeStruct((EDGES, LANES), jnp.float32)
    return pl.pallas_call(
        kernel,
        out_shape=[
            jax.ShapeDtypeStruct((FIELDS, 2 * HALO, NY, LANES), jnp.float32),
            jax.ShapeDtypeStruct((2, 2, 2 * FIELDS, LANES), jnp.float32),
            rows,
            rows,
        ]
        + sides,
        in_specs=[VMEM] * (3 + len(faces)),
        out_specs=[VMEM] * (4 + len(sides)),
        scratch_shapes=[pltpu.VMEM((LANES, LANES), jnp.float32)],
        compiler_params=ROOM,
        name="faces_and_rows",
    )(grid, odd_pairs, even_pairs, *faces)


def half_conductance(v):
    return 0.5 * (v * jnp.sqrt(v))


def step(cells, rates):
    return [v + (TIME_STEP * c) * r for v, c, r in zip(cells, DIFFUSION, rates)]


def rates(cells, s, beside):
    means = [s + n for _, n in beside]
    total = sum(means[1:], means[0])
    sums = []
    for f, v in enumerate(cells):
        terms = [m * fields[f] for m, (fields, _) in zip(means, beside)]
        sums.append(sum(terms[1:], terms[0]) - v * total)
    return sums


def each(function, cells, *others):
    fields, s = cells
    columns = zip(fields, *[other[0] for other in others])
    return [function(*c) for c in columns], function(s, *[other[1] for other in others])


def z_beside(cells, across):
    lane = lax.broadcasted_iota(jnp.int32, cells[1].shape, 1)

    def after(v, other):
        return pltpu.roll(jnp.where(lane == 0, other, v), LANES - 1, 1)

    def before(v, other):
        return pltpu.roll(jnp.where(lane == LANES - 1, other, v), 1, 1)

    return [each(after, cells, across), each(before, cells, across)]


def y_beside(cells):
    row = lax.broadcasted_iota(jnp.int32, (NY, LANES), 0)

    def after(v):
        return jnp.where(row == NY - 1, v, pltpu.roll(v, NY - 1, 0))

    def before(v):
        return jnp.where(row == 0, v, pltpu.roll(v, 1, 0))

    return [each(after, cells), each(before, cells)]


def first_inside(grid, layers, ends):
    def kernel(
        grid, layers, ends, wide, halves, beyond, first, first_beyond, halves_beyond, turned
    ):
        for bx in range(BRICK_X):
            for by in range(BRICK_Y):
                for half in range(TILES // 2):

                    def store(t, i, f, rows, x=bx * EDGE + half * 4, by=by):
                        beyond[f, x + t * 2 + i, pl.ds(by * EDGE, EDGE), :] = rows

                    lay_out([beyond_ends(ends, bx, by, half, r) for r in range(16)], turned, store)
        for f in range(FIELDS):
            for x in range(HALO):
                wide[f, x] = layers[f, x]
                wide[f, HALO + NX + x] = layers[f, HALO + x]
        for x in range(HALO):
            halves[x] = half_conductance(layers[0, x])
            halves[HALO + NX + x] = half_conductance(layers[0, HALO + x])

        def prepare(x, carry):
            for f in range(FIELDS):
                wide[f, x + HALO] = grid[f, x]
            halves[x + HALO] = half_conductance(grid[0, x])
            halves_beyond[x] = half_conductance(beyond[0, x])
            return carry

        lax.fori_loop(0, NX, prepare, 0, unroll=4)

        def at(ref, s, x):
            return [ref[f, x] for f in range(FIELDS)], s[x]

        def inside(x, carry):
            here, over = at(wide, halves, x + HALO), at(beyond, halves_beyond, x)
            beside = [at(wide, halves, x + HALO - 1), at(wide, halves, x + HALO + 1)]
            beside += y_beside(here) + z_beside(here, over)
            for f, v in enumerate(step(here[0], rates(*here, beside))):
                first[f, x] = v
            left, right = jnp.maximum(x - 1, 0), jnp.minimum(x + 1, NX - 1)
            beside = [at(beyond, halves_beyond, left), at(beyond, halves_beyond, right)]
            beside += y_beside(over) + z_beside(over, here)
            for f, v in enumerate(step(over[0], rates(*over, beside))):
                first_beyond[f, x] = v
            return carry

        lax.fori_loop(0, NX, inside, 0, unroll=2)

    def shape(*sizes):
        return jax.ShapeDtypeStruct(sizes + (NY, LANES), jnp.float32)

    return pl.pallas_call(
        kernel,
        out_shape=[
            shape(FIELDS, WIDE_X),
            shape(WIDE_X),
            shape(FIELDS, NX),
            shape(FIELDS, NX),
            shape(FIELDS, NX),
            shape(NX),
        ],
        in_specs=[VMEM] * 3,
        out_specs=[VMEM] * 6,
        scratch_shapes=[pltpu.VMEM((LANES, LANES), jnp.float32)],
        compiler_params=ROOM,
        cost_estimate=pl.CostEstimate(flops=2**22, bytes_accessed=2**21, transcendentals=0),
        name="first_inside",
    )(grid, layers, ends)


PARTS = 8


def last_sections(wide, halves, first, first_beyond, beyond, halves_beyond, above, below, sides):
    def kernel(wide, halves, first_in, beyond_in, beyond, halves_beyond, above, below, *refs):
        ins, (out, *refs) = refs[: len(sides)], refs[len(sides) :]
        edges, first, first_beyond, around, fs, fbs, below_halves, above_halves, result, sems = refs
        factors = [TIME_STEP * c for c in DIFFUSION]
        row = lax.broadcasted_iota(jnp.int32, (EDGE, LANES), 0)

        def side_edge(side):
            packed = ins[0 if len(ins) == 1 else side][...]
            fields = [
                pltpu.roll(packed, LANES - 1 - 2 * side_place(side, f), 1) for f in range(FIELDS)
            ]
            return fields, half_conductance(fields[0])

        for sent_edge, at_row in ((below, 0), (above, EDGE - 1)):
            edge = sent_edge[pl.ds(ROWS, EDGE), :]
            for bx in range(BRICK_X):
                for half in range(TILES // 2):
                    for i in range(2):
                        tile = pltpu.roll(edge, LANES - 1 - 2 * edge_place(bx, half, i), 1)
                        for t in range(2):
                            x = bx * EDGE + half * 4 + t * 2 + i
                            rows = pl.ds(x * EDGE + at_row, FIELDS, stride=NX * EDGE)
                            edges[rows, :] = tile[t * FIELDS :][:FIELDS]

        def at(ref, s, x):
            return [ref[f, x] for f in range(FIELDS)], s[x]

        for side, x in ((1, 0), (0, NX + 1)):
            here = at(wide, halves, x + 1)
            beside = [at(wide, halves, x), at(wide, halves, x + 2)]
            beside += y_beside(here) + z_beside(here, side_edge(side))
            for f, v in enumerate(step(here[0], rates(*here, beside))):
                first[pl.ds((f * NEAR_X + x) * NY, NY), :] = v
        for f in range(FIELDS):
            for x in range(NX):
                first[pl.ds((f * NEAR_X + x + 1) * NY, NY), :] = first_in[f, x]

        wide_rows = wide.reshape(FIELDS * WIDE_X * NY, LANES)
        half_rows = halves.reshape(WIDE_X * NY, LANES)

        for ref, sent_halves in ((below, below_halves), (above, above_halves)):
            sent_halves[...] = half_conductance(ref[pl.ds(0, sent_halves.shape[0]), :])

        def sent(ref, depth, f, x, count):
            return ref[pl.ds(row_of(f, x) + depth, count, stride=HALO), :]

        for ref, ref_halves, depth, y, tile_row in (
            (below, below_halves, 1, 0, 7),
            (above, above_halves, 0, NY - 1, 0),
        ):
            for x, count in ((0, 8), (8, 8), (16, 2)):
                s = half_rows[pl.ds((x + 1) * NY + y, count, stride=NY), :]
                mean = s + sent(ref_halves, depth, 0, x, count)
                for f in range(FIELDS):
                    v = wide_rows[pl.ds((f * WIDE_X + x + 1) * NY + y, count, stride=NY), :]
                    rows = pl.ds((f * NEAR_X + x) * NY + y, count, stride=NY)
                    more = mean * (sent(ref, depth, f, x, count) - v)
                    first[rows, :] = first[rows, :] + factors[f] * more
            for x in (0, 8):

                def line(depth, shift):
                    fields = [sent(ref, depth, f, x + 1 + shift, 8) for f in range(FIELDS)]
                    return fields, sent(ref_halves, depth, 0, x + 1 + shift, 8)

                here = line(depth, 0)
                inner = (
                    [
                        wide_rows[pl.ds((f * WIDE_X + x + HALO) * NY + y, 8, stride=NY), :]
                        for f in range(FIELDS)
                    ],
                    half_rows[pl.ds((x + HALO) * NY + y, 8, stride=NY), :],
                )
                over = [
                    edges[pl.ds((f * NX + x) * EDGE + 7 - tile_row, 8, stride=EDGE), :]
                    for f in range(FIELDS)
                ]
                beside = [line(1 - depth, 0), inner, line(depth, -1), line(depth, 1)]
                beside += z_beside(here, (over, half_conductance(over[0])))
                for f, v in enumerate(step(here[0], rates(*here, beside))):
                    around[pl.ds((f * NX + x) * EDGE + tile_row, 8, stride=EDGE), :] = v

        for x in range(NX):
            s = halves_beyond[x]
            near = half_conductance(edges[pl.ds(x * EDGE, EDGE), :])
            for f in range(FIELDS):
                tile = edges[pl.ds((f * NX + x) * EDGE, EDGE), :]
                v, fresh = beyond[f, x], beyond_in[f, x]
                more = [
                    jnp.where(row == at_row, (near + s[n * EDGE :][:EDGE]) * (tile - v[n * EDGE :][:EDGE]), 0.0)
                    for n, at_row in enumerate((0, EDGE - 1))
                ]
                first_beyond[f, x] = fresh + factors[f] * jnp.concatenate(more, 0)
        for side, x in ((1, 0), (0, NX - 1)):
            fields, s = side_edge(side)
            for f in range(FIELDS):
                more = (s + halves_beyond[x]) * (fields[f] - beyond[f, x])
                first_beyond[f, x] = first_beyond[f, x] + factors[f] * more

        def near(x):
            return [
                first[pl.ds(pl.multiple_of((f * NEAR_X + x) * NY, NY), NY), :] for f in range(FIELDS)
            ]

        def conductances(x, carry):
            fs[x] = half_conductance(near(x)[0])
            return carry

        lax.fori_loop(0, NEAR_X, conductances, 0, unroll=6)

        def conductances_beyond(x, carry):
            fbs[x] = half_conductance(first_beyond[0, x])
            return carry

        lax.fori_loop(0, NX, conductances_beyond, 0, unroll=4)

        def second(x, carry):
            here = near(x + 1), fs[x + 1]
            tiles = [
                around[pl.ds(pl.multiple_of((f * NX + x) * EDGE, EDGE), EDGE), :]
                for f in range(FIELDS)
            ]
            ring_of = each(
                lambda v, tile: jnp.concatenate([v, tile], 0), here, (tiles, half_conductance(tiles[0]))
            )
            beside = [(near(x), fs[x]), (near(x + 2), fs[x + 2])]
            beside += [
                each(lambda v: pltpu.roll(v, WIDE_Y - 1, 0)[:NY], ring_of),
                each(lambda v: pltpu.roll(v, 1, 0)[:NY], ring_of),
            ]
            beside += z_beside(here, at(first_beyond, fbs, x))
            for f, v in enumerate(step(here[0], rates(*here, beside))):
                result[f, x] = 0.5 * wide[f, x + HALO] + 0.5 * v
            return carry

        copies = []
        for part in range(PARTS):
            start = part * (NX // PARTS)
            lax.fori_loop(start, start + NX // PARTS, second, 0, unroll=NX // PARTS)
            layers = pl.ds(start, NX // PARTS)
            copies.append(
                pltpu.make_async_copy(result.at[:, layers], out.at[:, layers], sems.at[part])
            )
            copies[-1].start()
        for copy in copies:
            copy.wait()

    def scratch(*shape):
        return pltpu.VMEM(shape + (LANES,), jnp.float32)

    return pl.pallas_call(
        kernel,
        out_shape=jax.ShapeDtypeStruct((FIELDS, NX, NY, LANES), jnp.float32),
        in_specs=[VMEM] * (8 + len(sides)),
        out_specs=HBM,
        scratch_shapes=[
            scratch(FIELDS * NX * EDGE),
            scratch(FIELDS * NEAR_X * NY),
            scratch(FIELDS, NX, NY),
            scratch(FIELDS * NX * EDGE),
            scratch(NEAR_X, NY),
            scratch(NX, NY),
            scratch(5 * EDGE),
            scratch(5 * EDGE),
            scratch(FIELDS, NX, NY),
            pltpu.SemaphoreType.DMA((PARTS,)),
        ],
        compiler_params=ROOM,
        name="last_sections",
    )(wide, halves, first, first_beyond, beyond, halves_beyond, above, below, *sides)


def body(old_fields, new_owner, old_owner):
    across, along = lax.axis_size("gx"), lax.axis_size("gz")
    group_size = across * along
    box_count = new_owner.shape[0]
    capacity = 2 * (box_count // group_size)
    split = group_size <= 8
    joined = across == 2
    departing = pack_boxes(old_fields, new_owner, group_size, capacity, split)
    table = position_table(old_owner, group_size, capacity)
    if split:
        order = (3, 1, 4, 2, 6, 5, 7, 0)
        arrived = [
            lax.ppermute(departing[k], ("gx", "gz"), [(i, i ^ k) for i in range(group_size)])
            if k
            else departing[k]
            for k in order
        ]
    else:
        order = [0]
        arrived = [
            lax.all_to_all(departing[0], ("gx", "gz"), split_axis=0, concat_axis=0, tiled=True)
        ]
    held, odd_pairs, even_pairs, *faces = boxes_in_place(
        arrived, order, table, box_count, capacity, split, joined
    )

    def along_x(sides):
        if joined:
            return [lax.ppermute(sides[0], "gx", ring(across, 1))]
        return [lax.ppermute(side, "gx", ring(across, step)) for side, step in zip(sides, (-1, 1))]

    faces = along_x(faces)
    odd_pairs = lax.ppermute(odd_pairs, "gz", pairs(along, 1))
    even_pairs = lax.ppermute(even_pairs, "gz", pairs(along, 0))
    grid = grid_from_boxes(held)
    layers, ends, low, high, *sides = faces_and_rows(
        grid, faces, odd_pairs, even_pairs, joined
    )
    rows = lax.axis_size("gy")
    above = lax.ppermute(low, "gy", ring(rows, -1))
    below = lax.ppermute(high, "gy", ring(rows, 1))
    sides = along_x(sides)
    wide, halves, beyond, first, first_beyond, halves_beyond = first_inside(grid, layers, ends)
    return last_sections(
        wide, halves, first, first_beyond, beyond, halves_beyond, above, below, sides
    )


def solution(mesh):
    return jax.shard_map(
        body,
        mesh=mesh,
        in_specs=(P(("gx", "gy", "gz"), None, None), P(("gx", "gy", "gz")), P(("gx", "gy", "gz"))),
        out_specs=P(None, "gx", "gy", "gz"),
        check_vma=False,
    )
```

```python
import jax
import jax.numpy as jnp
from jax import lax
from jax.experimental import pallas as pl
from jax.experimental.pallas import tpu as pltpu
from jax.sharding import PartitionSpec as P

EDGE = 8
FIELDS = 4
BRICK_X = 2
BRICK_Y = 2
BRICK_Z = 16
CELLS = EDGE**3
LANES = 128
TILES = CELLS // LANES
BOX = (TILES // 2, 2 * FIELDS, LANES)


DIFFUSION = (1.0, 3.3, 0.9, 1.2)
TIME_STEP = 0.012

VMEM = pl.BlockSpec(memory_space=pltpu.VMEM)
SMEM = pl.BlockSpec(memory_space=pltpu.SMEM)
HBM = pl.BlockSpec(memory_space=pltpu.HBM)
ROOM = pltpu.CompilerParams(vmem_limit_bytes=16 * 2**20)


def in_hbm(array):
    return pltpu.with_memory_space_constraint(array, pltpu.HBM)


def group_place():
    return lax.axis_index("gx") * lax.axis_size("gz") + lax.axis_index("gz")


def rank_table(owner, table, counts, group, capacity, boxes, empty):
    def clear(i, carry):
        table[i] = empty
        return carry

    lax.fori_loop(0, group * capacity, clear, 0, unroll=16)
    for g in range(group):
        counts[g] = g * capacity

    def place(b, carry):
        o = owner[b]
        slot = counts[o]
        table[slot] = b
        counts[o] = slot + 1
        return carry

    lax.fori_loop(0, boxes, place, 0, unroll=8)


def pack_boxes(old_fields, new_owner, group, capacity, split):
    boxes = new_owner.shape[0]
    pieces = group if split else 1
    rows = group * capacity // pieces

    def kernel(owner_hbm, fields_hbm, *refs):
        outs, (owner, fields, table, counts, sems) = refs[:pieces], refs[pieces:]
        fetch_owner = pltpu.make_async_copy(owner_hbm, owner, sems.at[0])
        fetch_fields = pltpu.make_async_copy(fields_hbm, fields, sems.at[1])
        fetch_owner.start()
        fetch_fields.start()
        fetch_owner.wait()
        rank_table(owner, table, counts, group, capacity, boxes, 0)
        fetch_fields.wait()
        for k, out in enumerate(outs):
            base = (group_place() ^ k) * capacity if split else 0

            def copy(r, carry, out=out, base=base):
                box = table[base + r]
                for t in range(TILES):
                    out[r, t // 2, pl.ds(t % 2 * FIELDS, FIELDS), :] = fields[
                        box, :, pl.ds(t * LANES, LANES)
                    ]
                return carry

            lax.fori_loop(0, rows, copy, 0, unroll=16)

    return pl.pallas_call(
        kernel,
        out_shape=[jax.ShapeDtypeStruct((rows,) + BOX, jnp.float32)] * pieces,
        in_specs=[HBM, HBM],
        out_specs=[VMEM] * pieces,
        scratch_shapes=[
            pltpu.SMEM((boxes,), jnp.int32),
            pltpu.VMEM(old_fields.shape, jnp.float32),
            pltpu.SMEM((group * capacity,), jnp.int32),
            pltpu.SMEM((group,), jnp.int32),
            pltpu.SemaphoreType.DMA((2,)),
        ],
        compiler_params=ROOM,
        name="pack_boxes",
    )(in_hbm(new_owner), in_hbm(old_fields))


def position_table(old_owner, group, capacity):
    boxes = old_owner.shape[0]

    def kernel(owner, table, counts):
        rank_table(owner, table, counts, group, capacity, boxes, boxes)

    return pl.pallas_call(
        kernel,
        out_shape=pltpu.SMEM((group * capacity,), jnp.int32),
        in_specs=[SMEM],
        out_specs=SMEM,
        scratch_shapes=[pltpu.SMEM((group,), jnp.int32)],
        compiler_params=ROOM,
        cost_estimate=pl.CostEstimate(flops=0, bytes_accessed=2**22, transcendentals=0),
        name="position_table",
    )(old_owner)


def swap_boxes(columns):
    lane = lax.broadcasted_iota(jnp.int32, columns[0].shape, 1)
    for bit in range(4):
        width = EDGE << bit
        upper = (lane & width) != 0
        fresh = list(columns)
        for low in range(16):
            if low >> bit & 1:
                continue
            high = low | 1 << bit
            a, b = columns[low], columns[high]
            fresh[low] = jnp.where(upper, pltpu.roll(b, width, 1), a)
            fresh[high] = jnp.where(upper, b, pltpu.roll(a, LANES - width, 1))
        columns = fresh
    return columns


def ring(count, step):
    return [(i, (i + step) % count) for i in range(count)]


def pairs(count, first):
    return [((i + first) % count, ((i ^ 1) + first) % count) for i in range(count)]


def boxes_in_place(arrived, order, table, boxes, capacity, split, joined):
    pieces = len(arrived)
    rows = table.shape[0] // pieces
    half = boxes // BRICK_X
    face = (BRICK_Z, BRICK_Y * FIELDS, LANES)
    faces = [jax.ShapeDtypeStruct((2,) + face if joined else face, jnp.float32)] * (2 - joined)
    end = jax.ShapeDtypeStruct((2, 2 * FIELDS, LANES), jnp.float32)

    def kernel(table, *refs):
        ins, refs = refs[:pieces], refs[pieces:]
        held, odd_pairs, even_pairs, *outs = refs
        odd = lax.axis_index("gz") & 1 != 0
        for k, rows_in in zip(order, ins):
            base = (group_place() ^ k) * capacity if split else 0

            def scatter(r, carry, rows_in=rows_in, base=base):
                held[table[base + r]] = rows_in[r]
                return carry

            lax.fori_loop(0, rows, scatter, 0, unroll=16)
        for side in range(2):
            out = outs[0].at[side] if joined else outs[side]
            for by in range(BRICK_Y):
                for bz in range(BRICK_Z):
                    p = side * half + by * BRICK_Z + bz
                    out[bz, pl.ds(by * FIELDS, FIELDS), :] = held[
                        p, side, pl.ds(side * FIELDS, FIELDS), :
                    ]
        pair = lax.broadcasted_iota(jnp.int32, (2 * FIELDS, LANES), 1) % EDGE // HALO
        for group in range(2):
            ends = []
            for bz, first in ((0, 0), (BRICK_Z - 1, EDGE - HALO)):
                packed = jnp.zeros((2 * FIELDS, LANES), jnp.float32)
                for n in range(4):
                    b, part = divmod(group * 4 + n, 2)
                    cells = held[b * BRICK_Z + bz, part]
                    shift = (n * HALO - first) % LANES
                    packed = jnp.where(pair == n, pltpu.roll(cells, shift, 1) if shift else cells, packed)
                ends.append(packed)
            odd_pairs[group] = jnp.where(odd, ends[1], ends[0])
            even_pairs[group] = jnp.where(odd, ends[0], ends[1])

    return pl.pallas_call(
        kernel,
        out_shape=[jax.ShapeDtypeStruct((boxes + 1,) + BOX, jnp.float32), end, end] + faces,
        in_specs=[SMEM] + [VMEM] * pieces,
        out_specs=[VMEM] * (3 + len(faces)),
        compiler_params=ROOM,
        name="boxes_in_place",
    )(pltpu.with_memory_space_constraint(table, pltpu.SMEM), *arrived)


HALO = 2
NX = BRICK_X * EDGE
NY = BRICK_Y * EDGE
WIDE_X = NX + 2 * HALO
WIDE_Y = NY + EDGE
NEAR_X = NX + 2


def lay_out(columns, turned, store):
    for r in range(16):
        turned[pl.ds(r * 8, 8), :] = columns[r]
    for a in range(2):
        for i in range(2):
            for f in range(FIELDS):
                store(a, i, f, turned[pl.ds(i * 64 + a * FIELDS + f, 8, stride=8), :])


def grid_from_boxes(held):
    def kernel(held, grid, turned):
        for bx in range(BRICK_X):
            for by in range(BRICK_Y):
                first = (bx * BRICK_Y + by) * BRICK_Z
                for half in range(TILES // 2):

                    def store(t, i, f, rows, x=bx * EDGE + half * 4, by=by):
                        grid[f, x + t * 2 + i, pl.ds(by * EDGE, EDGE), :] = rows

                    columns = swap_boxes([held[first + bz, half] for bz in range(BRICK_Z)])
                    lay_out(columns, turned, store)

    return pl.pallas_call(
        kernel,
        out_shape=jax.ShapeDtypeStruct((FIELDS, NX, NY, LANES), jnp.float32),
        in_specs=[VMEM],
        out_specs=VMEM,
        scratch_shapes=[pltpu.VMEM((LANES, LANES), jnp.float32)],
        cost_estimate=pl.CostEstimate(flops=2**22, bytes_accessed=2**21, transcendentals=0),
        compiler_params=ROOM,
        name="grid_from_boxes",
    )(held)


ROWS = FIELDS * NEAR_X * HALO
EDGES = ROWS + EDGE


def row_of(f, x):
    return (f * NEAR_X + x) * HALO


def beyond_ends(ends, bx, by, half, r):
    group, n = divmod((bx * BRICK_Y + by) * 2 + half, 4)
    lane = lax.broadcasted_iota(jnp.int32, (EDGE, LANES), 1)
    first = EDGE * r + HALO * n
    return jnp.where(
        lane < LANES // 2,
        pltpu.roll(ends[0, group], (LANES - first) % LANES, 1),
        pltpu.roll(ends[1, group], (2 * LANES - HALO - first) % LANES, 1),
    )


def edge_place(bx, half, i):
    return (bx * 2 + half) * 2 + i


def side_place(side, f):
    return side * FIELDS + f


def faces_and_rows(grid, faces, odd_pairs, even_pairs, joined):
    sides = [jax.ShapeDtypeStruct((NY, LANES), jnp.float32)] * (2 - joined)

    def kernel(grid, odd_pairs, even_pairs, *refs):
        ins, refs = refs[: len(faces)], refs[len(faces) :]
        (layers, ends, low, high), refs = refs[:4], refs[4:]
        outs, (turned,) = refs[: len(sides)], refs[len(sides) :]
        odd = lax.axis_index("gz") & 1
        ends[odd] = even_pairs[...]
        ends[1 - odd] = odd_pairs[...]
        for side in range(2):
            face = ins[0].at[side] if joined else ins[side]

            def store(by, i, f, rows, first=0 if side else HALO):
                layers[f, first + i, pl.ds(by * EDGE, EDGE), :] = rows

            lay_out(swap_boxes([face[bz] for bz in range(BRICK_Z)]), turned, store)
        for f in range(FIELDS):
            for x in range(NEAR_X):
                cells = layers.at[f, 2 if x else 1] if x % (NX + 1) == 0 else grid.at[f, x - 1]
                low[pl.ds(row_of(f, x), HALO), :] = cells[pl.ds(0, HALO), :]
                high[pl.ds(row_of(f, x), HALO), :] = cells[pl.ds(NY - HALO, HALO), :]
        lane = lax.broadcasted_iota(jnp.int32, (EDGE, LANES), 1)
        for by, j, out in ((0, 0, low), (1, EDGE - 1, high)):
            edge = jnp.zeros((EDGE, LANES), jnp.float32)
            for bx in range(BRICK_X):
                for half in range(TILES // 2):
                    group, n = divmod((bx * BRICK_Y + by) * 2 + half, 4)
                    for i in range(2):
                        place = 2 * edge_place(bx, half, i)
                        lane_in = EDGE * (i * EDGE + j) + HALO * n
                        after = pltpu.roll(ends[0, group], (place + 1 - lane_in) % LANES, 1)
                        before = pltpu.roll(ends[1, group], (place - 1 - lane_in) % LANES, 1)
                        edge = jnp.where(lane == place, before, jnp.where(lane == place + 1, after, edge))
            out[pl.ds(ROWS, EDGE), :] = edge
        pair = lax.broadcasted_iota(jnp.int32, (NY, LANES), 1) // 2
        edges = [jnp.zeros((NY, LANES), jnp.float32)] * 2
        for side in range(2):
            cells = [[], [], [], []]
            for by in range(BRICK_Y):
                for j in range(EDGE):
                    turned[pl.ds(j * EDGE, EDGE), :] = beyond_ends(ends, side, by, side, side * EDGE + j)
                for f in range(FIELDS):
                    cells[f].append(turned[pl.ds(side * FIELDS + f, EDGE, stride=EDGE), :])
            for f in range(FIELDS):
                place = side_place(side, f)
                moved = pltpu.roll(jnp.concatenate(cells[f], 0), 2 * place + 1, 1)
                edges[side] = jnp.where(pair == place, moved, edges[side])
        if joined:
            outs[0][...] = jnp.where(pair < FIELDS, edges[0], edges[1])
        else:
            for out, edge in zip(outs, edges):
                out[...] = edge

    rows = jax.ShapeDtypeStruct((EDGES, LANES), jnp.float32)
    return pl.pallas_call(
        kernel,
        out_shape=[
            jax.ShapeDtypeStruct((FIELDS, 2 * HALO, NY, LANES), jnp.float32),
            jax.ShapeDtypeStruct((2, 2, 2 * FIELDS, LANES), jnp.float32),
            rows,
            rows,
        ]
        + sides,
        in_specs=[VMEM] * (3 + len(faces)),
        out_specs=[VMEM] * (4 + len(sides)),
        scratch_shapes=[pltpu.VMEM((LANES, LANES), jnp.float32)],
        compiler_params=ROOM,
        name="faces_and_rows",
    )(grid, odd_pairs, even_pairs, *faces)


def half_conductance(v):
    return 0.5 * (v * jnp.sqrt(v))


def step(cells, rates):
    return [v + (TIME_STEP * c) * r for v, c, r in zip(cells, DIFFUSION, rates)]


def rates(cells, s, beside):
    means = [s + n for _, n in beside]
    total = sum(means[1:], means[0])
    sums = []
    for f, v in enumerate(cells):
        terms = [m * fields[f] for m, (fields, _) in zip(means, beside)]
        sums.append(sum(terms[1:], terms[0]) - v * total)
    return sums


def each(function, cells, *others):
    fields, s = cells
    columns = zip(fields, *[other[0] for other in others])
    return [function(*c) for c in columns], function(s, *[other[1] for other in others])


def z_beside(cells, across):
    lane = lax.broadcasted_iota(jnp.int32, cells[1].shape, 1)

    def after(v, other):
        return pltpu.roll(jnp.where(lane == 0, other, v), LANES - 1, 1)

    def before(v, other):
        return pltpu.roll(jnp.where(lane == LANES - 1, other, v), 1, 1)

    return [each(after, cells, across), each(before, cells, across)]


def y_beside(cells):
    row = lax.broadcasted_iota(jnp.int32, (NY, LANES), 0)

    def after(v):
        return jnp.where(row == NY - 1, v, pltpu.roll(v, NY - 1, 0))

    def before(v):
        return jnp.where(row == 0, v, pltpu.roll(v, 1, 0))

    return [each(after, cells), each(before, cells)]


def first_inside(grid, layers, ends):
    def kernel(
        grid, layers, ends, wide, halves, beyond, first, first_beyond, halves_beyond, turned
    ):
        for bx in range(BRICK_X):
            for by in range(BRICK_Y):
                for half in range(TILES // 2):

                    def store(t, i, f, rows, x=bx * EDGE + half * 4, by=by):
                        beyond[f, x + t * 2 + i, pl.ds(by * EDGE, EDGE), :] = rows

                    lay_out([beyond_ends(ends, bx, by, half, r) for r in range(16)], turned, store)
        for f in range(FIELDS):
            for x in range(HALO):
                wide[f, x] = layers[f, x]
                wide[f, HALO + NX + x] = layers[f, HALO + x]
        for x in range(HALO):
            halves[x] = half_conductance(layers[0, x])
            halves[HALO + NX + x] = half_conductance(layers[0, HALO + x])

        def prepare(x, carry):
            for f in range(FIELDS):
                wide[f, x + HALO] = grid[f, x]
            halves[x + HALO] = half_conductance(grid[0, x])
            halves_beyond[x] = half_conductance(beyond[0, x])
            return carry

        lax.fori_loop(0, NX, prepare, 0, unroll=4)

        def at(ref, s, x):
            return [ref[f, x] for f in range(FIELDS)], s[x]

        def inside(x, carry):
            here, over = at(wide, halves, x + HALO), at(beyond, halves_beyond, x)
            beside = [at(wide, halves, x + HALO - 1), at(wide, halves, x + HALO + 1)]
            beside += y_beside(here) + z_beside(here, over)
            for f, v in enumerate(step(here[0], rates(*here, beside))):
                first[f, x] = v
            left, right = jnp.maximum(x - 1, 0), jnp.minimum(x + 1, NX - 1)
            beside = [at(beyond, halves_beyond, left), at(beyond, halves_beyond, right)]
            beside += y_beside(over) + z_beside(over, here)
            for f, v in enumerate(step(over[0], rates(*over, beside))):
                first_beyond[f, x] = v
            return carry

        lax.fori_loop(0, NX, inside, 0, unroll=2)

    def shape(*sizes):
        return jax.ShapeDtypeStruct(sizes + (NY, LANES), jnp.float32)

    return pl.pallas_call(
        kernel,
        out_shape=[
            shape(FIELDS, WIDE_X),
            shape(WIDE_X),
            shape(FIELDS, NX),
            shape(FIELDS, NX),
            shape(FIELDS, NX),
            shape(NX),
        ],
        in_specs=[VMEM] * 3,
        out_specs=[VMEM] * 6,
        scratch_shapes=[pltpu.VMEM((LANES, LANES), jnp.float32)],
        compiler_params=ROOM,
        cost_estimate=pl.CostEstimate(flops=2**22, bytes_accessed=2**21, transcendentals=0),
        name="first_inside",
    )(grid, layers, ends)


PARTS = 8


def last_sections(wide, halves, first, first_beyond, beyond, halves_beyond, above, below, sides):
    def kernel(wide, halves, first_in, beyond_in, beyond, halves_beyond, above, below, *refs):
        ins, (out, *refs) = refs[: len(sides)], refs[len(sides) :]
        edges, first, first_beyond, around, fs, fbs, below_halves, above_halves, result, sems = refs
        factors = [TIME_STEP * c for c in DIFFUSION]
        row = lax.broadcasted_iota(jnp.int32, (EDGE, LANES), 0)

        def side_edge(side):
            packed = ins[0 if len(ins) == 1 else side][...]
            fields = [
                pltpu.roll(packed, LANES - 1 - 2 * side_place(side, f), 1) for f in range(FIELDS)
            ]
            return fields, half_conductance(fields[0])

        for sent_edge, at_row in ((below, 0), (above, EDGE - 1)):
            edge = sent_edge[pl.ds(ROWS, EDGE), :]
            for bx in range(BRICK_X):
                for half in range(TILES // 2):
                    for i in range(2):
                        tile = pltpu.roll(edge, LANES - 1 - 2 * edge_place(bx, half, i), 1)
                        for t in range(2):
                            x = bx * EDGE + half * 4 + t * 2 + i
                            rows = pl.ds(x * EDGE + at_row, FIELDS, stride=NX * EDGE)
                            edges[rows, :] = tile[t * FIELDS :][:FIELDS]

        def at(ref, s, x):
            return [ref[f, x] for f in range(FIELDS)], s[x]

        for side, x in ((1, 0), (0, NX + 1)):
            here = at(wide, halves, x + 1)
            beside = [at(wide, halves, x), at(wide, halves, x + 2)]
            beside += y_beside(here) + z_beside(here, side_edge(side))
            for f, v in enumerate(step(here[0], rates(*here, beside))):
                first[pl.ds((f * NEAR_X + x) * NY, NY), :] = v
        for f in range(FIELDS):
            for x in range(NX):
                first[pl.ds((f * NEAR_X + x + 1) * NY, NY), :] = first_in[f, x]

        wide_rows = wide.reshape(FIELDS * WIDE_X * NY, LANES)
        half_rows = halves.reshape(WIDE_X * NY, LANES)

        for ref, sent_halves in ((below, below_halves), (above, above_halves)):
            sent_halves[...] = half_conductance(ref[pl.ds(0, sent_halves.shape[0]), :])

        def sent(ref, depth, f, x, count):
            return ref[pl.ds(row_of(f, x) + depth, count, stride=HALO), :]

        for ref, ref_halves, depth, y, tile_row in (
            (below, below_halves, 1, 0, 7),
            (above, above_halves, 0, NY - 1, 0),
        ):
            for x, count in ((0, 8), (8, 8), (16, 2)):
                s = half_rows[pl.ds((x + 1) * NY + y, count, stride=NY), :]
                mean = s + sent(ref_halves, depth, 0, x, count)
                for f in range(FIELDS):
                    v = wide_rows[pl.ds((f * WIDE_X + x + 1) * NY + y, count, stride=NY), :]
                    rows = pl.ds((f * NEAR_X + x) * NY + y, count, stride=NY)
                    more = mean * (sent(ref, depth, f, x, count) - v)
                    first[rows, :] = first[rows, :] + factors[f] * more
            for x in (0, 8):

                def line(depth, shift):
                    fields = [sent(ref, depth, f, x + 1 + shift, 8) for f in range(FIELDS)]
                    return fields, sent(ref_halves, depth, 0, x + 1 + shift, 8)

                here = line(depth, 0)
                inner = (
                    [
                        wide_rows[pl.ds((f * WIDE_X + x + HALO) * NY + y, 8, stride=NY), :]
                        for f in range(FIELDS)
                    ],
                    half_rows[pl.ds((x + HALO) * NY + y, 8, stride=NY), :],
                )
                over = [
                    edges[pl.ds((f * NX + x) * EDGE + 7 - tile_row, 8, stride=EDGE), :]
                    for f in range(FIELDS)
                ]
                beside = [line(1 - depth, 0), inner, line(depth, -1), line(depth, 1)]
                beside += z_beside(here, (over, half_conductance(over[0])))
                for f, v in enumerate(step(here[0], rates(*here, beside))):
                    around[pl.ds((f * NX + x) * EDGE + tile_row, 8, stride=EDGE), :] = v

        for x in range(NX):
            s = halves_beyond[x]
            near = half_conductance(edges[pl.ds(x * EDGE, EDGE), :])
            for f in range(FIELDS):
                tile = edges[pl.ds((f * NX + x) * EDGE, EDGE), :]
                v, fresh = beyond[f, x], beyond_in[f, x]
                more = [
                    jnp.where(row == at_row, (near + s[n * EDGE :][:EDGE]) * (tile - v[n * EDGE :][:EDGE]), 0.0)
                    for n, at_row in enumerate((0, EDGE - 1))
                ]
                first_beyond[f, x] = fresh + factors[f] * jnp.concatenate(more, 0)
        for side, x in ((1, 0), (0, NX - 1)):
            fields, s = side_edge(side)
            for f in range(FIELDS):
                more = (s + halves_beyond[x]) * (fields[f] - beyond[f, x])
                first_beyond[f, x] = first_beyond[f, x] + factors[f] * more

        def near(x):
            return [
                first[pl.ds(pl.multiple_of((f * NEAR_X + x) * NY, NY), NY), :] for f in range(FIELDS)
            ]

        def conductances(x, carry):
            fs[x] = half_conductance(near(x)[0])
            return carry

        lax.fori_loop(0, NEAR_X, conductances, 0, unroll=6)

        def conductances_beyond(x, carry):
            fbs[x] = half_conductance(first_beyond[0, x])
            return carry

        lax.fori_loop(0, NX, conductances_beyond, 0, unroll=4)

        def second(x, carry):
            here = near(x + 1), fs[x + 1]
            tiles = [
                around[pl.ds(pl.multiple_of((f * NX + x) * EDGE, EDGE), EDGE), :]
                for f in range(FIELDS)
            ]
            ring_of = each(
                lambda v, tile: jnp.concatenate([v, tile], 0), here, (tiles, half_conductance(tiles[0]))
            )
            beside = [(near(x), fs[x]), (near(x + 2), fs[x + 2])]
            beside += [
                each(lambda v: pltpu.roll(v, WIDE_Y - 1, 0)[:NY], ring_of),
                each(lambda v: pltpu.roll(v, 1, 0)[:NY], ring_of),
            ]
            beside += z_beside(here, at(first_beyond, fbs, x))
            for f, v in enumerate(step(here[0], rates(*here, beside))):
                result[f, x] = 0.5 * wide[f, x + HALO] + 0.5 * v
            return carry

        copies = []
        for part in range(PARTS):
            start = part * (NX // PARTS)
            lax.fori_loop(start, start + NX // PARTS, second, 0, unroll=NX // PARTS)
            layers = pl.ds(start, NX // PARTS)
            copies.append(
                pltpu.make_async_copy(result.at[:, layers], out.at[:, layers], sems.at[part])
            )
            copies[-1].start()
        for copy in copies:
            copy.wait()

    def scratch(*shape):
        return pltpu.VMEM(shape + (LANES,), jnp.float32)

    return pl.pallas_call(
        kernel,
        out_shape=jax.ShapeDtypeStruct((FIELDS, NX, NY, LANES), jnp.float32),
        in_specs=[VMEM] * (8 + len(sides)),
        out_specs=HBM,
        scratch_shapes=[
            scratch(FIELDS * NX * EDGE),
            scratch(FIELDS * NEAR_X * NY),
            scratch(FIELDS, NX, NY),
            scratch(FIELDS * NX * EDGE),
            scratch(NEAR_X, NY),
            scratch(NX, NY),
            scratch(5 * EDGE),
            scratch(5 * EDGE),
            scratch(FIELDS, NX, NY),
            pltpu.SemaphoreType.DMA((PARTS,)),
        ],
        compiler_params=ROOM,
        name="last_sections",
    )(wide, halves, first, first_beyond, beyond, halves_beyond, above, below, *sides)


def body(old_fields, new_owner, old_owner):
    across, along = lax.axis_size("gx"), lax.axis_size("gz")
    group_size = across * along
    box_count = new_owner.shape[0]
    capacity = 2 * (box_count // group_size)
    split = group_size <= 8
    joined = across == 2
    departing = pack_boxes(old_fields, new_owner, group_size, capacity, split)
    table = position_table(old_owner, group_size, capacity)
    if split:
        order = (3, 1, 4, 2, 6, 5, 7, 0)
        arrived = [
            lax.ppermute(departing[k], ("gx", "gz"), [(i, i ^ k) for i in range(group_size)])
            if k
            else departing[k]
            for k in order
        ]
    else:
        order = [0]
        arrived = [
            lax.all_to_all(departing[0], ("gx", "gz"), split_axis=0, concat_axis=0, tiled=True)
        ]
    held, odd_pairs, even_pairs, *faces = boxes_in_place(
        arrived, order, table, box_count, capacity, split, joined
    )

    def along_x(sides):
        if joined:
            return [lax.ppermute(sides[0], "gx", ring(across, 1))]
        return [lax.ppermute(side, "gx", ring(across, step)) for side, step in zip(sides, (-1, 1))]

    faces = along_x(faces)
    odd_pairs = lax.ppermute(odd_pairs, "gz", pairs(along, 1))
    even_pairs = lax.ppermute(even_pairs, "gz", pairs(along, 0))
    grid = grid_from_boxes(held)
    layers, ends, low, high, *sides = faces_and_rows(
        grid, faces, odd_pairs, even_pairs, joined
    )
    rows = lax.axis_size("gy")
    above = lax.ppermute(low, "gy", ring(rows, -1))
    below = lax.ppermute(high, "gy", ring(rows, 1))
    sides = along_x(sides)
    wide, halves, beyond, first, first_beyond, halves_beyond = first_inside(grid, layers, ends)
    return last_sections(
        wide, halves, first, first_beyond, beyond, halves_beyond, above, below, sides
    )


def solution(mesh):
    return jax.shard_map(
        body,
        mesh=mesh,
        in_specs=(P(("gx", "gy", "gz"), None, None), P(("gx", "gy", "gz")), P(("gx", "gy", "gz"))),
        out_specs=P(None, "gx", "gy", "gz"),
        check_vma=False,
    )
```
